32 devices in a mesh: items: 8 (over z, x), rays: 4 (over y, core).
Axes of the slice: x: 2, y: 2, z: 4, core: 2. Of those that a mesh axis runs over, the one named last changes fastest.
Arguments:
- rays: bfloat16 [8, 4096, 768], P('items', 'rays'), may hold values from -6 to 6
- latents: bfloat16 [8, 1152, 768], P('items', 'rays'), may hold values from -6 to 6
- ray_scene: int32 [8, 4096], P('items', 'rays'), may hold values from 0 to 3
- latent_scene: int32 [8, 1152], P('items'), may hold values from 0 to 3, as said below
- latent_pad: int32 [8, 1152], P('items'), may hold values from 0 to 1, as said below
- cotangent: bfloat16 [8, 4096, 768], P('items', 'rays'), may hold values from -6 to 6
- query_weight: bfloat16 [768, 768], replicated, may hold values from -0.21875 to 0.21875
- key_weight: bfloat16 [768, 768], replicated, may hold values from -0.21875 to 0.21875
- value_weight: bfloat16 [768, 768], replicated, may hold values from -0.21875 to 0.21875
- out_weight: bfloat16 [768, 768], replicated, may hold values from -3 to 3
- out_bias: float32 [768], replicated, may hold values from -3 to 3
- up_weight: bfloat16 [768, 1536], replicated, may hold values from -0.21875 to 0.21875
- up_bias: float32 [1536], replicated, may hold values from -3 to 3
- down_weight: bfloat16 [1536, 768], replicated, may hold values from -0.15625 to 0.15625
- down_bias: float32 [768], replicated, may hold values from -3 to 3
- ray_gain: float32 [768], replicated, may hold values from 0.25 to 1.75
- ray_shift: float32 [768], replicated, may hold values from -3 to 3
- latent_gain: float32 [768], replicated, may hold values from 0.25 to 1.75
- latent_shift: float32 [768], replicated, may hold values from -3 to 3
- mlp_gain: float32 [768], replicated, may hold values from 0.25 to 1.75
- mlp_shift: float32 [768], replicated, may hold values from -3 to 3
Outputs:
- ray_out: bfloat16 [8, 4096, 768], P('items', 'rays')
- ray_grad: bfloat16 [8, 4096, 768], P('items', 'rays')
- latent_grad: bfloat16 [8, 1152, 768], P('items', 'rays')
- query_grad: float32 [768, 768], replicated
- key_grad: float32 [768, 768], replicated
- value_grad: float32 [768, 768], replicated
- out_grad: float32 [768, 768], replicated
- out_bias_grad: float32 [768], replicated
- up_grad: float32 [768, 1536], replicated
- up_bias_grad: float32 [1536], replicated
- down_grad: float32 [1536, 768], replicated
- down_bias_grad: float32 [768], replicated
- ray_gain_grad: float32 [768], replicated
- ray_shift_grad: float32 [768], replicated
- latent_gain_grad: float32 [768], replicated
- latent_shift_grad: float32 [768], replicated
- mlp_gain_grad: float32 [768], replicated
- mlp_shift_grad: float32 [768], replicated
The draws below stay inside these ranges and needn't reach their ends.
Inputs may be any that keep to these rules, and one draw needn't show every extreme that they name: `latent_scene`: along each item's 1152 latent tokens the scene number never falls, and each of the 4 scenes has one or more unpadded tokens. `latent_pad`: padding tokens, one or more in each item, are the last of the item's latent tokens.
All inputs are finite; a program needn't handle non-finite values.
Results may differ from the reference program's by a relative error of at most 0.012.
The reference program's roundings to bfloat16 on the way count: a program that leaves them out, or rounds other values in their place, can miss the bound.
Values may be sent and summed in bfloat16 or wider, within the bound.
A program may use at most 256 MiB of HBM per device.

```python
import jax
import jax.numpy as jnp
from jax import lax

D = 768
HEADS = 12
HEAD_DIM = 64
FF = 1536
RAY_DEV = 1024
LAT_DEV = 288
SCENES = 4
ITEMS = 8
RAYS = 4096
LAT = 1152


def scene_layout(key):
    base_key = jax.random.fold_in(key, 11)
    first_key, second_key, third_key, fourth_key = jax.random.split(base_key, 4)
    quarter = max(LAT_DEV // 4, 1)
    column_shape = (ITEMS, 1)
    first_end = 1 + jax.random.randint(first_key, column_shape, 0, LAT_DEV - 1)
    last_start = LAT - LAT_DEV
    second_end = last_start + 1 + jax.random.randint(second_key, column_shape, 0, quarter)
    third_end = second_end + 1 + jax.random.randint(third_key, column_shape, 0, quarter)
    valid_end = LAT - 1 - jax.random.randint(fourth_key, column_shape, 0, quarter)
    position = jnp.arange(LAT, dtype=jnp.int32)[None, :]
    scene_ids = (position >= first_end).astype(jnp.int32) + (position >= second_end).astype(jnp.int32) + (position >= third_end).astype(jnp.int32)
    padding = (position >= valid_end).astype(jnp.int32)
    return (scene_ids, padding)


def draw_latent_scene(key, part):
    return scene_layout(key)[0]


def draw_latent_pad(key, part):
    return scene_layout(key)[1]


def set_ends(entries, key, least, top_value):
    longest = entries.shape.index(max(entries.shape))
    spots = []
    for shift in (0, 1):
        where = [jax.random.randint(jax.random.fold_in(key, axis), (), 0, length) for axis, length in enumerate(entries.shape)]
        where[longest] = (where[longest] + shift) % entries.shape[longest]
        spots.append(tuple(where))
    return entries.at[spots[0]].set(least).at[spots[1]].set(top_value)


def steps_of(stream_key, extent, cuts, low, largest):
    def one(axis_at, parts):
        steps = jax.random.uniform(jax.random.fold_in(jax.random.fold_in(stream_key, 6), axis_at), (parts,), jnp.float32, low / len(cuts), largest / len(cuts))
        return jnp.repeat(jnp.exp(steps), extent[axis_at] // parts).reshape((-1,) + (1,) * (len(extent) - axis_at - 1))

    loudness = one(*cuts[0])
    for cut in cuts[1:]:
        loudness = loudness * one(*cut)
    return loudness


def scatter_about(stream_key, extent, width, bound, cuts=(), kind=jnp.bfloat16):
    level = steps_of(stream_key, extent, cuts, -0.22, 0.18) if cuts else 1.0
    drawn = jax.random.normal(stream_key, extent, jnp.float32) * width * level
    return jnp.minimum(jnp.maximum(drawn, -bound), bound).astype(kind)


def setup_inputs(seed: int = 0) -> dict:
    key_list = jax.random.split(jax.random.key(seed), 22)
    return {
        "rays": scatter_about(key_list[0], (ITEMS, RAYS, D), 1.0, 6.0, ((0, 8), (1, 4))),
        "latents": scatter_about(key_list[1], (ITEMS, LAT, D), 1.0, 6.0, ((0, 8), (1, 4))),
        "ray_scene": set_ends(jax.random.randint(key_list[2], (ITEMS, RAYS), 0, SCENES), jax.random.fold_in(key_list[2], 1), 0, SCENES - 1).astype(jnp.int32),
        "latent_scene": draw_latent_scene(jax.random.fold_in(key_list[21], 71), 0),
        "latent_pad": draw_latent_pad(jax.random.fold_in(key_list[21], 71), 0),
        "cotangent": scatter_about(key_list[5], (ITEMS, RAYS, D), 1.0, 6.0, ((0, 8), (1, 4))),
        "query_weight": scatter_about(key_list[6], (D, D), D ** -0.5, 0.21875),
        "key_weight": scatter_about(key_list[7], (D, D), D ** -0.5, 0.21875),
        "value_weight": scatter_about(key_list[8], (D, D), D ** -0.5, 0.21875),
        "out_weight": scatter_about(key_list[9], (D, D), (D // 256 + 1) ** -0.5, 3.0),
        "out_bias": scatter_about(key_list[10], (D,), 0.5, 3.0, (), jnp.float32),
        "up_weight": scatter_about(key_list[11], (D, FF), D ** -0.5, 0.21875),
        "up_bias": scatter_about(key_list[12], (FF,), 0.5, 3.0, (), jnp.float32),
        "down_weight": scatter_about(key_list[13], (FF, D), FF ** -0.5, 0.15625),
        "down_bias": scatter_about(key_list[14], (D,), 0.5, 3.0, (), jnp.float32),
        "ray_gain": jnp.clip(1.0 + 0.15 * jax.random.normal(key_list[15], (D,), jnp.float32), 0.25, 1.75),
        "ray_shift": scatter_about(key_list[16], (D,), 0.5, 3.0, (), jnp.float32),
        "latent_gain": jnp.clip(1.0 + 0.15 * jax.random.normal(key_list[17], (D,), jnp.float32), 0.25, 1.75),
        "latent_shift": scatter_about(key_list[18], (D,), 0.5, 3.0, (), jnp.float32),
        "mlp_gain": jnp.clip(1.0 + 0.15 * jax.random.normal(key_list[19], (D,), jnp.float32), 0.25, 1.75),
        "mlp_shift": scatter_about(key_list[20], (D,), 0.5, 3.0, (), jnp.float32),
    }


@jax.custom_vjp
def low(v):
    return lax.optimization_barrier(v.astype(jnp.bfloat16)).astype(jnp.float32)

@jax.custom_vjp
def low_back(v):
    return v

def low_keep(v):
    return (low(v), None)

def low_pass(kept, grad):
    return (grad,)

def back_keep(v):
    return (v, None)

def back_low(kept, grad):
    return (low(grad),)
low.defvjp(low_keep, low_pass)
low_back.defvjp(back_keep, back_low)
EPSILON = 1e-05
MASKED = -1000000000.0
HIGHEST = lax.Precision.HIGHEST

def both_round(values):
    return low(low_back(values))

def layer_norm(inputs, norm_gain, norm_shift):
    center = inputs - lax.optimization_barrier(jnp.mean(inputs, axis=-1, keepdims=True))
    spread = lax.optimization_barrier(jnp.mean(center * center, axis=-1, keepdims=True))
    return center * lax.rsqrt(spread + EPSILON) * norm_gain + norm_shift

def matmul(left_side, right_side):
    return jnp.dot(left_side, right_side, precision=HIGHEST, preferred_element_type=jnp.float32)

def head_split(matrix):
    return matrix.reshape(matrix.shape[0], HEADS, HEAD_DIM)

def attend(queries, key_rows, value_rows, ray_ids, latent_ids, pad_flags):

    def one_block(inputs):
        query_block, block_ids = inputs
        allowed = (block_ids[:, None] == latent_ids[None, :]) & (pad_flags[None, :] == 0)
        scores = jnp.einsum('rhd,lhd->hrl', head_split(query_block), head_split(key_rows), precision=HIGHEST) * HEAD_DIM ** (-0.5)
        scores = jnp.where(allowed[None], low_back(scores), MASKED)
        row_max = lax.optimization_barrier(jnp.max(scores, axis=-1, keepdims=True))
        lifted = jnp.exp(scores - row_max)
        softmax_rows = low(lifted / lax.optimization_barrier(jnp.sum(lifted, axis=-1, keepdims=True)))
        mixture = jnp.einsum('hrl,lhd->rhd', softmax_rows, head_split(value_rows), precision=HIGHEST)
        return mixture.reshape(query_block.shape)
    block_count = queries.shape[0] // RAY_DEV
    mixture = lax.map(jax.checkpoint(one_block), (queries.reshape(block_count, RAY_DEV, queries.shape[1]), ray_ids.reshape(block_count, RAY_DEV)))
    return mixture.reshape(queries.shape)

def block_forward(params, ray_rows, latent_rows, ray_ids, latent_ids, pad_flags):
    query_weight, key_weight, value_weight, out_weight, out_bias, up_weight, up_bias, down_weight, down_bias, ray_gain, ray_shift, latent_gain, latent_shift, mlp_gain, mlp_shift = params
    ray_normed = low(layer_norm(ray_rows, ray_gain, ray_shift))
    queries = both_round(matmul(ray_normed, query_weight))
    latent_normed = low(layer_norm(latent_rows, latent_gain, latent_shift))
    key_rows = low(matmul(latent_normed, key_weight))
    value_rows = low(matmul(latent_normed, value_weight))
    mixture = both_round(attend(queries, key_rows, value_rows, ray_ids, latent_ids, pad_flags))
    hidden = ray_rows + low_back(matmul(mixture, out_weight) + out_bias)
    mlp_normed = low(layer_norm(hidden, mlp_gain, mlp_shift))
    pre_act = low_back(matmul(mlp_normed, up_weight) + up_bias)
    activated = low(jax.nn.gelu(pre_act))
    return hidden + low_back(matmul(activated, down_weight) + down_bias)

def reference(rays, latents, ray_scene, latent_scene, latent_pad, cotangent, query_weight, key_weight, value_weight, out_weight, out_bias, up_weight, up_bias, down_weight, down_bias, ray_gain, ray_shift, latent_gain, latent_shift, mlp_gain, mlp_shift):
    params = tuple((member.astype(jnp.float32) for member in (query_weight, key_weight, value_weight, out_weight, out_bias, up_weight, up_bias, down_weight, down_bias, ray_gain, ray_shift, latent_gain, latent_shift, mlp_gain, mlp_shift)))

    def one_item(totals, inputs):
        ray_item, latent_item, ray_ids, latent_ids, pad_flags, upstream = inputs

        def forward(weights, ray_rows, latent_rows):
            return block_forward(weights, ray_rows, latent_rows, ray_ids, latent_ids, pad_flags)
        output, pullback = jax.vjp(forward, params, ray_item.astype(jnp.float32), latent_item.astype(jnp.float32))
        weight_grads, ray_part, latent_part = pullback(upstream.astype(jnp.float32))
        totals = jax.tree.map(lambda first_term, second_term: first_term + second_term, totals, weight_grads)
        return (totals, (output.astype(jnp.bfloat16), ray_part.astype(jnp.bfloat16), latent_part.astype(jnp.bfloat16)))
    zeros_init = jax.tree.map(jnp.zeros_like, params)
    totals, results = lax.scan(one_item, zeros_init, (rays, latents, ray_scene, latent_scene, latent_pad, cotangent))
    ray_out, ray_grad, latent_grad = results
    return (ray_out, ray_grad, latent_grad, totals[0], totals[1], totals[2], totals[3], totals[4], totals[5], totals[6], totals[7], totals[8], totals[9], totals[10], totals[11], totals[12], totals[13], totals[14])
```

```python
import functools

import jax
import jax.numpy as jnp
from jax import lax
from jax.experimental import pallas as pl
from jax.experimental.pallas import tpu as pltpu
from jax.sharding import PartitionSpec as P

HEADS = 12
HEAD_DIM = 64
PAIRS = HEADS // 2
SCENES = 4
EPSILON = 1e-05
SCALE = HEAD_DIM ** (-0.5)
BLOCK = 128
WINDOW = 256
OUTSIDE = -1e30
MESH = pl.DeviceIdType.MESH
F32 = jnp.float32
BF16 = jnp.bfloat16
MIB = 2**20


def dot(left, right, left_dim=1, right_dim=0):
    return lax.dot_general(
        left, right, (((left_dim,), (right_dim,)), ((), ())), preferred_element_type=F32
    )


def stand(rows):
    center = rows - jnp.mean(rows, axis=-1, keepdims=True)
    inverse = lax.rsqrt(jnp.mean(center * center, axis=-1, keepdims=True) + EPSILON)
    return center * inverse, inverse


def norm_back(grad_out, standard, inverse, gain):
    scaled = grad_out * gain
    return inverse * (
        scaled
        - jnp.mean(scaled, axis=-1, keepdims=True)
        - standard * jnp.mean(scaled * standard, axis=-1, keepdims=True)
    )


def vmem():
    return pl.BlockSpec(memory_space=pltpu.VMEM)


def smem():
    return pl.BlockSpec(memory_space=pltpu.SMEM)


def anywhere():
    return pl.BlockSpec(memory_space=pl.ANY)


def peer(axis, bit):
    return {axis: lax.bitwise_xor(lax.axis_index(axis), bit)}


def greet(partners):
    barrier = pltpu.get_barrier_semaphore()
    for axis, bit in partners:
        pl.semaphore_signal(barrier, inc=1, device_id=peer(axis, bit), device_id_type=MESH)
    pl.semaphore_wait(barrier, len(partners))


def project_kernel(
    rays, latents, query_w, key_w, value_w, ray_gain, ray_shift, latent_gain, latent_shift,
    ray_normed, queries, keys, values, latent_normed, latent_all,
    landed, send_sem, recv_sem,
):
    me = lax.axis_index("rays")
    lat = latents.shape[0]
    near, far = ("rays", 1), ("rays", 2)
    greet([near, far])

    def copy(src, slot, partner, index):
        return pltpu.make_async_remote_copy(
            src_ref=src,
            dst_ref=landed.at[slot],
            send_sem=send_sem.at[index],
            recv_sem=recv_sem.at[index],
            device_id=peer(*partner),
            device_id_type=MESH,
        )

    to_far = copy(latents, 1, far, 1)
    to_near = copy(latents, 0, near, 0)
    to_far.start()
    to_near.start()

    chunk = 256

    @pl.loop(0, rays.shape[0] // chunk)
    def _(i):
        rows = pl.ds(pl.multiple_of(i * chunk, chunk), chunk)
        standard, _ = stand(rays[rows, :].astype(F32))
        normed = (standard * ray_gain[...] + ray_shift[...]).astype(BF16)
        ray_normed[rows, :] = normed
        projected = dot(normed, query_w[...]).astype(BF16)
        queries[rows, :] = (projected.astype(F32) * SCALE).astype(BF16)

    def one(raw, owner):
        rows = pl.ds(pl.multiple_of(owner * lat, 32), lat)
        latent_all[rows, :] = raw
        standard, _ = stand(raw.astype(F32))
        normed = (standard * latent_gain[...] + latent_shift[...]).astype(BF16)
        latent_normed[rows, :] = normed
        keys[rows, :] = dot(normed, key_w[...]).astype(BF16)
        values[rows, :] = dot(normed, value_w[...]).astype(BF16)

    total = 4 * lat
    keys[total:, :] = jnp.zeros((keys.shape[0] - total, keys.shape[1]), BF16)
    values[total:, :] = jnp.zeros((keys.shape[0] - total, keys.shape[1]), BF16)
    one(latents[...], me)
    to_far.wait_recv()
    passed = copy(landed.at[1], 2, near, 2)
    passed.start()
    to_near.wait_recv()
    one(landed[0], lax.bitwise_xor(me, 1))
    one(landed[1], lax.bitwise_xor(me, 2))
    passed.wait_recv()
    one(landed[2], lax.bitwise_xor(me, 3))
    to_far.wait_send()
    to_near.wait_send()
    passed.wait_send()


def lanes_of(shape):
    return lax.broadcasted_iota(jnp.int32, shape, len(shape) - 1)


def sort_rows(target, source, position_row):
    count = source.shape[0]
    step = 256

    @pl.loop(0, count // step)
    def _(i):
        first = pl.multiple_of(i * step, step)
        index = lax.broadcasted_iota(jnp.int32, (step, count), 0) + first
        chosen = jnp.where(index == position_row[...], 1.0, 0.0).astype(BF16)
        target[pl.ds(first, step), :] = dot(chosen, source[...]).astype(BF16)


def unsort_rows(target, source, position_column):
    count = source.shape[0]
    step = 256

    @pl.loop(0, count // step)
    def _(i):
        first = pl.multiple_of(i * step, step)
        index = lax.broadcasted_iota(jnp.int32, (step, count), 1)
        chosen = jnp.where(index == position_column[pl.ds(first, step), :], 1.0, 0.0).astype(BF16)
        target[pl.ds(first, step), :] = dot(chosen, source[...]).astype(BF16)


def latent_features(meta, extra, with_ones):
    shape = extra.shape
    row = lax.broadcasted_iota(jnp.int32, shape, 0)
    lane = lanes_of(shape)
    first = jnp.full(shape, meta[5], jnp.int32)
    last = jnp.full(shape, meta[6], jnp.int32)
    for s in range(1, SCENES):
        first = jnp.where(lane == s, meta[5 + s], first)
        last = jnp.where(lane == s, meta[6 + s], last)
    inside = (row >= first) & (row < last)
    value = jnp.where(inside | (lane >= SCENES), 0.0, OUTSIDE)
    if with_ones:
        value = jnp.where((lane >= SCENES) & (lane < SCENES + 3), 1.0, value)
    extra[...] = value.astype(BF16)


def ray_features(meta, block):
    shape = (BLOCK, 128)
    row = lax.broadcasted_iota(jnp.int32, shape, 0) + block * BLOCK
    lane = lanes_of(shape)
    value = jnp.zeros(shape, F32)
    for s in range(SCENES):
        value = jnp.where((lane == s) & (row >= meta[s]) & (row < meta[s + 1]), 1.0, value)
    return value


def half_masks():
    lane = lanes_of((BLOCK, 128))
    low = jnp.where(lane < HEAD_DIM, 1.0, 0.0)
    return low, 1.0 - low


def pick_halves(both):
    lane = lanes_of((BLOCK, 128))
    return jnp.where(lane < HEAD_DIM, both[:BLOCK, :128], both[BLOCK:, :128])


def attend_kernel(
    meta, queries, keys, values, position_row, position_column,
    mixture, sorted_queries, sorted_mixture, log_total,
    latent_extra, stacked, total, peak,
):
    rays = queries.shape[0]
    latent_features(meta, latent_extra, False)
    sort_rows(sorted_queries, queries, position_row)
    ones = jnp.where(lanes_of((WINDOW, 128)) == 0, 1.0, 0.0).astype(BF16)
    low, high = half_masks()
    lane = lanes_of((BLOCK, 128))

    @pl.loop(0, rays // BLOCK)
    def _(block):
        rows = pl.ds(pl.multiple_of(block * BLOCK, BLOCK), BLOCK)
        extra = ray_features(meta, block).astype(BF16)
        for p in range(PAIRS):
            pair = sorted_queries[rows, 128 * p : 128 * (p + 1)].astype(F32)
            stacked[p, :BLOCK, :128] = (pair * low).astype(BF16)
            stacked[p, BLOCK:, :128] = (pair * high).astype(BF16)
            stacked[p, :BLOCK, 128:] = extra
            stacked[p, BLOCK:, 128:] = extra
            total[p] = jnp.zeros((2 * BLOCK, 256), F32)
            peak[p] = jnp.full((2 * BLOCK, 1), -3e38, F32)

        @pl.loop(0, meta[18 + block])
        def _(w):
            window = pl.ds(pl.multiple_of(meta[10 + block] + w * WINDOW, 16), WINDOW)
            extra_keys = latent_extra[window, :]
            for p in range(PAIRS):
                key_side = jnp.concatenate([keys[window, 128 * p : 128 * (p + 1)], extra_keys], axis=1)
                scores = dot(stacked[p], key_side, 1, 1)
                before = peak[p]
                now = jnp.maximum(before, jnp.max(scores, axis=1, keepdims=True))
                lifted = jnp.exp(scores - now).astype(BF16)
                value_side = jnp.concatenate([values[window, 128 * p : 128 * (p + 1)], ones], axis=1)
                total[p] = total[p] * jnp.exp(before - now) + dot(lifted, value_side)
                peak[p] = now

        logs = jnp.zeros((BLOCK, 128), F32)
        for p in range(PAIRS):
            both = total[p]
            sums = both[:, 128:129]
            mixed = pick_halves(both[:, :128] * (1.0 / sums))
            sorted_mixture[rows, 128 * p : 128 * (p + 1)] = mixed.astype(BF16)
            log_rows = peak[p] + jnp.log(sums)
            logs = jnp.where(lane == 2 * p, log_rows[:BLOCK], logs)
            logs = jnp.where(lane == 2 * p + 1, log_rows[BLOCK:], logs)
        log_total[rows, :] = logs

    unsort_rows(mixture, sorted_mixture, position_column)


def three_parts(column, first_lane):
    lane = lanes_of((BLOCK, 128))
    value = -column
    top = value.astype(BF16).astype(F32)
    rest = value - top
    middle = rest.astype(BF16).astype(F32)
    lowest = rest - middle
    out = jnp.where(lane == first_lane, top, 0.0)
    out = jnp.where(lane == first_lane + 1, middle, out)
    return jnp.where(lane == first_lane + 2, lowest, out)


def attend_back_kernel(
    meta, sorted_queries, keys, values, sorted_mixture, log_total, grad_mixture, position_row, position_column,
    grad_queries, grad_keys, grad_values,
    latent_extra, stacked, stacked_grad, sorted_grad, key_total, value_total, query_total,
):
    rays = sorted_queries.shape[0]
    latent_features(meta, latent_extra, True)
    sort_rows(sorted_grad, grad_mixture, position_row)
    ones = jnp.where(lanes_of((WINDOW, 128)) < 3, 1.0, 0.0).astype(BF16)
    low, high = half_masks()
    key_total[...] = jnp.zeros(key_total.shape, F32)
    value_total[...] = jnp.zeros(value_total.shape, F32)

    @pl.loop(0, rays // BLOCK)
    def _(block):
        rows = pl.ds(pl.multiple_of(block * BLOCK, BLOCK), BLOCK)
        extra = ray_features(meta, block)
        logs = log_total[rows, :]
        for p in range(PAIRS):
            columns = slice(128 * p, 128 * (p + 1))
            pair = sorted_queries[rows, columns].astype(F32)
            grad = sorted_grad[rows, columns].astype(F32)
            product = grad * sorted_mixture[rows, columns].astype(F32)
            for side, mask in enumerate((low, high)):
                half = slice(side * BLOCK, (side + 1) * BLOCK)
                head = 2 * p + side
                stacked[p, half, :128] = (pair * mask).astype(BF16)
                stacked[p, half, 128:] = (extra + three_parts(logs[:, head : head + 1], SCENES)).astype(BF16)
                inner = jnp.sum(product * mask, axis=1, keepdims=True)
                stacked_grad[p, half, :128] = (grad * mask).astype(BF16)
                stacked_grad[p, half, 128:] = three_parts(inner, 0).astype(BF16)
            query_total[p] = jnp.zeros((2 * BLOCK, 128), F32)

        @pl.loop(0, meta[18 + block])
        def _(w):
            window = pl.ds(pl.multiple_of(meta[10 + block] + w * WINDOW, 16), WINDOW)
            extra_keys = latent_extra[window, :]
            for p in range(PAIRS):
                columns = slice(128 * p, 128 * (p + 1))
                key_pair = keys[window, columns]
                probs = jnp.exp(dot(jnp.concatenate([key_pair, extra_keys], axis=1), stacked[p], 1, 1))
                value_side = jnp.concatenate([values[window, columns], ones], axis=1)
                centered = dot(value_side, stacked_grad[p], 1, 1)
                grad_scores = (probs * centered).astype(BF16)
                value_total[window, columns] += dot(probs.astype(BF16), stacked_grad[p, :, :128])
                key_total[window, columns] += dot(grad_scores, stacked[p, :, :128])
                query_total[p] += dot(grad_scores, key_pair, 0, 0)

        for p in range(PAIRS):
            sorted_grad[rows, 128 * p : 128 * (p + 1)] = (pick_halves(query_total[p]) * SCALE).astype(BF16)

    unsort_rows(grad_queries, sorted_grad, position_column)
    count = grad_keys.shape[0]
    grad_keys[...] = key_total[:count, :].astype(BF16)
    grad_values[...] = value_total[:count, :].astype(BF16)


def mlp_kernel(
    rays, mixture, cotangent, out_w, up_w, down_w, out_bias, up_bias, down_bias, mlp_gain, mlp_shift,
    ray_out, grad_mixture, grad_hidden, early, sums,
    act, grad_pre, normed, branch,
):
    chunk = 256
    width = rays.shape[1]
    sums[...] = jnp.zeros(sums.shape, F32)
    root = 0.7978845608028654
    cubic = 0.044715

    @pl.loop(0, rays.shape[0] // chunk)
    def _(i):
        rows = pl.ds(pl.multiple_of(i * chunk, chunk), chunk)
        hidden = rays[rows, :].astype(F32) + dot(mixture[rows, :], out_w[...]) + out_bias[...]
        standard, inverse = stand(hidden)
        low = (standard * mlp_gain[...] + mlp_shift[...]).astype(BF16)
        normed[rows, :] = low
        upstream = cotangent[rows, :]
        half = 768
        out = hidden + down_bias[...]
        grad_mlp = jnp.zeros((chunk, width), F32)
        for j in range(up_w.shape[1] // half):
            cols = slice(j * half, (j + 1) * half)
            pre = dot(low, up_w[:, cols]) + up_bias[:, cols]
            square = pre * pre
            bend = jnp.tanh(root * pre * (1.0 + cubic * square))
            rise = 0.5 * (1.0 + bend)
            active = (pre * rise).astype(BF16)
            slope = rise + 0.5 * pre * (1.0 - bend * bend) * (root * (1.0 + 3.0 * cubic * square))
            act[rows, cols] = active
            out = out + dot(active, down_w[cols, :])
            back = (dot(upstream, down_w[cols, :], 1, 1) * slope).astype(BF16)
            grad_pre[rows, cols] = back
            sums[1 + j : 2 + j, :] += jnp.sum(back.astype(F32), axis=0, keepdims=True)
            grad_mlp = grad_mlp + dot(back, up_w[:, cols], 1, 1)
        ray_out[rows, :] = out.astype(BF16)
        wide = upstream.astype(F32)
        sums[0:1, :] += jnp.sum(wide, axis=0, keepdims=True)
        sums[3:4, :] += jnp.sum(grad_mlp * standard, axis=0, keepdims=True)
        sums[4:5, :] += jnp.sum(grad_mlp, axis=0, keepdims=True)
        through = wide + norm_back(grad_mlp, standard, inverse, mlp_gain[...])
        grad_hidden[rows, :] = through
        rounded = through.astype(BF16)
        branch[rows, :] = rounded
        sums[5:6, :] += jnp.sum(rounded.astype(F32), axis=0, keepdims=True)
        grad_mixture[rows, :] = dot(rounded, out_w[...], 1, 1).astype(BF16)

    step = 256

    @pl.loop(0, down_w.shape[0] // step)
    def _(j):
        cols = pl.ds(pl.multiple_of(j * step, step), step)
        early[cols, :] = dot(act[:, cols], cotangent[...], 0, 0).astype(BF16)

    @pl.loop(0, width // step)
    def _(j):
        first = pl.multiple_of(j * step, step)
        cols = pl.ds(first, step)
        for h in range(2):
            part = dot(normed[:, cols], grad_pre[:, h * width : (h + 1) * width], 0, 0)
            early[pl.ds(first + (2 + h) * width, step), :] = part.astype(BF16)
        early[pl.ds(first + 4 * width, step), :] = dot(mixture[:, cols], branch[...], 0, 0).astype(BF16)


def reduce_kernel(
    orders, size,
    ray_normed, grad_queries, latent_normed, latent_all, grad_keys, grad_values, grad_hidden, rays,
    query_w, key_w, value_w, ray_gain, latent_gain, early, early_sums,
    ray_grad, latent_grad, summed, small,
    acc, landed, gathered, smalls, small_landed, latent_part, latent_landed, latent_mid,
    send_sem, recv_sem, back_send, back_recv, small_send, small_recv, latent_send, latent_recv, local_sem,
):
    bits = len(orders[0])
    partners = sorted(orders[0])
    width = rays.shape[1]
    early_rows = early.shape[0]
    greet(partners)
    load = pltpu.make_async_copy(early, acc.at[pl.ds(0, early_rows)], local_sem.at[0])
    load.start()

    def bit_of(partner):
        axis, bit = partner
        return lax.rem(lax.div(lax.axis_index(axis), bit), 2)

    groups = []
    for g, order in enumerate(orders):
        groups.append({"order": order, "start": g * size, "size": size, "base": g * size, "step": 0, "sends": [], "starts": [], "live": None})

    def remote(src, dst, send, recv, partner):
        return pltpu.make_async_remote_copy(
            src_ref=src, dst_ref=dst, send_sem=send, recv_sem=recv,
            device_id=peer(*partner), device_id_type=MESH,
        )

    def begin(g):
        group = groups[g]
        step = group["step"]
        partner = group["order"][step]
        half = group["size"] // 2
        mine = bit_of(partner)
        give = pl.multiple_of(group["start"] + (1 - mine) * half, 16)
        keep = pl.multiple_of(group["start"] + mine * half, 16)
        slot = group["base"] + size - group["size"]
        copy = remote(
            acc.at[pl.ds(give, half)], landed.at[pl.ds(slot, half)],
            send_sem.at[g * bits + step], recv_sem.at[g * bits + step], partner,
        )
        copy.start()
        group["live"] = (copy, keep, slot, half)
        group["starts"].append(group["start"])

    def finish(g):
        group = groups[g]
        copy, keep, slot, half = group["live"]
        copy.wait_recv()
        tile = min(half, 64)
        result = gathered if group["step"] == bits - 1 else acc

        @pl.loop(0, half // tile)
        def _(i):
            here = pl.ds(pl.multiple_of(keep + i * tile, 16), tile)
            there = pl.ds(pl.multiple_of(slot + i * tile, 16), tile)
            result[here, :] = (acc[here, :].astype(F32) + landed[there, :].astype(F32)).astype(BF16)

        copy.wait_send()
        group["start"], group["size"] = keep, half
        group["step"] += 1

    def begin_back(g):
        group = groups[g]
        step = group["step"] - 1
        partner = group["order"][step]
        rows = pl.ds(pl.multiple_of(group["start"], 16), group["size"])
        copy = remote(
            gathered.at[rows], gathered.at[rows],
            back_send.at[g * bits + step], back_recv.at[g * bits + step], partner,
        )
        copy.start()
        group["live"] = copy

    def finish_back(g):
        group = groups[g]
        group["live"].wait_recv()
        group["live"].wait_send()
        group["step"] -= 1
        group["start"] = group["starts"][group["step"]]
        group["size"] *= 2

    phase = [0] * len(groups)
    stores = []

    def advance(g):
        at = phase[g]
        phase[g] += 1
        if at == 0:
            begin(g)
        elif at < bits:
            finish(g)
            begin(g)
        elif at == bits:
            finish(g)
            begin_back(g)
        elif at < 2 * bits:
            finish_back(g)
            begin_back(g)
        elif at == 2 * bits:
            finish_back(g)
            rows = pl.ds(g * size, size)
            store = pltpu.make_async_copy(gathered.at[rows], summed.at[rows], local_sem.at[1 + g])
            store.start()
            stores.append(store)

    me = lax.axis_index("rays")
    lat = latent_landed.shape[1]
    near, far = ("rays", 1), ("rays", 2)

    smalls[0] = jnp.zeros(smalls.shape[1:], F32)
    smalls[0, 0:8, :] = early_sums[...]
    load.wait()
    ready = early_rows // size
    for g in range(ready):
        advance(g)

    for i in range(4):
        rows = slice(i * lat, (i + 1) * lat)
        part = dot(grad_keys[rows, :], key_w[...], 1, 1) + dot(grad_values[rows, :], value_w[...], 1, 1)
        standard, _ = stand(latent_all[rows, :].astype(F32))
        smalls[0, 8:9, :] += jnp.sum(part * standard, axis=0, keepdims=True)
        smalls[0, 9:10, :] += jnp.sum(part, axis=0, keepdims=True)
        latent_part[i] = part.astype(BF16)
    own_bit = lax.rem(me, 2)
    first_copies = []
    for i in range(2):
        copy = remote(
            latent_part.at[2 * i + 1 - own_bit], latent_landed.at[i], latent_send.at[i], latent_recv.at[i], near
        )
        copy.start()
        first_copies.append(copy)

    for g in range(ready):
        advance(g)

    step = 256
    for which, (left, right) in enumerate(
        ((ray_normed, grad_queries), (latent_normed, grad_keys), (latent_normed, grad_values))
    ):

        @pl.loop(0, width // step)
        def _(j):
            first = pl.multiple_of(j * step, step)
            part = dot(left[:, pl.ds(first, step)], right[...], 0, 0)
            acc[pl.ds(first + early_rows + which * width, step), :] = part.astype(BF16)

        if which == 0:
            for copy in first_copies:
                copy.wait_recv()
                copy.wait_send()
            other = lax.bitwise_xor(me, 2)
            sent = lax.div(other, 2)
            latent_mid[...] = (latent_part[other].astype(F32) + latent_landed[sent].astype(F32)).astype(BF16)
            second = remote(latent_mid, latent_landed.at[2], latent_send.at[2], latent_recv.at[2], far)
            second.start()
            for g in range(ready):
                advance(g)
    for g in range(ready, len(groups)):
        advance(g)

    chunk = 256

    @pl.loop(0, rays.shape[0] // chunk)
    def _(i):
        rows = pl.ds(pl.multiple_of(i * chunk, chunk), chunk)
        grad_normed = dot(grad_queries[rows, :], query_w[...], 1, 1)
        standard, inverse = stand(rays[rows, :].astype(F32))
        smalls[0, 6:7, :] += jnp.sum(grad_normed * standard, axis=0, keepdims=True)
        smalls[0, 7:8, :] += jnp.sum(grad_normed, axis=0, keepdims=True)
        ray_grad[rows, :] = (
            grad_hidden[rows, :] + norm_back(grad_normed, standard, inverse, ray_gain[...])
        ).astype(BF16)

    small_copies = []

    def small_begin(t):
        copy = remote(smalls.at[t], small_landed.at[t], small_send.at[t], small_recv.at[t], partners[t])
        copy.start()
        small_copies.append(copy)

    small_begin(0)
    for g in range(ready):
        advance(g)

    second.wait_recv()
    second.wait_send()
    own = lax.div(me, 2)
    grad_normed = (
        latent_part[me].astype(F32) + latent_landed[own].astype(F32) + latent_landed[2].astype(F32)
    )
    standard, inverse = stand(latent_all[pl.ds(pl.multiple_of(me * lat, 32), lat), :].astype(F32))
    latent_grad[...] = norm_back(grad_normed, standard, inverse, latent_gain[...]).astype(BF16)

    small_step = 0
    while any(at <= 2 * bits for at in phase):
        for g in range(len(groups)):
            advance(g)
        if small_step < bits:
            small_copies[small_step].wait_recv()
            smalls[small_step + 1] = smalls[small_step] + small_landed[small_step]
            small_copies[small_step].wait_send()
            small_step += 1
            if small_step < bits:
                small_begin(small_step)
    small[...] = smalls[bits]
    for store in stores:
        store.wait()


def log2(n):
    return n.bit_length() - 1


def ways(items, ray_parts):
    if (items, ray_parts) == (8, 4):
        core, y, x, z, zz = ("rays", 1), ("rays", 2), ("items", 1), ("items", 2), ("items", 4)
        a = (core, x, y, z, zz)
        b = (core, y, x, z, zz)
        c = (core, z, zz, x, y)
        return 1024, (a, b, c, a, b, c)
    order = tuple(("items", 1 << i) for i in range(log2(items))) + tuple(
        ("rays", 1 << i) for i in range(log2(ray_parts))
    )
    return 16 * items * ray_parts, (order,) * (6144 // (16 * items * ray_parts))


def on_device(
    items, ray_parts,
    rays, latents, ray_scene, latent_scene, latent_pad, cotangent,
    query_weight, key_weight, value_weight, out_weight, out_bias, up_weight, up_bias, down_weight, down_bias,
    ray_gain, ray_shift, latent_gain, latent_shift, mlp_gain, mlp_shift,
):
    _, count, width = rays.shape
    lat = latents.shape[1]
    total = lat * ray_parts
    padded = total + WINDOW
    hidden_width = up_weight.shape[1]
    x = rays[0]
    upstream = cotangent[0]

    def row(v):
        return v.reshape(1, -1)

    scene = ray_scene[0]
    order_key = scene * count + jnp.arange(count, dtype=jnp.int32)
    position = jnp.sum((order_key[None, :] < order_key[:, None]).astype(jnp.int32), axis=1)
    scene_list = jnp.arange(SCENES + 1, dtype=jnp.int32)
    ray_first = jnp.sum((scene[None, :] < scene_list[:, None]).astype(jnp.int32), axis=1)
    lat_first = jnp.sum(
        ((latent_scene[0][None, :] < scene_list[:, None]) & (latent_pad[0][None, :] == 0)).astype(jnp.int32), axis=1
    )
    block_first = jnp.arange(count // BLOCK, dtype=jnp.int32) * BLOCK

    def bound(at, edges):
        scene_at = jnp.sum((ray_first[None, 1:SCENES] <= at[:, None]).astype(jnp.int32), axis=1)
        return jnp.sum(jnp.where(scene_at[:, None] == scene_list[None, :SCENES], edges[None, :], 0), axis=1)

    low = bound(block_first, lat_first[:SCENES]) // 16 * 16
    high = bound(block_first + BLOCK - 1, lat_first[1:])
    windows = (high - low + WINDOW - 1) // WINDOW
    meta = jnp.concatenate([ray_first, lat_first, low, windows]).astype(jnp.int32)
    position_row = position.reshape(1, count)
    position_column = position.reshape(count, 1)

    big = functools.partial(pltpu.CompilerParams, vmem_limit_bytes=58 * MIB)
    shape = jax.ShapeDtypeStruct
    rows_bf16 = shape((count, width), BF16)

    ray_normed, queries, keys, values, latent_normed, latent_all = pl.pallas_call(
        project_kernel,
        out_shape=(
            rows_bf16, rows_bf16, shape((padded, width), BF16), shape((padded, width), BF16),
            shape((total, width), BF16), shape((total, width), BF16),
        ),
        in_specs=[vmem()] * 9,
        out_specs=[vmem()] * 6,
        scratch_shapes=[
            pltpu.VMEM((3, lat, width), BF16), pltpu.SemaphoreType.DMA((3,)), pltpu.SemaphoreType.DMA((3,)),
        ],
        compiler_params=big(collective_id=1, has_side_effects=True),
        name="project",
    )(
        x, latents[0], query_weight, key_weight, value_weight,
        row(ray_gain), row(ray_shift), row(latent_gain), row(latent_shift),
    )

    mixture, sorted_queries, sorted_mixture, log_total = pl.pallas_call(
        attend_kernel,
        out_shape=(rows_bf16, rows_bf16, rows_bf16, shape((count, 128), F32)),
        in_specs=[smem()] + [vmem()] * 5,
        out_specs=[vmem()] * 4,
        scratch_shapes=[
            pltpu.VMEM((padded, 128), BF16),
            pltpu.VMEM((PAIRS, 2 * BLOCK, 256), BF16),
            pltpu.VMEM((PAIRS, 2 * BLOCK, 256), F32),
            pltpu.VMEM((PAIRS, 2 * BLOCK, 1), F32),
        ],
        compiler_params=big(),
        name="attend",
    )(meta, queries, keys, values, position_row, position_column)

    ray_out, grad_mixture, grad_hidden, early, early_sums = pl.pallas_call(
        mlp_kernel,
        out_shape=(
            rows_bf16, rows_bf16, shape((count, width), F32),
            shape((2 * hidden_width + width, width), BF16), shape((8, width), F32),
        ),
        in_specs=[vmem()] * 11,
        out_specs=[vmem()] * 5,
        scratch_shapes=[
            pltpu.VMEM((count, hidden_width), BF16), pltpu.VMEM((count, hidden_width), BF16),
            pltpu.VMEM((count, width), BF16), pltpu.VMEM((count, width), BF16),
        ],
        compiler_params=big(),
        name="mlp",
    )(
        x, mixture, upstream, out_weight, up_weight, down_weight,
        row(out_bias), row(up_bias), row(down_bias), row(mlp_gain), row(mlp_shift),
    )

    grad_queries, grad_keys, grad_values = pl.pallas_call(
        attend_back_kernel,
        out_shape=(rows_bf16, shape((total, width), BF16), shape((total, width), BF16)),
        in_specs=[smem()] + [vmem()] * 8,
        out_specs=[vmem()] * 3,
        scratch_shapes=[
            pltpu.VMEM((padded, 128), BF16),
            pltpu.VMEM((PAIRS, 2 * BLOCK, 256), BF16),
            pltpu.VMEM((PAIRS, 2 * BLOCK, 256), BF16),
            pltpu.VMEM((count, width), BF16),
            pltpu.VMEM((padded, width), F32),
            pltpu.VMEM((padded, width), F32),
            pltpu.VMEM((PAIRS, 2 * BLOCK, 128), F32),
        ],
        compiler_params=big(),
        name="attend_back",
    )(
        meta, sorted_queries, keys, values, sorted_mixture, log_total, grad_mixture, position_row, position_column
    )

    size, orders = ways(items, ray_parts)
    bits, groups = len(orders[0]), len(orders)
    dma = pltpu.SemaphoreType.DMA
    rows_all = size * groups
    ray_grad, latent_grad, summed, small = pl.pallas_call(
        functools.partial(reduce_kernel, orders, size),
        out_shape=(
            rows_bf16, shape((lat, width), BF16), shape((rows_all, width), BF16), shape((16, width), F32),
        ),
        in_specs=[vmem()] * 13 + [anywhere(), vmem()],
        out_specs=[vmem(), vmem(), anywhere(), vmem()],
        scratch_shapes=[
            pltpu.VMEM((rows_all, width), BF16),
            pltpu.VMEM((rows_all, width), BF16),
            pltpu.VMEM((rows_all, width), BF16),
            pltpu.VMEM((bits + 1, 16, width), F32),
            pltpu.VMEM((bits, 16, width), F32),
            pltpu.VMEM((4, lat, width), BF16),
            pltpu.VMEM((3, lat, width), BF16),
            pltpu.VMEM((lat, width), BF16),
            dma((groups * bits,)), dma((groups * bits,)), dma((groups * bits,)), dma((groups * bits,)),
            dma((bits,)), dma((bits,)), dma((3,)), dma((3,)), dma((1 + groups,)),
        ],
        compiler_params=big(collective_id=2, has_side_effects=True),
        name="reduce",
    )(
        ray_normed, grad_queries, latent_normed, latent_all, grad_keys, grad_values, grad_hidden, x,
        query_weight, key_weight, value_weight, row(ray_gain), row(latent_gain), early, early_sums,
    )

    def part(i):
        return summed[i * width : (i + 1) * width].astype(F32)

    down_grad = summed[: 2 * width].astype(F32)
    up_grad = jnp.concatenate([part(2), part(3)], axis=1)
    return (
        ray_out[None], ray_grad[None], latent_grad[None],
        part(5), part(6), part(7), part(4), small[5],
        up_grad, small[1:3].reshape(-1), down_grad, small[0],
        small[6], small[7], small[8], small[9], small[3], small[4],
    )


def solution(mesh):
    split = P("items", "rays", None)
    in_specs = (split, split, P("items", "rays"), P("items", None), P("items", None), split) + (P(),) * 15
    out_specs = (split, split, split) + (P(),) * 15
    return jax.shard_map(
        functools.partial(on_device, mesh.shape["items"], mesh.shape["rays"]),
        mesh=mesh, in_specs=in_specs, out_specs=out_specs, check_vma=False,
    )
```

```python
import functools

import jax
import jax.numpy as jnp
from jax import lax
from jax.experimental import pallas as pl
from jax.experimental.pallas import tpu as pltpu
from jax.sharding import PartitionSpec as P

HEADS = 12
HEAD_DIM = 64
PAIRS = HEADS // 2
SCENES = 4
EPSILON = 1e-05
SCALE = HEAD_DIM ** (-0.5)
BLOCK = 128
WINDOW = 256
OUTSIDE = -1e30
MESH = pl.DeviceIdType.MESH
F32 = jnp.float32
BF16 = jnp.bfloat16
MIB = 2**20


def dot(left, right, left_dim=1, right_dim=0):
    return lax.dot_general(
        left, right, (((left_dim,), (right_dim,)), ((), ())), preferred_element_type=F32
    )


def stand(rows):
    center = rows - jnp.mean(rows, axis=-1, keepdims=True)
    inverse = lax.rsqrt(jnp.mean(center * center, axis=-1, keepdims=True) + EPSILON)
    return center * inverse, inverse


def norm_back(grad_out, standard, inverse, gain):
    scaled = grad_out * gain
    return inverse * (
        scaled
        - jnp.mean(scaled, axis=-1, keepdims=True)
        - standard * jnp.mean(scaled * standard, axis=-1, keepdims=True)
    )


def vmem():
    return pl.BlockSpec(memory_space=pltpu.VMEM)


def smem():
    return pl.BlockSpec(memory_space=pltpu.SMEM)


def anywhere():
    return pl.BlockSpec(memory_space=pl.ANY)


def peer(axis, bit):
    return {axis: lax.bitwise_xor(lax.axis_index(axis), bit)}


def greet(partners):
    barrier = pltpu.get_barrier_semaphore()
    for axis, bit in partners:
        pl.semaphore_signal(barrier, inc=1, device_id=peer(axis, bit), device_id_type=MESH)
    pl.semaphore_wait(barrier, len(partners))


def project_kernel(
    rays, latents, query_w, key_w, value_w, ray_gain, ray_shift, latent_gain, latent_shift,
    ray_normed, queries, keys, values, latent_normed, latent_all,
    landed, send_sem, recv_sem,
):
    me = lax.axis_index("rays")
    lat = latents.shape[0]
    near, far = ("rays", 1), ("rays", 2)
    greet([near, far])

    def copy(src, slot, partner, index):
        return pltpu.make_async_remote_copy(
            src_ref=src,
            dst_ref=landed.at[slot],
            send_sem=send_sem.at[index],
            recv_sem=recv_sem.at[index],
            device_id=peer(*partner),
            device_id_type=MESH,
        )

    to_far = copy(latents, 1, far, 1)
    to_near = copy(latents, 0, near, 0)
    to_far.start()
    to_near.start()

    chunk = 256

    @pl.loop(0, rays.shape[0] // chunk)
    def _(i):
        rows = pl.ds(pl.multiple_of(i * chunk, chunk), chunk)
        standard, _ = stand(rays[rows, :].astype(F32))
        normed = (standard * ray_gain[...] + ray_shift[...]).astype(BF16)
        ray_normed[rows, :] = normed
        projected = dot(normed, query_w[...]).astype(BF16)
        queries[rows, :] = (projected.astype(F32) * SCALE).astype(BF16)

    def one(raw, owner):
        rows = pl.ds(pl.multiple_of(owner * lat, 32), lat)
        latent_all[rows, :] = raw
        standard, _ = stand(raw.astype(F32))
        normed = (standard * latent_gain[...] + latent_shift[...]).astype(BF16)
        latent_normed[rows, :] = normed
        keys[rows, :] = dot(normed, key_w[...]).astype(BF16)
        values[rows, :] = dot(normed, value_w[...]).astype(BF16)

    total = 4 * lat
    keys[total:, :] = jnp.zeros((keys.shape[0] - total, keys.shape[1]), BF16)
    values[total:, :] = jnp.zeros((keys.shape[0] - total, keys.shape[1]), BF16)
    one(latents[...], me)
    to_far.wait_recv()
    passed = copy(landed.at[1], 2, near, 2)
    passed.start()
    to_near.wait_recv()
    one(landed[0], lax.bitwise_xor(me, 1))
    one(landed[1], lax.bitwise_xor(me, 2))
    passed.wait_recv()
    one(landed[2], lax.bitwise_xor(me, 3))
    to_far.wait_send()
    to_near.wait_send()
    passed.wait_send()


def lanes_of(shape):
    return lax.broadcasted_iota(jnp.int32, shape, len(shape) - 1)


def rows_of(shape):
    return lax.broadcasted_iota(jnp.int32, shape, 0)


def sort_plan(ray_scene, latent_scene, latent_pad, meta, position_row, position_column):
    count = ray_scene.shape[1]
    for s in range(1, SCENES):
        meta[s] = jnp.sum(jnp.where(ray_scene[...] < s, 1, 0))
    meta[0] = 0
    meta[SCENES] = count
    meta[SCENES + 1] = 0
    for s in range(1, SCENES + 1):
        meta[SCENES + 1 + s] = jnp.sum(jnp.where((latent_scene[...] < s) & (latent_pad[...] == 0), 1, 0))
    order_row = (ray_scene[...] * count + lanes_of((1, count))).astype(F32)
    order_column = jnp.broadcast_to(order_row, (8, count)).T[:, :1]
    step = 256
    smaller = jnp.zeros((1, count), F32)
    for i in range(count // step):
        before = jnp.where(order_column[i * step : (i + 1) * step] < order_row, 1.0, 0.0)
        smaller = smaller + jnp.sum(before, axis=0, keepdims=True)
    position_row[...] = smaller.astype(jnp.int32)
    position_column[...] = jnp.broadcast_to(smaller, (8, count)).T[:, :1].astype(jnp.int32)


def block_range(meta, block):
    first, last = block * BLOCK, block * BLOCK + BLOCK - 1
    low = sum(jnp.where(meta[s] <= first, 1, 0) for s in range(1, SCENES))
    high = sum(jnp.where(meta[s] <= last, 1, 0) for s in range(1, SCENES))
    start = meta[SCENES + 1 + low] // 16 * 16
    return start, (meta[SCENES + 2 + high] - start + WINDOW - 1) // WINDOW


def sort_rows(target, source, position_row):
    count = source.shape[0]
    step = 512

    @pl.loop(0, count // step)
    def _(i):
        first = pl.multiple_of(i * step, step)
        index = rows_of((step, count)) + first
        chosen = jnp.where(index == position_row[...], 1.0, 0.0).astype(BF16)
        target[pl.ds(first, step), :] = dot(chosen, source[...]).astype(BF16)


def unsort_rows(target, source, position_column):
    count = source.shape[0]
    step = 512

    @pl.loop(0, count // step)
    def _(i):
        first = pl.multiple_of(i * step, step)
        index = lanes_of((step, count))
        chosen = jnp.where(index == position_column[pl.ds(first, step), :], 1.0, 0.0).astype(BF16)
        target[pl.ds(first, step), :] = dot(chosen, source[...]).astype(BF16)


def latent_features(meta, extra, with_ones):
    shape = extra.shape
    row = rows_of(shape)
    lane = lanes_of((1, shape[1]))
    first = jnp.full((1, shape[1]), meta[SCENES + 1], jnp.int32)
    last = jnp.full((1, shape[1]), meta[SCENES + 2], jnp.int32)
    for s in range(1, SCENES):
        first = jnp.where(lane == s, meta[SCENES + 1 + s], first)
        last = jnp.where(lane == s, meta[SCENES + 2 + s], last)
    first = jnp.where(lane >= SCENES, 0, first)
    last = jnp.where(lane >= SCENES, shape[0], last)
    value = jnp.where((row >= first) & (row < last), 0.0, OUTSIDE)
    if with_ones:
        value = value + jnp.where((lane >= SCENES) & (lane < SCENES + 3), 1.0, 0.0)
    extra[...] = value.astype(BF16)


def ray_features(meta, block):
    shape = (BLOCK, 128)
    row = rows_of(shape) + block * BLOCK
    lane = lanes_of((1, 128))
    first = jnp.full((1, 128), count_none, jnp.int32)
    last = jnp.zeros((1, 128), jnp.int32)
    for s in range(SCENES):
        first = jnp.where(lane == s, meta[s], first)
        last = jnp.where(lane == s, meta[s + 1], last)
    return jnp.where((row >= first) & (row < last), 1.0, 0.0)


count_none = 2**30


def half_masks():
    lane = lanes_of((BLOCK, 128))
    low = jnp.where(lane < HEAD_DIM, 1.0, 0.0)
    return low, 1.0 - low


def pick_halves(both):
    lane = lanes_of((BLOCK, 128))
    return jnp.where(lane < HEAD_DIM, both[:BLOCK, :128], both[BLOCK:, :128])


def pair_columns(p):
    return slice(128 * p, 128 * (p + 1))


def attend_kernel(
    queries, keys, values, ray_scene, latent_scene, latent_pad,
    mixture, sorted_queries, sorted_mixture, log_total, meta, position_row, position_column,
    latent_extra, stacked, total, peak, held,
):
    rays = queries.shape[0]
    sort_plan(ray_scene, latent_scene, latent_pad, meta, position_row, position_column)
    latent_features(meta, latent_extra, False)
    sort_rows(sorted_queries, queries, position_row)
    ones = jnp.where(lanes_of((WINDOW, 128)) == 0, 1.0, 0.0).astype(BF16)
    low, high = half_masks()
    lane = lanes_of((BLOCK, 128))

    @pl.loop(0, rays // BLOCK)
    def _(block):
        rows = pl.ds(pl.multiple_of(block * BLOCK, BLOCK), BLOCK)
        start, windows = block_range(meta, block)
        extra = ray_features(meta, block).astype(BF16)
        for p in range(PAIRS):
            pair = sorted_queries[rows, pair_columns(p)].astype(F32)
            stacked[p, :BLOCK, :128] = (pair * low).astype(BF16)
            stacked[p, BLOCK:, :128] = (pair * high).astype(BF16)
            stacked[p, :BLOCK, 128:] = extra
            stacked[p, BLOCK:, 128:] = extra
            peak[p] = jnp.full((2 * BLOCK, 128), -3e38, F32)
            total[p] = jnp.zeros((2 * BLOCK, 256), F32)

        @pl.loop(0, windows)
        def _(w):
            window = pl.ds(pl.multiple_of(start + w * WINDOW, 16), WINDOW)
            extra_keys = latent_extra[window, :]
            for p in range(PAIRS):
                key_side = jnp.concatenate([keys[window, pair_columns(p)], extra_keys], axis=1)
                scores = dot(stacked[p], key_side, 1, 1)
                held[w, p] = scores
                peak[p] = jnp.maximum(peak[p], jnp.maximum(scores[:, :128], scores[:, 128:]))

        for p in range(PAIRS):
            peak[p] = jnp.broadcast_to(jnp.max(peak[p], axis=1, keepdims=True), (2 * BLOCK, 128))

        @pl.loop(0, windows)
        def _(w):
            window = pl.ds(pl.multiple_of(start + w * WINDOW, 16), WINDOW)
            for p in range(PAIRS):
                top = peak[p]
                lifted = jnp.exp(held[w, p] - jnp.concatenate([top, top], axis=1)).astype(BF16)
                value_side = jnp.concatenate([values[window, pair_columns(p)], ones], axis=1)
                total[p] += dot(lifted, value_side)

        logs = jnp.zeros((BLOCK, 128), F32)
        for p in range(PAIRS):
            both = total[p]
            sums = both[:, 128:129]
            mixed = pick_halves(both[:, :128] * (1.0 / sums))
            sorted_mixture[rows, pair_columns(p)] = mixed.astype(BF16)
            log_rows = peak[p] + jnp.log(sums)
            logs = jnp.where(lane == 2 * p, log_rows[:BLOCK], logs)
            logs = jnp.where(lane == 2 * p + 1, log_rows[BLOCK:], logs)
        log_total[rows, :] = logs

    unsort_rows(mixture, sorted_mixture, position_column)


def three_parts(column, first_lane):
    lane = lanes_of((BLOCK, 128))
    value = -column
    top = value.astype(BF16).astype(F32)
    rest = value - top
    middle = rest.astype(BF16).astype(F32)
    lowest = rest - middle
    out = jnp.where(lane == first_lane, top, 0.0)
    out = jnp.where(lane == first_lane + 1, middle, out)
    return jnp.where(lane == first_lane + 2, lowest, out)


def attend_back_kernel(
    meta, sorted_queries, keys, values, sorted_mixture, log_total, grad_mixture, position_row, position_column,
    grad_queries, grad_keys, grad_values,
    latent_extra, stacked, stacked_grad, sorted_grad, key_total, value_total, query_total, probs_low, scores_low,
):
    rays = sorted_queries.shape[0]
    latent_features(meta, latent_extra, True)
    sort_rows(sorted_grad, grad_mixture, position_row)
    ones = jnp.where(lanes_of((WINDOW, 128)) < 3, 1.0, 0.0).astype(BF16)
    low, high = half_masks()
    key_total[...] = jnp.zeros(key_total.shape, F32)
    value_total[...] = jnp.zeros(value_total.shape, F32)

    @pl.loop(0, rays // BLOCK)
    def _(block):
        rows = pl.ds(pl.multiple_of(block * BLOCK, BLOCK), BLOCK)
        start, windows = block_range(meta, block)
        extra = ray_features(meta, block)
        logs = log_total[rows, :]
        for p in range(PAIRS):
            columns = pair_columns(p)
            pair = sorted_queries[rows, columns].astype(F32)
            grad = sorted_grad[rows, columns].astype(F32)
            product = grad * sorted_mixture[rows, columns].astype(F32)
            for side, mask in enumerate((low, high)):
                half = slice(side * BLOCK, (side + 1) * BLOCK)
                head = 2 * p + side
                stacked[p, half, :128] = (pair * mask).astype(BF16)
                stacked[p, half, 128:] = (extra + three_parts(logs[:, head : head + 1], SCENES)).astype(BF16)
                inner = jnp.sum(product * mask, axis=1, keepdims=True)
                stacked_grad[p, half, :128] = (grad * mask).astype(BF16)
                stacked_grad[p, half, 128:] = three_parts(inner, 0).astype(BF16)
            query_total[p] = jnp.zeros((2 * BLOCK, 128), F32)

        @pl.loop(0, windows)
        def _(w):
            window = pl.ds(pl.multiple_of(start + w * WINDOW, 16), WINDOW)
            extra_keys = latent_extra[window, :]
            for p in range(PAIRS):
                columns = pair_columns(p)
                probs = jnp.exp(dot(jnp.concatenate([keys[window, columns], extra_keys], axis=1), stacked[p], 1, 1))
                value_side = jnp.concatenate([values[window, columns], ones], axis=1)
                centered = dot(value_side, stacked_grad[p], 1, 1)
                probs_low[p] = probs.astype(BF16)
                scores_low[p] = (probs * centered).astype(BF16)
            for p in range(PAIRS):
                columns = pair_columns(p)
                value_total[window, columns] += dot(probs_low[p], stacked_grad[p, :, :128])
                key_total[window, columns] += dot(scores_low[p], stacked[p, :, :128])
                query_total[p] += dot(scores_low[p], keys[window, columns], 0, 0)

        for p in range(PAIRS):
            sorted_grad[rows, pair_columns(p)] = (pick_halves(query_total[p]) * SCALE).astype(BF16)

    unsort_rows(grad_queries, sorted_grad, position_column)
    count = grad_keys.shape[0]
    grad_keys[...] = key_total[:count, :].astype(BF16)
    grad_values[...] = value_total[:count, :].astype(BF16)


def big(**rest):
    return pltpu.CompilerParams(vmem_limit_bytes=60 * MIB, **rest)


def run_attend(queries, keys, values, ray_scene, latent_scene, latent_pad):
    count, width = queries.shape
    padded = keys.shape[0]
    shape = jax.ShapeDtypeStruct
    rows_bf16 = shape((count, width), BF16)
    most = (padded - 1) // WINDOW + 1
    return pl.pallas_call(
        attend_kernel,
        out_shape=(
            rows_bf16, rows_bf16, rows_bf16, shape((count, 128), F32), shape((2 * SCENES + 2,), jnp.int32),
            shape((1, count), jnp.int32), shape((count, 1), jnp.int32),
        ),
        in_specs=[vmem()] * 6,
        out_specs=[vmem()] * 4 + [smem(), vmem(), vmem()],
        scratch_shapes=[
            pltpu.VMEM((padded, 128), BF16),
            pltpu.VMEM((PAIRS, 2 * BLOCK, 256), BF16),
            pltpu.VMEM((PAIRS, 2 * BLOCK, 256), F32),
            pltpu.VMEM((PAIRS, 2 * BLOCK, 128), F32),
            pltpu.VMEM((most, PAIRS, 2 * BLOCK, WINDOW), F32),
        ],
        compiler_params=big(),
        name="attend",
    )(queries, keys, values, ray_scene, latent_scene, latent_pad)


def mix_of(forward):
    return forward[0]


def run_attend_back(forward, keys, values, grad_mixture, *_):
    _, sorted_queries, sorted_mixture, log_total, meta, position_row, position_column = forward
    count, width = grad_mixture.shape
    padded = keys.shape[0]
    total = padded - WINDOW
    shape = jax.ShapeDtypeStruct
    return pl.pallas_call(
        attend_back_kernel,
        out_shape=(shape((count, width), BF16), shape((total, width), BF16), shape((total, width), BF16)),
        in_specs=[smem()] + [vmem()] * 8,
        out_specs=[vmem()] * 3,
        scratch_shapes=[
            pltpu.VMEM((padded, 128), BF16),
            pltpu.VMEM((PAIRS, 2 * BLOCK, 256), BF16),
            pltpu.VMEM((PAIRS, 2 * BLOCK, 256), BF16),
            pltpu.VMEM((count, width), BF16),
            pltpu.VMEM((padded, width), F32),
            pltpu.VMEM((padded, width), F32),
            pltpu.VMEM((PAIRS, 2 * BLOCK, 128), F32),
            pltpu.VMEM((PAIRS, WINDOW, 2 * BLOCK), BF16),
            pltpu.VMEM((PAIRS, WINDOW, 2 * BLOCK), BF16),
        ],
        compiler_params=big(),
        name="attend_back",
    )(meta, sorted_queries, keys, values, sorted_mixture, log_total, grad_mixture, position_row, position_column)


def bit_of(partner):
    axis, bit = partner
    return lax.rem(lax.div(lax.axis_index(axis), bit), 2)


def remote(src, dst, send, recv, partner):
    return pltpu.make_async_remote_copy(
        src_ref=src, dst_ref=dst, send_sem=send, recv_sem=recv, device_id=peer(*partner), device_id_type=MESH
    )


def part_start(order, size, flipped=()):
    start = 0
    for i, partner in enumerate(order[:2]):
        mine = bit_of(partner)
        if partner in flipped:
            mine = 1 - mine
        start = start + mine * (size >> (i + 1))
    return start


def mlp_kernel(
    core, orders, size,
    rays, mixture, cotangent, out_w, up_w, down_w, out_bias, up_bias, down_bias, mlp_gain, mlp_shift,
    ray_out, grad_mixture, grad_hidden, quarters, sums,
    act, grad_pre, normed, branch, early, landed, send_sem, recv_sem,
):
    chunk = 256
    width = rays.shape[1]
    half_width = width // 2
    greet([core])
    mine = bit_of(core)
    sums[...] = jnp.zeros(sums.shape, F32)
    root = 0.7978845608028654
    cubic = 0.044715

    @pl.loop(0, rays.shape[0] // chunk)
    def _(i):
        rows = pl.ds(pl.multiple_of(i * chunk, chunk), chunk)
        hidden = rays[rows, :].astype(F32) + dot(mixture[rows, :], out_w[...]) + out_bias[...]
        standard, inverse = stand(hidden)
        low = (standard * mlp_gain[...] + mlp_shift[...]).astype(BF16)
        normed[rows, :] = low
        upstream = cotangent[rows, :]
        half = 768
        out = hidden + down_bias[...]
        grad_mlp = jnp.zeros((chunk, width), F32)
        for j in range(up_w.shape[1] // half):
            cols = slice(j * half, (j + 1) * half)
            pre = dot(low, up_w[:, cols]) + up_bias[:, cols]
            square = pre * pre
            bend = jnp.tanh(root * pre * (1.0 + cubic * square))
            rise = 0.5 * (1.0 + bend)
            active = (pre * rise).astype(BF16)
            slope = rise + 0.5 * pre * (1.0 - bend * bend) * (root * (1.0 + 3.0 * cubic * square))
            act[rows, cols] = active
            out = out + dot(active, down_w[cols, :])
            back = (dot(upstream, down_w[cols, :], 1, 1) * slope).astype(BF16)
            grad_pre[rows, cols] = back
            sums[1 + j : 2 + j, :] += jnp.sum(back.astype(F32), axis=0, keepdims=True)
            grad_mlp = grad_mlp + dot(back, up_w[:, cols], 1, 1)
        ray_out[rows, :] = out.astype(BF16)
        wide = upstream.astype(F32)
        sums[0:1, :] += jnp.sum(wide, axis=0, keepdims=True)
        sums[3:4, :] += jnp.sum(grad_mlp * standard, axis=0, keepdims=True)
        sums[4:5, :] += jnp.sum(grad_mlp, axis=0, keepdims=True)
        through = wide + norm_back(grad_mlp, standard, inverse, mlp_gain[...])
        grad_hidden[rows, :] = through
        rounded = through.astype(BF16)
        branch[rows, :] = rounded
        sums[5:6, :] += jnp.sum(rounded.astype(F32), axis=0, keepdims=True)
        grad_mixture[rows, :] = dot(rounded, out_w[...], 1, 1).astype(BF16)

    step = 256
    tiles = width // step

    def swap(tile):
        rows = pl.ds(pl.multiple_of(lax.div(tile, tiles) * size + lax.rem(tile, tiles) * step, step), step)
        return remote(early.at[1 - mine, rows], landed.at[rows], send_sem.at[tile], recv_sem.at[tile], core)

    def store(tile, left, right):
        rows = pl.ds(pl.multiple_of(lax.div(tile, tiles) * size + lax.rem(tile, tiles) * step, step), step)
        part = dot(left, right, 0, 0).astype(BF16)
        early[0, rows, :] = part[:, :half_width]
        early[1, rows, :] = part[:, half_width:]
        swap(tile).start()

    @pl.loop(0, 2 * tiles)
    def _(j):
        store(j, act[:, pl.ds(pl.multiple_of(j * step, step), step)], cotangent[...])

    for h in range(2):

        @pl.loop(0, tiles)
        def _(j):
            cols = pl.ds(pl.multiple_of(j * step, step), step)
            store(j + (2 + h) * tiles, normed[:, cols], grad_pre[:, h * width : (h + 1) * width])

    @pl.loop(0, tiles)
    def _(j):
        store(j + 4 * tiles, mixture[:, pl.ds(pl.multiple_of(j * step, step), step)], branch[...])

    @pl.loop(0, 5 * tiles)
    def _(tile):
        swap(tile).wait_recv()

    quarter = size // 4
    for g, order in enumerate(orders):
        first, second = sorted(order[:2])
        for target, flipped in enumerate(((), (first,), (second,), (first, second))):
            start = pl.multiple_of(g * size + part_start(order, size, flipped), 16)
            rows = pl.ds(start, quarter)
            quarters[target, g] = (early[mine, rows, :].astype(F32) + landed[rows, :].astype(F32)).astype(BF16)

    @pl.loop(0, 5 * tiles)
    def _(tile):
        swap(tile).wait_send()


def reduce_kernel(
    core, orders, size, script, early_groups,
    quarters, from_first, from_second, from_both,
    latent_normed, grad_keys, grad_values, key_w, value_w, latent_all,
    ray_normed, grad_queries, query_w, rays, grad_hidden,
    ray_gain, latent_gain, early_sums,
    ray_grad, latent_grad, summed, small,
    v_quarters, v_first, v_second, v_both,
    v_latent_normed, v_grad_keys, v_grad_values, v_key_w, v_value_w, v_latent_all,
    v_ray_normed, v_grad_queries, v_query_w, v_rays, v_grad_hidden,
    late, late_landed, acc, landed, gathered,
    smalls, small_landed, latent_part, latent_landed, latent_mid,
    load_sem, swap_send, swap_recv, send_sem, recv_sem, back_send, back_recv,
    small_send, small_recv, latent_send, latent_recv, store_sem,
):
    bits = len(orders[0])
    partners = sorted(orders[0] + (core,))
    width = rays.shape[1]
    half_width = width // 2
    quarter = size // 4
    held = (
        v_quarters, v_first, v_second, v_both,
        v_latent_normed, v_grad_keys, v_grad_values, v_key_w, v_value_w, v_latent_all,
        v_ray_normed, v_grad_queries, v_query_w, v_rays, v_grad_hidden,
    )
    given = (
        quarters.at[0], from_first, from_second, from_both,
        latent_normed, grad_keys, grad_values, key_w, value_w, latent_all,
        ray_normed, grad_queries, query_w, rays, grad_hidden,
    )
    loads = [pltpu.make_async_copy(src, dst, load_sem.at[i]) for i, (src, dst) in enumerate(zip(given, held))]
    for load in loads:
        load.start()
    greet(partners)
    mine = bit_of(core)
    loaded = [0]

    def need(count):
        while loaded[0] < count:
            loads[loaded[0]].wait()
            loaded[0] += 1

    smalls[0] = jnp.zeros(smalls.shape[1:], F32)
    smalls[0, 0:8, :] = early_sums[...]


    class Group:
        pass

    groups = []
    for g, order in enumerate(orders):
        group = Group()
        group.order, group.start, group.size, group.step, group.starts, group.live = order, g * size, size, 0, [], None
        group.index, group.at, group.shift = g, 0, early_groups * (size - quarter)
        groups.append(group)

    def rows_at(start, count):
        return pl.ds(pl.multiple_of(start, 16), count)

    def add_rows(target, there, first, second, here, count):
        tile = next(t for t in (64, 48, 32, 16) if count % t == 0)

        @pl.loop(0, count // tile)
        def _(i):
            one = first[rows_at(here[0] + i * tile, tile), :].astype(F32)
            two = second[rows_at(here[1] + i * tile, tile), :].astype(F32)
            target[rows_at(there + i * tile, tile), :] = (one + two).astype(BF16)

    def swap_begin(group):
        rows = rows_at((group.index - early_groups) * size, size)
        i = group.index - early_groups
        group.live = remote(late.at[1 - mine, rows], late_landed.at[rows], swap_send.at[i], swap_recv.at[i], core)
        group.live.start()

    def swap_finish(group):
        group.live.wait_recv()
        base = (group.index - early_groups) * size
        add_rows(acc, group.start - group.shift, late.at[mine], late_landed, (base, base), size)
        group.live.wait_send()

    def halve_begin(group):
        partner = group.order[group.step]
        half = group.size // 2
        bit = bit_of(partner)
        give, keep = group.start + (1 - bit) * half, group.start + bit * half
        if group.index < early_groups:
            slot = (group.index + 1) * quarter - group.size
        else:
            slot = early_groups * quarter + (group.index - early_groups + 1) * size - group.size
        i = group.index * bits + group.step
        copy = remote(
            acc.at[rows_at(give - group.shift, half)], landed.at[rows_at(slot, half)], send_sem.at[i], recv_sem.at[i], partner
        )
        copy.start()
        group.starts.append(group.start)
        group.live = (copy, keep, slot, half)

    def halve_finish(group):
        copy, keep, slot, half = group.live
        copy.wait_recv()
        last = group.step == bits - 1
        here = keep - group.shift
        add_rows(gathered.at[mine] if last else acc, keep if last else here, acc, landed, (here, slot), half)
        copy.wait_send()
        group.start, group.size = keep, half
        group.step += 1

    def double_begin(group):
        rows = rows_at(group.start, group.size)
        step = group.step - 1
        i = group.index * (bits + 1) + step + 1
        partner = group.order[step] if step >= 0 else core
        piece = gathered.at[mine, rows]
        group.live = remote(piece, piece, back_send.at[i], back_recv.at[i], partner)
        group.live.start()

    def double_finish(group):
        group.live.wait_recv()
        group.live.wait_send()
        group.step -= 1
        if group.step >= 0:
            group.start = group.starts[group.step]
            group.size *= 2

    stores = []

    def store(group):
        rows = pl.ds(group.index * size, size)
        for side in range(2):
            copy = pltpu.make_async_copy(
                gathered.at[side, rows], summed.at[side, rows], store_sem.at[2 * group.index + side]
            )
            copy.start()
            stores.append(copy)

    def plan(group):
        steps = []
        halvings = bits
        if group.index < early_groups:
            halvings = bits - 2
        else:
            steps.append((swap_begin, swap_finish))
        steps += [(halve_begin, halve_finish)] * halvings
        steps += [(double_begin, double_finish)] * (bits + 1)
        return steps

    plans = [plan(group) for group in groups]

    def advance(g):
        group, steps = groups[g], plans[g]
        if group.at > 0:
            steps[group.at - 1][1](group)
        if group.at < len(steps):
            steps[group.at][0](group)
        else:
            store(group)
        group.at += 1


    me = lax.axis_index("rays")
    lat = latent_mid.shape[0]
    near, far = ("rays", 1), ("rays", 2)
    near_copies = [
        remote(latent_part.at[2 * i + 1 - lax.rem(me, 2)], latent_landed.at[i], latent_send.at[i], latent_recv.at[i], near)
        for i in range(2)
    ]
    far_copy = remote(latent_mid, latent_landed.at[2], latent_send.at[2], latent_recv.at[2], far)
    small_copies = [
        remote(smalls.at[t], small_landed.at[t], small_send.at[t], small_recv.at[t], partners[t])
        for t in range(bits + 1)
    ]

    def early_begin():
        need(4)
        for g in range(early_groups):
            group = groups[g]
            start = g * size
            for i, partner in enumerate(group.order[:2]):
                group.starts.append(start)
                start = start + bit_of(partner) * (size >> (i + 1))
            group.start, group.size, group.step, group.shift = start, quarter, 2, start - g * quarter
            total = v_quarters[g].astype(F32) + v_first[g].astype(F32) + v_second[g].astype(F32) + v_both[g].astype(F32)
            acc[pl.ds(g * quarter, quarter), :] = total.astype(BF16)
            advance(g)

    step = 256

    def weight_grad(index, left, right):
        @pl.loop(0, width // step)
        def _(j):
            first = pl.multiple_of(j * step, step)
            part = dot(left[:, pl.ds(first, step)], right[...], 0, 0).astype(BF16)
            rows = pl.ds(pl.multiple_of(index * size + first, step), step)
            late[0, rows, :] = part[:, :half_width]
            late[1, rows, :] = part[:, half_width:]

        advance(early_groups + index)

    def query_part():
        need(12)
        weight_grad(0, v_ray_normed, v_grad_queries)

    def key_part():
        need(6)
        weight_grad(1, v_latent_normed, v_grad_keys)

    def value_part():
        need(7)
        weight_grad(2, v_latent_normed, v_grad_values)

    def latents_begin():
        need(10)
        for i in range(4):
            rows = slice(i * lat, (i + 1) * lat)
            part = dot(v_grad_keys[rows, :], v_key_w[...], 1, 1) + dot(v_grad_values[rows, :], v_value_w[...], 1, 1)
            standard, _ = stand(v_latent_all[rows, :].astype(F32))
            smalls[0, 8:9, :] += jnp.sum(part * standard, axis=0, keepdims=True)
            smalls[0, 9:10, :] += jnp.sum(part, axis=0, keepdims=True)
            latent_part[i] = part.astype(BF16)
        for copy in near_copies:
            copy.start()

    def latents_next():
        for copy in near_copies:
            copy.wait_recv()
            copy.wait_send()
        other = lax.bitwise_xor(me, 2)
        latent_mid[...] = (
            latent_part[other].astype(F32) + latent_landed[lax.div(other, 2)].astype(F32)
        ).astype(BF16)
        far_copy.start()

    def latents_end():
        far_copy.wait_recv()
        far_copy.wait_send()
        grad_normed = (
            latent_part[me].astype(F32) + latent_landed[lax.div(me, 2)].astype(F32) + latent_landed[2].astype(F32)
        )
        standard, inverse = stand(v_latent_all[pl.ds(pl.multiple_of(me * lat, 32), lat), :].astype(F32))
        latent_grad[...] = norm_back(grad_normed, standard, inverse, latent_gain[...]).astype(BF16)

    def rays_part():
        need(15)
        chunk = 256

        @pl.loop(0, rays.shape[0] // chunk)
        def _(i):
            rows = pl.ds(pl.multiple_of(i * chunk, chunk), chunk)
            grad_normed = dot(v_grad_queries[rows, :], v_query_w[...], 1, 1)
            standard, inverse = stand(v_rays[rows, :].astype(F32))
            smalls[0, 6:7, :] += jnp.sum(grad_normed * standard, axis=0, keepdims=True)
            smalls[0, 7:8, :] += jnp.sum(grad_normed, axis=0, keepdims=True)
            ray_grad[rows, :] = (
                v_grad_hidden[rows, :] + norm_back(grad_normed, standard, inverse, ray_gain[...])
            ).astype(BF16)

        small_copies[0].start()

    small_at = [0]

    def small_next():
        t = small_at[0]
        small_copies[t].wait_recv()
        smalls[t + 1] = smalls[t] + small_landed[t]
        small_copies[t].wait_send()
        small_at[0] += 1
        if t + 1 <= bits:
            small_copies[t + 1].start()
        else:
            small[...] = smalls[bits + 1]

    tasks = {
        "E": early_begin, "Q": query_part, "K": key_part, "V": value_part, "L": latents_begin, "M": latents_next,
        "N": latents_end, "R": rays_part, "S": small_next,
    }
    for letter in script:
        if letter in tasks:
            tasks[letter]()
        else:
            advance(int(letter))
    while small_at[0] <= bits:
        small_next()
    while any(group.at <= len(steps) for group, steps in zip(groups, plans)):
        for g in range(len(groups)):
            if groups[g].at <= len(plans[g]):
                advance(g)
    for copy in stores:
        copy.wait()


def widen_kernel(size, summed, *refs):
    down, up, out, query, key, value, held, wide, load_sem, store_sem = refs
    width = held.shape[3] * 2
    half = width // 2
    step = held.shape[2]
    jobs = []
    for g in range(8):
        for r in range(0, width, step):
            if g < 2:
                target = down.at[pl.ds(g * width + r, step), :]
            elif g < 4:
                target = up.at[pl.ds(r, step), pl.ds((g - 2) * width, width)]
            else:
                target = (out, query, key, value)[g - 4].at[pl.ds(r, step), :]
            jobs.append((summed.at[:, pl.ds(g * size + r, step), :], target))
    slots = held.shape[0]
    loads = [pltpu.make_async_copy(src, held.at[i % slots], load_sem.at[i % slots]) for i, (src, _) in enumerate(jobs)]
    saves = [pltpu.make_async_copy(wide.at[i % slots], dst, store_sem.at[i % slots]) for i, (_, dst) in enumerate(jobs)]
    for i in range(slots):
        loads[i].start()
    for i in range(len(jobs)):
        slot = i % slots
        loads[i].wait()
        if i >= slots:
            saves[i - slots].wait()
        wide[slot, :, :half] = held[slot, 0].astype(F32)
        wide[slot, :, half:] = held[slot, 1].astype(F32)
        saves[i].start()
        if i + slots < len(jobs):
            loads[i + slots].start()
    for i in range(len(jobs) - slots, len(jobs)):
        saves[i].wait()


def log2(n):
    return n.bit_length() - 1


EARLY = 5


def ways(items, ray_parts):
    core, y, x = ("rays", 1), ("rays", 2), ("items", 1)
    others = tuple(("items", 2 << i) for i in range(log2(items) - 1)) + tuple(
        ("rays", 4 << i) for i in range(log2(ray_parts) - 2)
    )
    a, b, c, d = (x, y) + others, (y, x) + others, (x, y) + others[::-1], (y, x) + others[::-1]
    orders = (a, d, b, c, a, d, a, c)
    return core, x, y, orders, "EKVQL0126M73451RN0S27615S4036S1275S04S"


def on_device(
    items, ray_parts,
    rays, latents, ray_scene, latent_scene, latent_pad, cotangent,
    query_weight, key_weight, value_weight, out_weight, out_bias, up_weight, up_bias, down_weight, down_bias,
    ray_gain, ray_shift, latent_gain, latent_shift, mlp_gain, mlp_shift,
):
    _, count, width = rays.shape
    lat = latents.shape[1]
    total = lat * ray_parts
    padded = total + WINDOW
    hidden_width = up_weight.shape[1]
    x = rays[0]
    upstream = cotangent[0]

    def row(v):
        return v.reshape(1, -1)

    shape = jax.ShapeDtypeStruct
    rows_bf16 = shape((count, width), BF16)
    total_bf16 = shape((total, width), BF16)
    dma = pltpu.SemaphoreType.DMA

    ray_normed, queries, keys, values, latent_normed, latent_all = pl.pallas_call(
        project_kernel,
        out_shape=(
            rows_bf16, rows_bf16, shape((padded, width), BF16), shape((padded, width), BF16), total_bf16, total_bf16,
        ),
        in_specs=[vmem()] * 9,
        out_specs=[vmem()] * 6,
        scratch_shapes=[pltpu.VMEM((3, lat, width), BF16), dma((3,)), dma((3,))],
        compiler_params=big(collective_id=1, has_side_effects=True),
        name="project",
    )(
        x, latents[0], query_weight, key_weight, value_weight,
        row(ray_gain), row(ray_shift), row(latent_gain), row(latent_shift),
    )

    forward = run_attend(queries, keys, values, ray_scene, latent_scene, latent_pad)
    mixture = forward[0]

    core, first, second, orders, script = ways(items, ray_parts)
    bits = len(orders[0])
    unit = 16 << bits
    size = (width + unit - 1) // unit * unit
    quarter = size // 4
    half_width = width // 2
    groups = len(orders)
    late_groups = groups - EARLY
    quarter_bf16 = (EARLY, quarter, half_width)

    ray_out, grad_mixture, grad_hidden, quarters, early_sums = pl.pallas_call(
        functools.partial(mlp_kernel, core, orders[:EARLY], size),
        out_shape=(
            rows_bf16, rows_bf16, shape((count, width), F32), shape((4,) + quarter_bf16, BF16), shape((8, width), F32),
        ),
        in_specs=[vmem()] * 11,
        out_specs=[vmem()] * 5,
        scratch_shapes=[
            pltpu.VMEM((count, hidden_width), BF16), pltpu.VMEM((count, hidden_width), BF16),
            pltpu.VMEM((count, width), BF16), pltpu.VMEM((count, width), BF16),
            pltpu.VMEM((2, EARLY * size, half_width), BF16), pltpu.VMEM((EARLY * size, half_width), BF16),
            dma((15,)), dma((15,)),
        ],
        compiler_params=big(collective_id=2, has_side_effects=True),
        name="mlp",
    )(
        x, mixture, upstream, out_weight, up_weight, down_weight,
        row(out_bias), row(up_bias), row(down_bias), row(mlp_gain), row(mlp_shift),
    )

    def flip(index, partners):
        item, part = index // ray_parts, index % ray_parts
        for axis, bit in partners:
            item, part = (item ^ bit, part) if axis == "items" else (item, part ^ bit)
        return item * ray_parts + part

    def exchange(array, *partners):
        return lax.ppermute(
            array, ("items", "rays"), [(i, flip(i, partners)) for i in range(items * ray_parts)]
        )

    low_bit, high_bit = sorted((first, second))
    from_low = exchange(quarters[1], low_bit)
    from_high = exchange(quarters[2], high_bit)
    from_both = exchange(quarters[3], low_bit, high_bit)

    grad_queries, grad_keys, grad_values = run_attend_back(forward, keys, values, grad_mixture)

    held = [shape(quarter_bf16, BF16)] * 4 + [total_bf16] * 3 + [rows_bf16] * 0
    square = shape((width, width), BF16)
    held = held + [square, square, total_bf16, rows_bf16, rows_bf16, square, rows_bf16, shape((count, width), F32)]
    ray_grad, latent_grad, summed, small = pl.pallas_call(
        functools.partial(reduce_kernel, core, orders, size, script, EARLY),
        out_shape=(
            rows_bf16, shape((lat, width), BF16), shape((2, groups * size, half_width), BF16), shape((16, width), F32),
        ),
        in_specs=[anywhere()] * 15 + [vmem()] * 3,
        out_specs=[vmem(), vmem(), anywhere(), vmem()],
        scratch_shapes=[pltpu.VMEM(h.shape, h.dtype) for h in held] + [
            pltpu.VMEM((2, late_groups * size, half_width), BF16),
            pltpu.VMEM((late_groups * size, half_width), BF16),
            pltpu.VMEM((EARLY * quarter + late_groups * size, half_width), BF16),
            pltpu.VMEM((EARLY * quarter + late_groups * size, half_width), BF16),
            pltpu.VMEM((2, groups * size, half_width), BF16),
            pltpu.VMEM((bits + 2, 16, width), F32),
            pltpu.VMEM((bits + 1, 16, width), F32),
            pltpu.VMEM((4, lat, width), BF16),
            pltpu.VMEM((3, lat, width), BF16),
            pltpu.VMEM((lat, width), BF16),
            dma((15,)), dma((late_groups,)), dma((late_groups,)),
            dma((groups * bits,)), dma((groups * bits,)), dma((groups * (bits + 1),)), dma((groups * (bits + 1),)),
            dma((bits + 1,)), dma((bits + 1,)), dma((3,)), dma((3,)), dma((2 * groups,)),
        ],
        compiler_params=big(collective_id=3, has_side_effects=True),
        name="reduce",
    )(
        quarters, from_low, from_high, from_both,
        latent_normed, grad_keys, grad_values, key_weight, value_weight, latent_all,
        ray_normed, grad_queries, query_weight, x, grad_hidden,
        row(ray_gain), row(latent_gain), early_sums,
    )

    wide = shape((width, width), F32)
    step, slots = 256, 4
    down_grad, up_grad, out_grad, query_grad, key_grad, value_grad = pl.pallas_call(
        functools.partial(widen_kernel, size),
        out_shape=(shape((2 * width, width), F32), shape((width, 2 * width), F32), wide, wide, wide, wide),
        in_specs=[anywhere()],
        out_specs=[anywhere()] * 6,
        scratch_shapes=[
            pltpu.VMEM((slots, 2, step, half_width), BF16), pltpu.VMEM((slots, step, width), F32),
            dma((slots,)), dma((slots,)),
        ],
        name="widen",
    )(summed)

    return (
        ray_out[None], ray_grad[None], latent_grad[None],
        query_grad, key_grad, value_grad, out_grad, small[5],
        up_grad, small[1:3].reshape(-1), down_grad, small[0],
        small[6], small[7], small[8], small[9], small[3], small[4],
    )


def solution(mesh):
    split = P("items", "rays", None)
    in_specs = (split, split, P("items", "rays"), P("items", None), P("items", None), split) + (P(),) * 15
    out_specs = (split, split, split) + (P(),) * 15
    return jax.shard_map(
        functools.partial(on_device, mesh.shape["items"], mesh.shape["rays"]),
        mesh=mesh, in_specs=in_specs, out_specs=out_specs, check_vma=False,
    )
```

```python
import functools

import jax
import jax.numpy as jnp
from jax import lax
from jax.experimental import pallas as pl
from jax.experimental.pallas import tpu as pltpu
from jax.sharding import PartitionSpec as P

HEADS = 12
HEAD_DIM = 64
PAIRS = HEADS // 2
SCENES = 4
EPSILON = 1e-05
SCALE = HEAD_DIM ** (-0.5)
BLOCK = 128
WINDOW = 256
OUTSIDE = -1e30
MESH = pl.DeviceIdType.MESH
F32 = jnp.float32
BF16 = jnp.bfloat16
MIB = 2**20


def dot(left, right, left_dim=1, right_dim=0):
    return lax.dot_general(
        left, right, (((left_dim,), (right_dim,)), ((), ())), preferred_element_type=F32
    )


def stand(rows):
    center = rows - jnp.mean(rows, axis=-1, keepdims=True)
    inverse = lax.rsqrt(jnp.mean(center * center, axis=-1, keepdims=True) + EPSILON)
    return center * inverse, inverse


def norm_back(grad_out, standard, inverse, gain):
    scaled = grad_out * gain
    return inverse * (
        scaled
        - jnp.mean(scaled, axis=-1, keepdims=True)
        - standard * jnp.mean(scaled * standard, axis=-1, keepdims=True)
    )


def as_row(vector):
    return vector[...].reshape(1, -1)


def vmem():
    return pl.BlockSpec(memory_space=pltpu.VMEM)


def smem():
    return pl.BlockSpec(memory_space=pltpu.SMEM)


def anywhere():
    return pl.BlockSpec(memory_space=pl.ANY)


def peer(axis, bit):
    return {axis: lax.bitwise_xor(lax.axis_index(axis), bit)}


def greet(partners):
    barrier = pltpu.get_barrier_semaphore()
    for axis, bit in partners:
        pl.semaphore_signal(barrier, inc=1, device_id=peer(axis, bit), device_id_type=MESH)
    pl.semaphore_wait(barrier, len(partners))


def project_kernel(
    rays, latents, query_w, key_w, value_w, ray_gain, ray_shift, latent_gain, latent_shift,
    ray_normed, queries, keys, values, latent_normed, latent_all,
    landed, send_sem, recv_sem,
):
    me = lax.axis_index("rays")
    lat = latents.shape[0]
    near, far = ("rays", 1), ("rays", 2)
    greet([near, far])

    def copy(src, slot, partner, index):
        return pltpu.make_async_remote_copy(
            src_ref=src,
            dst_ref=landed.at[slot],
            send_sem=send_sem.at[index],
            recv_sem=recv_sem.at[index],
            device_id=peer(*partner),
            device_id_type=MESH,
        )

    to_far = copy(latents, 1, far, 1)
    to_near = copy(latents, 0, near, 0)
    to_far.start()
    to_near.start()

    chunk = 256

    @pl.loop(0, rays.shape[0] // chunk)
    def _(i):
        rows = pl.ds(pl.multiple_of(i * chunk, chunk), chunk)
        standard, _ = stand(rays[rows, :].astype(F32))
        normed = (standard * as_row(ray_gain) + as_row(ray_shift)).astype(BF16)
        ray_normed[rows, :] = normed
        projected = dot(normed, query_w[...]).astype(BF16)
        queries[rows, :] = (projected.astype(F32) * SCALE).astype(BF16)

    def one(raw, owner):
        rows = pl.ds(pl.multiple_of(owner * lat, 32), lat)
        latent_all[rows, :] = raw
        standard, _ = stand(raw.astype(F32))
        normed = (standard * as_row(latent_gain) + as_row(latent_shift)).astype(BF16)
        latent_normed[rows, :] = normed
        keys[rows, :] = dot(normed, key_w[...]).astype(BF16)
        values[rows, :] = dot(normed, value_w[...]).astype(BF16)

    total = 4 * lat
    keys[total:, :] = jnp.zeros((keys.shape[0] - total, keys.shape[1]), BF16)
    values[total:, :] = jnp.zeros((keys.shape[0] - total, keys.shape[1]), BF16)
    one(latents[...], me)
    to_far.wait_recv()
    passed = copy(landed.at[1], 2, near, 2)
    passed.start()
    to_near.wait_recv()
    one(landed[0], lax.bitwise_xor(me, 1))
    one(landed[1], lax.bitwise_xor(me, 2))
    passed.wait_recv()
    one(landed[2], lax.bitwise_xor(me, 3))
    to_far.wait_send()
    to_near.wait_send()
    passed.wait_send()


def lanes_of(shape):
    return lax.broadcasted_iota(jnp.int32, shape, len(shape) - 1)


def rows_of(shape):
    return lax.broadcasted_iota(jnp.int32, shape, 0)


def sort_plan(ray_scene, latent_scene, latent_pad, meta, position_row, position_column):
    count = ray_scene.shape[1]
    for s in range(1, SCENES):
        meta[s] = jnp.sum(jnp.where(ray_scene[...] < s, 1, 0))
    meta[0] = 0
    meta[SCENES] = count
    meta[SCENES + 1] = 0
    for s in range(1, SCENES + 1):
        meta[SCENES + 1 + s] = jnp.sum(jnp.where((latent_scene[...] < s) & (latent_pad[...] == 0), 1, 0))
    order_row = (ray_scene[...] * count + lanes_of((1, count))).astype(F32)
    order_column = jnp.broadcast_to(order_row, (8, count)).T[:, :1]
    step = 256
    smaller = jnp.zeros((1, count), F32)
    for i in range(count // step):
        before = jnp.where(order_column[i * step : (i + 1) * step] < order_row, 1.0, 0.0)
        smaller = smaller + jnp.sum(before, axis=0, keepdims=True)
    position_row[...] = smaller.astype(jnp.int32)
    position_column[...] = jnp.broadcast_to(smaller, (8, count)).T[:, :1].astype(jnp.int32)


def block_range(meta, block):
    first, last = block * BLOCK, block * BLOCK + BLOCK - 1
    low = sum(jnp.where(meta[s] <= first, 1, 0) for s in range(1, SCENES))
    high = sum(jnp.where(meta[s] <= last, 1, 0) for s in range(1, SCENES))
    start = meta[SCENES + 1 + low] // 16 * 16
    return start, (meta[SCENES + 2 + high] - start + WINDOW - 1) // WINDOW


def sort_rows(target, source, position_row):
    count = source.shape[0]
    step = 512

    @pl.loop(0, count // step)
    def _(i):
        first = pl.multiple_of(i * step, step)
        index = rows_of((step, count)) + first
        chosen = jnp.where(index == position_row[...], 1.0, 0.0).astype(BF16)
        target[pl.ds(first, step), :] = dot(chosen, source[...]).astype(BF16)


def unsort_rows(target, source, position_column):
    count = source.shape[0]
    step = 512

    @pl.loop(0, count // step)
    def _(i):
        first = pl.multiple_of(i * step, step)
        index = lanes_of((step, count))
        chosen = jnp.where(index == position_column[pl.ds(first, step), :], 1.0, 0.0).astype(BF16)
        target[pl.ds(first, step), :] = dot(chosen, source[...]).astype(BF16)


def latent_features(meta, extra, with_ones):
    shape = extra.shape
    row = rows_of(shape)
    lane = lanes_of((1, shape[1]))
    first = jnp.full((1, shape[1]), meta[SCENES + 1], jnp.int32)
    last = jnp.full((1, shape[1]), meta[SCENES + 2], jnp.int32)
    for s in range(1, SCENES):
        first = jnp.where(lane == s, meta[SCENES + 1 + s], first)
        last = jnp.where(lane == s, meta[SCENES + 2 + s], last)
    first = jnp.where(lane >= SCENES, 0, first)
    last = jnp.where(lane >= SCENES, shape[0], last)
    value = jnp.where((row >= first) & (row < last), 0.0, OUTSIDE)
    if with_ones:
        value = value + jnp.where((lane >= SCENES) & (lane < SCENES + 3), 1.0, 0.0)
    extra[...] = value.astype(BF16)


def ray_features(meta, block):
    shape = (BLOCK, 128)
    row = rows_of(shape) + block * BLOCK
    lane = lanes_of((1, 128))
    first = jnp.full((1, 128), count_none, jnp.int32)
    last = jnp.zeros((1, 128), jnp.int32)
    for s in range(SCENES):
        first = jnp.where(lane == s, meta[s], first)
        last = jnp.where(lane == s, meta[s + 1], last)
    return jnp.where((row >= first) & (row < last), 1.0, 0.0)


count_none = 2**30


def half_masks():
    lane = lanes_of((BLOCK, 128))
    low = jnp.where(lane < HEAD_DIM, 1.0, 0.0)
    return low, 1.0 - low


def pick_halves(both):
    lane = lanes_of((BLOCK, 128))
    return jnp.where(lane < HEAD_DIM, both[:BLOCK, :128], both[BLOCK:, :128])


def pair_columns(p):
    return slice(128 * p, 128 * (p + 1))


def attend_kernel(
    queries, keys, values, ray_scene, latent_scene, latent_pad,
    mixture, sorted_queries, sorted_mixture, log_total, meta, position_row, position_column,
    latent_extra, stacked, total, peak, held,
):
    rays = queries.shape[0]
    sort_plan(ray_scene, latent_scene, latent_pad, meta, position_row, position_column)
    latent_features(meta, latent_extra, False)
    sort_rows(sorted_queries, queries, position_row)
    ones = jnp.where(lanes_of((WINDOW, 128)) == 0, 1.0, 0.0).astype(BF16)
    low, high = half_masks()
    lane = lanes_of((BLOCK, 128))

    @pl.loop(0, rays // BLOCK)
    def _(block):
        rows = pl.ds(pl.multiple_of(block * BLOCK, BLOCK), BLOCK)
        start, windows = block_range(meta, block)
        extra = ray_features(meta, block).astype(BF16)
        for p in range(PAIRS):
            pair = sorted_queries[rows, pair_columns(p)].astype(F32)
            stacked[p, :BLOCK, :128] = (pair * low).astype(BF16)
            stacked[p, BLOCK:, :128] = (pair * high).astype(BF16)
            stacked[p, :BLOCK, 128:] = extra
            stacked[p, BLOCK:, 128:] = extra
            peak[p] = jnp.full((2 * BLOCK, 128), -3e38, F32)
            total[p] = jnp.zeros((2 * BLOCK, 256), F32)

        @pl.loop(0, windows)
        def _(w):
            window = pl.ds(pl.multiple_of(start + w * WINDOW, 16), WINDOW)
            extra_keys = latent_extra[window, :]
            for p in range(PAIRS):
                key_side = jnp.concatenate([keys[window, pair_columns(p)], extra_keys], axis=1)
                scores = dot(stacked[p], key_side, 1, 1)
                held[w, p] = scores
                peak[p] = jnp.maximum(peak[p], jnp.maximum(scores[:, :128], scores[:, 128:]))

        for p in range(PAIRS):
            peak[p] = jnp.broadcast_to(jnp.max(peak[p], axis=1, keepdims=True), (2 * BLOCK, 128))

        @pl.loop(0, windows)
        def _(w):
            window = pl.ds(pl.multiple_of(start + w * WINDOW, 16), WINDOW)
            for p in range(PAIRS):
                top = peak[p]
                lifted = jnp.exp(held[w, p] - jnp.concatenate([top, top], axis=1)).astype(BF16)
                value_side = jnp.concatenate([values[window, pair_columns(p)], ones], axis=1)
                total[p] += dot(lifted, value_side)

        logs = jnp.zeros((BLOCK, 128), F32)
        for p in range(PAIRS):
            both = total[p]
            sums = both[:, 128:129]
            mixed = pick_halves(both[:, :128] * (1.0 / sums))
            sorted_mixture[rows, pair_columns(p)] = mixed.astype(BF16)
            log_rows = peak[p] + jnp.log(sums)
            logs = jnp.where(lane == 2 * p, log_rows[:BLOCK], logs)
            logs = jnp.where(lane == 2 * p + 1, log_rows[BLOCK:], logs)
        log_total[rows, :] = logs

    unsort_rows(mixture, sorted_mixture, position_column)


def three_parts(column, first_lane):
    lane = lanes_of((BLOCK, 128))
    value = -column
    top = value.astype(BF16).astype(F32)
    rest = value - top
    middle = rest.astype(BF16).astype(F32)
    lowest = rest - middle
    out = jnp.where(lane == first_lane, top, 0.0)
    out = jnp.where(lane == first_lane + 1, middle, out)
    return jnp.where(lane == first_lane + 2, lowest, out)


def attend_back_kernel(
    meta, sorted_queries, keys, values, sorted_mixture, log_total, grad_mixture, position_row, position_column,
    grad_queries, grad_keys, grad_values,
    latent_extra, stacked, stacked_grad, sorted_grad, key_total, value_total, query_total, probs_low, scores_low,
):
    rays = sorted_queries.shape[0]
    latent_features(meta, latent_extra, True)
    sort_rows(sorted_grad, grad_mixture, position_row)
    ones = jnp.where(lanes_of((WINDOW, 128)) < 3, 1.0, 0.0).astype(BF16)
    low, high = half_masks()
    key_total[...] = jnp.zeros(key_total.shape, F32)
    value_total[...] = jnp.zeros(value_total.shape, F32)

    @pl.loop(0, rays // BLOCK)
    def _(block):
        rows = pl.ds(pl.multiple_of(block * BLOCK, BLOCK), BLOCK)
        start, windows = block_range(meta, block)
        extra = ray_features(meta, block)
        logs = log_total[rows, :]
        for p in range(PAIRS):
            columns = pair_columns(p)
            pair = sorted_queries[rows, columns].astype(F32)
            grad = sorted_grad[rows, columns].astype(F32)
            product = grad * sorted_mixture[rows, columns].astype(F32)
            for side, mask in enumerate((low, high)):
                half = slice(side * BLOCK, (side + 1) * BLOCK)
                head = 2 * p + side
                stacked[p, half, :128] = (pair * mask).astype(BF16)
                stacked[p, half, 128:] = (extra + three_parts(logs[:, head : head + 1], SCENES)).astype(BF16)
                inner = jnp.sum(product * mask, axis=1, keepdims=True)
                stacked_grad[p, half, :128] = (grad * mask).astype(BF16)
                stacked_grad[p, half, 128:] = three_parts(inner, 0).astype(BF16)
            query_total[p] = jnp.zeros((2 * BLOCK, 128), F32)

        @pl.loop(0, windows)
        def _(w):
            window = pl.ds(pl.multiple_of(start + w * WINDOW, 16), WINDOW)
            extra_keys = latent_extra[window, :]
            for p in range(PAIRS):
                columns = pair_columns(p)
                probs = jnp.exp(dot(jnp.concatenate([keys[window, columns], extra_keys], axis=1), stacked[p], 1, 1))
                value_side = jnp.concatenate([values[window, columns], ones], axis=1)
                centered = dot(value_side, stacked_grad[p], 1, 1)
                probs_low[p] = probs.astype(BF16)
                scores_low[p] = (probs * centered).astype(BF16)
            for p in range(PAIRS):
                columns = pair_columns(p)
                value_total[window, columns] += dot(probs_low[p], stacked_grad[p, :, :128])
                key_total[window, columns] += dot(scores_low[p], stacked[p, :, :128])
                query_total[p] += dot(scores_low[p], keys[window, columns], 0, 0)

        for p in range(PAIRS):
            sorted_grad[rows, pair_columns(p)] = (pick_halves(query_total[p]) * SCALE).astype(BF16)

    unsort_rows(grad_queries, sorted_grad, position_column)
    count = grad_keys.shape[0]
    grad_keys[...] = key_total[:count, :].astype(BF16)
    grad_values[...] = value_total[:count, :].astype(BF16)


def big(**rest):
    return pltpu.CompilerParams(vmem_limit_bytes=60 * MIB, **rest)


def run_attend(queries, keys, values, ray_scene, latent_scene, latent_pad):
    count, width = queries.shape
    padded = keys.shape[0]
    shape = jax.ShapeDtypeStruct
    rows_bf16 = shape((count, width), BF16)
    most = (padded - 1) // WINDOW + 1
    return pl.pallas_call(
        attend_kernel,
        out_shape=(
            rows_bf16, rows_bf16, rows_bf16, shape((count, 128), F32), shape((2 * SCENES + 2,), jnp.int32),
            shape((1, count), jnp.int32), shape((count, 1), jnp.int32),
        ),
        in_specs=[vmem()] * 6,
        out_specs=[vmem()] * 4 + [smem(), vmem(), vmem()],
        scratch_shapes=[
            pltpu.VMEM((padded, 128), BF16),
            pltpu.VMEM((PAIRS, 2 * BLOCK, 256), BF16),
            pltpu.VMEM((PAIRS, 2 * BLOCK, 256), F32),
            pltpu.VMEM((PAIRS, 2 * BLOCK, 128), F32),
            pltpu.VMEM((most, PAIRS, 2 * BLOCK, WINDOW), F32),
        ],
        compiler_params=big(),
        name="attend",
    )(queries, keys, values, ray_scene, latent_scene, latent_pad)


def mix_of(forward):
    return forward[0]


def run_attend_back(forward, keys, values, grad_mixture, *_):
    _, sorted_queries, sorted_mixture, log_total, meta, position_row, position_column = forward
    count, width = grad_mixture.shape
    padded = keys.shape[0]
    total = padded - WINDOW
    shape = jax.ShapeDtypeStruct
    return pl.pallas_call(
        attend_back_kernel,
        out_shape=(shape((count, width), BF16), shape((total, width), BF16), shape((total, width), BF16)),
        in_specs=[smem()] + [vmem()] * 8,
        out_specs=[vmem()] * 3,
        scratch_shapes=[
            pltpu.VMEM((padded, 128), BF16),
            pltpu.VMEM((PAIRS, 2 * BLOCK, 256), BF16),
            pltpu.VMEM((PAIRS, 2 * BLOCK, 256), BF16),
            pltpu.VMEM((count, width), BF16),
            pltpu.VMEM((padded, width), F32),
            pltpu.VMEM((padded, width), F32),
            pltpu.VMEM((PAIRS, 2 * BLOCK, 128), F32),
            pltpu.VMEM((PAIRS, WINDOW, 2 * BLOCK), BF16),
            pltpu.VMEM((PAIRS, WINDOW, 2 * BLOCK), BF16),
        ],
        compiler_params=big(),
        name="attend_back",
    )(meta, sorted_queries, keys, values, sorted_mixture, log_total, grad_mixture, position_row, position_column)


def bit_of(partner):
    axis, bit = partner
    return lax.rem(lax.div(lax.axis_index(axis), bit), 2)


def remote(src, dst, send, recv, partner):
    return pltpu.make_async_remote_copy(
        src_ref=src, dst_ref=dst, send_sem=send, recv_sem=recv, device_id=peer(*partner), device_id_type=MESH
    )


def quarter_start(first, second, size, flips):
    one = bit_of(first) if not flips[0] else 1 - bit_of(first)
    two = bit_of(second) if not flips[1] else 1 - bit_of(second)
    return one * (size // 2) + two * (size // 4)


def mlp_kernel(
    core, first, second, size,
    rays, mixture, cotangent, out_w, up_w, down_w, out_bias, up_bias, down_bias, mlp_gain, mlp_shift,
    ray_out, grad_mixture, grad_hidden, kept, to_first, to_second, to_both, sums,
    act, grad_pre, normed, branch, early, landed, send_sem, recv_sem,
):
    chunk = 256
    width = rays.shape[1]
    half_width = width // 2
    greet([core])
    mine = bit_of(core)
    sums[...] = jnp.zeros(sums.shape, F32)
    root = 0.7978845608028654
    cubic = 0.044715

    @pl.loop(0, rays.shape[0] // chunk)
    def _(i):
        rows = pl.ds(pl.multiple_of(i * chunk, chunk), chunk)
        hidden = rays[rows, :].astype(F32) + dot(mixture[rows, :], out_w[...]) + as_row(out_bias)
        standard, inverse = stand(hidden)
        low = (standard * as_row(mlp_gain) + as_row(mlp_shift)).astype(BF16)
        normed[rows, :] = low
        upstream = cotangent[rows, :]
        half = 768
        out = hidden + as_row(down_bias)
        grad_mlp = jnp.zeros((chunk, width), F32)
        for j in range(up_w.shape[1] // half):
            cols = slice(j * half, (j + 1) * half)
            pre = dot(low, up_w[:, cols]) + up_bias[cols].reshape(1, half)
            square = pre * pre
            bend = jnp.tanh(root * pre * (1.0 + cubic * square))
            rise = 0.5 * (1.0 + bend)
            active = (pre * rise).astype(BF16)
            slope = rise + 0.5 * pre * (1.0 - bend * bend) * (root * (1.0 + 3.0 * cubic * square))
            act[rows, cols] = active
            out = out + dot(active, down_w[cols, :])
            back = (dot(upstream, down_w[cols, :], 1, 1) * slope).astype(BF16)
            grad_pre[rows, cols] = back
            sums[1 + j : 2 + j, :] += jnp.sum(back.astype(F32), axis=0, keepdims=True)
            grad_mlp = grad_mlp + dot(back, up_w[:, cols], 1, 1)
        ray_out[rows, :] = out.astype(BF16)
        wide = upstream.astype(F32)
        sums[0:1, :] += jnp.sum(wide, axis=0, keepdims=True)
        sums[3:4, :] += jnp.sum(grad_mlp * standard, axis=0, keepdims=True)
        sums[4:5, :] += jnp.sum(grad_mlp, axis=0, keepdims=True)
        through = wide + norm_back(grad_mlp, standard, inverse, as_row(mlp_gain))
        grad_hidden[rows, :] = through
        rounded = through.astype(BF16)
        branch[rows, :] = rounded
        sums[5:6, :] += jnp.sum(rounded.astype(F32), axis=0, keepdims=True)
        grad_mixture[rows, :] = dot(rounded, out_w[...], 1, 1).astype(BF16)

    step = 256
    tiles = width // step

    def swap(tile):
        rows = pl.ds(pl.multiple_of(lax.div(tile, tiles) * size + lax.rem(tile, tiles) * step, step), step)
        return remote(early.at[1 - mine, rows], landed.at[rows], send_sem.at[tile], recv_sem.at[tile], core)

    def store(tile, left, right):
        rows = pl.ds(pl.multiple_of(lax.div(tile, tiles) * size + lax.rem(tile, tiles) * step, step), step)
        part = dot(left, right, 0, 0).astype(BF16)
        early[0, rows, :] = part[:, :half_width]
        early[1, rows, :] = part[:, half_width:]
        swap(tile).start()

    @pl.loop(0, 2 * tiles)
    def _(j):
        store(j, act[:, pl.ds(pl.multiple_of(j * step, step), step)], cotangent[...])

    for h in range(2):

        @pl.loop(0, tiles)
        def _(j):
            cols = pl.ds(pl.multiple_of(j * step, step), step)
            store(j + (2 + h) * tiles, normed[:, cols], grad_pre[:, h * width : (h + 1) * width])

    @pl.loop(0, tiles)
    def _(j):
        store(j + 4 * tiles, mixture[:, pl.ds(pl.multiple_of(j * step, step), step)], branch[...])

    @pl.loop(0, 5 * tiles)
    def _(tile):
        swap(tile).wait_recv()

    quarter = size // 4
    for g in range(EARLY):
        for target, flips in ((kept, (0, 0)), (to_first, (1, 0)), (to_second, (0, 1)), (to_both, (1, 1))):
            rows = pl.ds(pl.multiple_of(g * size + quarter_start(first, second, size, flips), 16), quarter)
            target[g] = (early[mine, rows, :].astype(F32) + landed[rows, :].astype(F32)).astype(BF16)

    @pl.loop(0, 5 * tiles)
    def _(tile):
        swap(tile).wait_send()


def reduce_kernel(
    core, bits, halvings, doublings, size, script,
    kept, from_first, from_second, from_both,
    latent_normed, grad_keys, grad_values, key_w, value_w, latent_all,
    ray_normed, grad_queries, query_w, rays, grad_hidden,
    ray_gain, latent_gain, early_sums,
    ray_grad, latent_grad, summed, small,
    v_kept, v_first, v_second, v_both,
    v_latent_normed, v_grad_keys, v_grad_values, v_key_w, v_value_w, v_latent_all,
    v_ray_normed, v_grad_queries, v_query_w, v_rays, v_grad_hidden,
    late, late_landed, early_acc, early_landed, late_acc, late_in, gathered,
    smalls, small_landed, latent_part, latent_landed, latent_mid,
    load_sem, swap_send, swap_recv, send_sem, recv_sem, back_send, back_recv,
    small_send, small_recv, latent_send, latent_recv, store_sem,
):
    count = len(bits)
    partners = sorted(bits + (core,))
    width = rays.shape[1]
    half_width = width // 2
    piece = size >> count
    held = (
        v_kept, v_first, v_second, v_both,
        v_latent_normed, v_grad_keys, v_grad_values, v_key_w, v_value_w, v_latent_all,
        v_ray_normed, v_grad_queries, v_query_w, v_rays, v_grad_hidden,
    )
    given = (
        kept, from_first, from_second, from_both,
        latent_normed, grad_keys, grad_values, key_w, value_w, latent_all,
        ray_normed, grad_queries, query_w, rays, grad_hidden,
    )
    loads = [pltpu.make_async_copy(src, dst, load_sem.at[i]) for i, (src, dst) in enumerate(zip(given, held))]
    for load in loads:
        load.start()
    greet(partners)
    mine = bit_of(core)
    loaded = [0]

    def need(last):
        while loaded[0] < last:
            loads[loaded[0]].wait()
            loaded[0] += 1

    smalls[0] = jnp.zeros(smalls.shape[1:], F32)
    smalls[0, 0:8, :] = early_sums[...]


    class Group:
        pass

    groups = []
    for g in range(EARLY + late_landed.shape[0] // size):
        group = Group()
        group.index, group.at, group.live = g, 0, None
        group.early = g < EARLY
        group.free = list(bits[2:] if group.early else bits)
        group.halvings, group.doublings = list(halvings[g]), list(doublings[g])
        group.done = []
        group.acc = early_acc.at[g] if group.early else late_acc.at[g - EARLY]
        group.landed = early_landed.at[g] if group.early else late_in.at[g - EARLY]
        groups.append(group)

    def combos(names):
        for i in range(1 << len(names)):
            yield {name: (i >> k) & 1 for k, name in enumerate(names)}

    def dims(group):
        return bits[2:] if group.early else bits

    def swap_begin(group):
        i = group.index - EARLY
        rows = pl.ds(i * size, size)
        group.live = remote(late.at[1 - mine, rows], late_landed.at[rows], swap_send.at[i], swap_recv.at[i], core)
        group.live.start()

    def swap_finish(group):
        group.live.wait_recv()
        base = (group.index - EARLY) * size
        for i in range(1 << count):
            rows = slice(base + i * piece, base + (i + 1) * piece)
            total = late[mine, rows, :].astype(F32) + late_landed[rows, :].astype(F32)
            group.acc[tuple((i >> (count - 1 - k)) & 1 for k in range(count))] = total.astype(BF16)
        group.live.wait_send()

    def halve_begin(group):
        bit = group.halvings[len(group.done)]
        i = group.index * count + len(group.done)

        def at(value):
            return tuple(
                pl.ds(value, 1) if d == bit else pl.ds(bit_of(d), 1) if d in group.done else slice(None)
                for d in dims(group)
            )

        own = bit_of(bit)
        group.live = remote(group.acc.at[at(1 - own)], group.landed.at[at(own)], send_sem.at[i], recv_sem.at[i], bit)
        group.live.start()

    def halve_finish(group):
        bit = group.halvings[len(group.done)]
        group.live.wait_recv()
        own = bit_of(bit)
        group.done.append(bit)
        last = len(group.done) == len(dims(group))
        for combo in combos([d for d in dims(group) if d not in group.done]):
            keep = tuple(combo[d] if d in combo else bit_of(d) for d in dims(group))
            there = tuple(1 - own if d == bit else k for d, k in zip(dims(group), keep))
            total = (group.acc[keep].astype(F32) + group.landed[there].astype(F32)).astype(BF16)
            if last:
                gathered[(mine, group.index) + tuple(bit_of(d) for d in bits)] = total
            else:
                group.acc[keep] = total
        group.live.wait_send()

    def double_begin(group):
        done = group.doublings[: group.step]
        bit = group.doublings[group.step] if group.step < count else core
        i = group.index * (count + 1) + group.step
        part = gathered.at[
            (mine, group.index) + tuple(slice(None) if d in done else pl.ds(bit_of(d), 1) for d in bits)
        ]
        group.live = remote(part, part, back_send.at[i], back_recv.at[i], bit)
        group.live.start()
        group.step += 1

    def double_finish(group):
        group.live.wait_recv()
        group.live.wait_send()

    stores = []

    def store(group):
        for side in range(2):
            copy = pltpu.make_async_copy(
                gathered.at[side, group.index], summed.at[side, group.index], store_sem.at[2 * group.index + side]
            )
            copy.start()
            stores.append(copy)

    def plan(group):
        group.step = 0
        steps = [] if group.early else [(swap_begin, swap_finish)]
        steps += [(halve_begin, halve_finish)] * len(group.halvings)
        steps += [(double_begin, double_finish)] * (count + 1)
        return steps

    plans = [plan(group) for group in groups]

    def advance(g):
        group, steps = groups[g], plans[g]
        if group.at > 0:
            steps[group.at - 1][1](group)
        if group.at < len(steps):
            steps[group.at][0](group)
        else:
            store(group)
        group.at += 1


    me = lax.axis_index("rays")
    lat = latent_mid.shape[0]
    near, far = ("rays", 1), ("rays", 2)
    near_copies = [
        remote(latent_part.at[2 * i + 1 - lax.rem(me, 2)], latent_landed.at[i], latent_send.at[i], latent_recv.at[i], near)
        for i in range(2)
    ]
    far_copy = remote(latent_mid, latent_landed.at[2], latent_send.at[2], latent_recv.at[2], far)
    small_copies = [
        remote(smalls.at[t], small_landed.at[t], small_send.at[t], small_recv.at[t], partners[t])
        for t in range(count + 1)
    ]

    def early_begin():
        need(4)
        for g in range(EARLY):
            for i in range(1 << (count - 2)):
                rows = slice(i * piece, (i + 1) * piece)
                total = v_kept[g, rows, :].astype(F32)
                for other in (v_first, v_second, v_both):
                    total = total + other[g, rows, :].astype(F32)
                early_acc[(g,) + tuple((i >> (count - 3 - k)) & 1 for k in range(count - 2))] = total.astype(BF16)
            advance(g)

    step = 256

    def weight_grad(index, left, right):
        @pl.loop(0, width // step)
        def _(j):
            first = pl.multiple_of(j * step, step)
            part = dot(left[:, pl.ds(first, step)], right[...], 0, 0).astype(BF16)
            rows = pl.ds(pl.multiple_of(index * size + first, step), step)
            late[0, rows, :] = part[:, :half_width]
            late[1, rows, :] = part[:, half_width:]

        advance(EARLY + index)

    def query_part():
        need(12)
        weight_grad(0, v_ray_normed, v_grad_queries)

    def key_part():
        need(6)
        weight_grad(1, v_latent_normed, v_grad_keys)

    def value_part():
        need(7)
        weight_grad(2, v_latent_normed, v_grad_values)

    def latents_begin():
        need(10)
        for i in range(4):
            rows = slice(i * lat, (i + 1) * lat)
            part = dot(v_grad_keys[rows, :], v_key_w[...], 1, 1) + dot(v_grad_values[rows, :], v_value_w[...], 1, 1)
            standard, _ = stand(v_latent_all[rows, :].astype(F32))
            smalls[0, 8:9, :] += jnp.sum(part * standard, axis=0, keepdims=True)
            smalls[0, 9:10, :] += jnp.sum(part, axis=0, keepdims=True)
            latent_part[i] = part.astype(BF16)
        for copy in near_copies:
            copy.start()

    def latents_next():
        for copy in near_copies:
            copy.wait_recv()
            copy.wait_send()
        other = lax.bitwise_xor(me, 2)
        latent_mid[...] = (
            latent_part[other].astype(F32) + latent_landed[lax.div(other, 2)].astype(F32)
        ).astype(BF16)
        far_copy.start()

    def latents_end():
        far_copy.wait_recv()
        far_copy.wait_send()
        grad_normed = (
            latent_part[me].astype(F32) + latent_landed[lax.div(me, 2)].astype(F32) + latent_landed[2].astype(F32)
        )
        standard, inverse = stand(v_latent_all[pl.ds(pl.multiple_of(me * lat, 32), lat), :].astype(F32))
        latent_grad[...] = norm_back(grad_normed, standard, inverse, as_row(latent_gain)).astype(BF16)

    def rays_part():
        need(15)
        chunk = 256

        @pl.loop(0, rays.shape[0] // chunk)
        def _(i):
            rows = pl.ds(pl.multiple_of(i * chunk, chunk), chunk)
            grad_normed = dot(v_grad_queries[rows, :], v_query_w[...], 1, 1)
            standard, inverse = stand(v_rays[rows, :].astype(F32))
            smalls[0, 6:7, :] += jnp.sum(grad_normed * standard, axis=0, keepdims=True)
            smalls[0, 7:8, :] += jnp.sum(grad_normed, axis=0, keepdims=True)
            ray_grad[rows, :] = (
                v_grad_hidden[rows, :] + norm_back(grad_normed, standard, inverse, as_row(ray_gain))
            ).astype(BF16)

        small_copies[0].start()

    small_at = [0]

    def small_next():
        t = small_at[0]
        small_copies[t].wait_recv()
        smalls[t + 1] = smalls[t] + small_landed[t]
        small_copies[t].wait_send()
        small_at[0] += 1
        if t + 1 <= count:
            small_copies[t + 1].start()
        else:
            small[...] = smalls[count + 1]

    tasks = {
        "E": early_begin, "Q": query_part, "K": key_part, "V": value_part, "L": latents_begin, "M": latents_next,
        "N": latents_end, "R": rays_part, "S": small_next,
    }
    for letter in script:
        if letter in tasks:
            tasks[letter]()
        else:
            advance(int(letter))
    while small_at[0] <= count:
        small_next()
    while any(group.at <= len(steps) for group, steps in zip(groups, plans)):
        for g in range(len(groups)):
            if groups[g].at <= len(plans[g]):
                advance(g)
    for copy in stores:
        copy.wait()


def widen_kernel(size, summed, small, *refs):
    down, up, out, query, key, value = refs[:6]
    vectors, up_bias, (held, wide, load_sem, store_sem) = refs[6:14], refs[14], refs[15:]
    for at, vector in zip((5, 0, 6, 7, 8, 9, 3, 4), vectors):
        vector[...] = small[at]
    up_bias[: small.shape[1]] = small[1]
    up_bias[small.shape[1] :] = small[2]
    width = held.shape[3] * 2
    half = width // 2
    step = held.shape[2]
    jobs = []
    for g in range(8):
        for r in range(0, width, step):
            if g < 2:
                target = down.at[pl.ds(g * width + r, step), :]
            elif g < 4:
                target = up.at[pl.ds(r, step), pl.ds((g - 2) * width, width)]
            else:
                target = (out, query, key, value)[g - 4].at[pl.ds(r, step), :]
            jobs.append((summed.at[:, pl.ds(g * size + r, step), :], target))
    slots = held.shape[0]
    loads = [pltpu.make_async_copy(src, held.at[i % slots], load_sem.at[i % slots]) for i, (src, _) in enumerate(jobs)]
    saves = [pltpu.make_async_copy(wide.at[i % slots], dst, store_sem.at[i % slots]) for i, (_, dst) in enumerate(jobs)]
    for i in range(slots):
        loads[i].start()
    for i in range(len(jobs)):
        slot = i % slots
        loads[i].wait()
        if i >= slots:
            saves[i - slots].wait()
        wide[slot, :, :half] = held[slot, 0].astype(F32)
        wide[slot, :, half:] = held[slot, 1].astype(F32)
        saves[i].start()
        if i + slots < len(jobs):
            loads[i + slots].start()
    for i in range(len(jobs) - slots, len(jobs)):
        saves[i].wait()


def log2(n):
    return n.bit_length() - 1


EARLY = 5


HALVINGS = ("wz", "zw", "zw", "wz", "zw", "yxzw", "zxyw", "yxwz")
DOUBLINGS = ("wzxy", "zwyx", "wzyx", "wyxz", "wzyx", "xwyz", "zwyx", "xzwy")
SCRIPT = (
    "EQKV01526L7340125RM63547S012S365S407S12NS5304657",
    "163726517031467032562475465767",
)


def ways(items, ray_parts):
    core, y, x = ("rays", 1), ("rays", 2), ("items", 1)
    bits = (x, y) + tuple(("items", 2 << i) for i in range(log2(items) - 1)) + tuple(
        ("rays", 4 << i) for i in range(log2(ray_parts) - 2)
    )
    if len(bits) != 4:
        return core, bits, (bits[2:],) * EARLY + (bits,) * 3, (bits[::-1],) * (EARLY + 3), "EKQVLRMN"
    name = dict(zip("xyzw", bits))
    halvings = tuple(tuple(name[c] for c in word) for word in HALVINGS)
    doublings = tuple(tuple(name[c] for c in word) for word in DOUBLINGS)
    return core, bits, halvings, doublings, "".join(SCRIPT)


def on_device(
    items, ray_parts,
    rays, latents, ray_scene, latent_scene, latent_pad, cotangent,
    query_weight, key_weight, value_weight, out_weight, out_bias, up_weight, up_bias, down_weight, down_bias,
    ray_gain, ray_shift, latent_gain, latent_shift, mlp_gain, mlp_shift,
):
    _, count, width = rays.shape
    lat = latents.shape[1]
    total = lat * ray_parts
    padded = total + WINDOW
    hidden_width = up_weight.shape[1]
    x = rays[0]
    upstream = cotangent[0]

    shape = jax.ShapeDtypeStruct
    rows_bf16 = shape((count, width), BF16)
    total_bf16 = shape((total, width), BF16)
    dma = pltpu.SemaphoreType.DMA

    ray_normed, queries, keys, values, latent_normed, latent_all = pl.pallas_call(
        project_kernel,
        out_shape=(
            rows_bf16, rows_bf16, shape((padded, width), BF16), shape((padded, width), BF16), total_bf16, total_bf16,
        ),
        in_specs=[vmem()] * 9,
        out_specs=[vmem()] * 6,
        scratch_shapes=[pltpu.VMEM((3, lat, width), BF16), dma((3,)), dma((3,))],
        compiler_params=big(collective_id=1, has_side_effects=True),
        name="project",
    )(
        x, latents[0], query_weight, key_weight, value_weight,
        ray_gain, ray_shift, latent_gain, latent_shift,
    )

    forward = run_attend(queries, keys, values, ray_scene, latent_scene, latent_pad)
    mixture = forward[0]

    core, bits, halvings, doublings, script = ways(items, ray_parts)
    first, second = bits[:2]
    nbits = len(bits)
    unit = 16 << nbits
    size = (width + unit - 1) // unit * unit
    quarter = size // 4
    half_width = width // 2
    groups = len(halvings)
    late_groups = groups - EARLY
    piece = (size >> nbits, half_width)
    quarter_bf16 = (EARLY, quarter, half_width)

    ray_out, grad_mixture, grad_hidden, kept, to_first, to_second, to_both, early_sums = pl.pallas_call(
        functools.partial(mlp_kernel, core, first, second, size),
        out_shape=(
            rows_bf16, rows_bf16, shape((count, width), F32),
            shape(quarter_bf16, BF16), shape(quarter_bf16, BF16), shape(quarter_bf16, BF16), shape(quarter_bf16, BF16),
            shape((8, width), F32),
        ),
        in_specs=[vmem()] * 11,
        out_specs=[vmem()] * 8,
        scratch_shapes=[
            pltpu.VMEM((count, hidden_width), BF16), pltpu.VMEM((count, hidden_width), BF16),
            pltpu.VMEM((count, width), BF16), pltpu.VMEM((count, width), BF16),
            pltpu.VMEM((2, EARLY * size, half_width), BF16), pltpu.VMEM((EARLY * size, half_width), BF16),
            dma((15,)), dma((15,)),
        ],
        compiler_params=big(collective_id=2, has_side_effects=True),
        name="mlp",
    )(
        x, mixture, upstream, out_weight, up_weight, down_weight,
        out_bias, up_bias, down_bias, mlp_gain, mlp_shift,
    )

    def flip(index, partners):
        item, part = index // ray_parts, index % ray_parts
        for axis, bit in partners:
            item, part = (item ^ bit, part) if axis == "items" else (item, part ^ bit)
        return item * ray_parts + part

    def exchange(array, *partners):
        return lax.ppermute(
            array, ("items", "rays"), [(i, flip(i, partners)) for i in range(items * ray_parts)]
        )

    from_first = exchange(to_first, first)
    from_second = exchange(to_second, second)
    from_both = exchange(to_both, first, second)

    grad_queries, grad_keys, grad_values = run_attend_back(forward, keys, values, grad_mixture)

    held = [shape(quarter_bf16, BF16)] * 4 + [total_bf16] * 3 + [rows_bf16] * 0
    square = shape((width, width), BF16)
    held = held + [square, square, total_bf16, rows_bf16, rows_bf16, square, rows_bf16, shape((count, width), F32)]
    ray_grad, latent_grad, summed, small = pl.pallas_call(
        functools.partial(reduce_kernel, core, bits, halvings, doublings, size, script),
        out_shape=(
            rows_bf16, shape((lat, width), BF16), shape((2, groups) + (2,) * nbits + piece, BF16),
            shape((16, width), F32),
        ),
        in_specs=[anywhere()] * 15 + [vmem()] * 3,
        out_specs=[vmem(), vmem(), anywhere(), vmem()],
        scratch_shapes=[pltpu.VMEM(h.shape, h.dtype) for h in held] + [
            pltpu.VMEM((2, late_groups * size, half_width), BF16),
            pltpu.VMEM((late_groups * size, half_width), BF16),
            pltpu.VMEM((EARLY,) + (2,) * (nbits - 2) + piece, BF16),
            pltpu.VMEM((EARLY,) + (2,) * (nbits - 2) + piece, BF16),
            pltpu.VMEM((late_groups,) + (2,) * nbits + piece, BF16),
            pltpu.VMEM((late_groups,) + (2,) * nbits + piece, BF16),
            pltpu.VMEM((2, groups) + (2,) * nbits + piece, BF16),
            pltpu.VMEM((nbits + 2, 16, width), F32),
            pltpu.VMEM((nbits + 1, 16, width), F32),
            pltpu.VMEM((4, lat, width), BF16),
            pltpu.VMEM((3, lat, width), BF16),
            pltpu.VMEM((lat, width), BF16),
            dma((15,)), dma((late_groups,)), dma((late_groups,)),
            dma((groups * nbits,)), dma((groups * nbits,)), dma((groups * (nbits + 1),)), dma((groups * (nbits + 1),)),
            dma((nbits + 1,)), dma((nbits + 1,)), dma((3,)), dma((3,)), dma((2 * groups,)),
        ],
        compiler_params=big(collective_id=3, has_side_effects=True),
        name="reduce",
    )(
        kept, from_first, from_second, from_both,
        latent_normed, grad_keys, grad_values, key_weight, value_weight, latent_all,
        ray_normed, grad_queries, query_weight, x, grad_hidden,
        ray_gain, latent_gain, early_sums,
    )

    wide = shape((width, width), F32)
    step, slots = 256, 4
    (
        down_grad, up_grad, out_grad, query_grad, key_grad, value_grad,
        out_bias_grad, down_bias_grad, ray_gain_grad, ray_shift_grad, latent_gain_grad, latent_shift_grad,
        mlp_gain_grad, mlp_shift_grad, up_bias_grad,
    ) = pl.pallas_call(
        functools.partial(widen_kernel, size),
        out_shape=(shape((2 * width, width), F32), shape((width, 2 * width), F32), wide, wide, wide, wide)
        + (shape((width,), F32),) * 8 + (shape((hidden_width,), F32),),
        in_specs=[anywhere(), vmem()],
        out_specs=[anywhere()] * 6 + [vmem()] * 9,
        scratch_shapes=[
            pltpu.VMEM((slots, 2, step, half_width), BF16), pltpu.VMEM((slots, step, width), F32),
            dma((slots,)), dma((slots,)),
        ],
        name="widen",
    )(summed.reshape(2, groups * size, half_width), small)

    return (
        ray_out[None], ray_grad[None], latent_grad[None],
        query_grad, key_grad, value_grad, out_grad, out_bias_grad,
        up_grad, up_bias_grad, down_grad, down_bias_grad,
        ray_gain_grad, ray_shift_grad, latent_gain_grad, latent_shift_grad, mlp_gain_grad, mlp_shift_grad,
    )


def solution(mesh):
    split = P("items", "rays", None)
    in_specs = (split, split, P("items", "rays"), P("items", None), P("items", None), split) + (P(),) * 15
    out_specs = (split, split, split) + (P(),) * 15
    return jax.shard_map(
        functools.partial(on_device, mesh.shape["items"], mesh.shape["rays"]),
        mesh=mesh, in_specs=in_specs, out_specs=out_specs, check_vma=False,
    )
```

```python
import functools

import jax
import jax.numpy as jnp
from jax import lax
from jax.experimental import pallas as pl
from jax.experimental.pallas import tpu as pltpu
from jax.sharding import PartitionSpec as P

HEADS = 12
HEAD_DIM = 64
PAIRS = HEADS // 2
SCENES = 4
EPSILON = 1e-05
SCALE = HEAD_DIM ** (-0.5)
BLOCK = 128
WINDOW = 256
OUTSIDE = -1e30
MESH = pl.DeviceIdType.MESH
F32 = jnp.float32
BF16 = jnp.bfloat16
MIB = 2**20


def dot(left, right, left_dim=1, right_dim=0):
    return lax.dot_general(
        left, right, (((left_dim,), (right_dim,)), ((), ())), preferred_element_type=F32
    )


def stand(rows):
    center = rows - jnp.mean(rows, axis=-1, keepdims=True)
    inverse = lax.rsqrt(jnp.mean(center * center, axis=-1, keepdims=True) + EPSILON)
    return center * inverse, inverse


def norm_back(grad_out, standard, inverse, gain):
    scaled = grad_out * gain
    return inverse * (
        scaled
        - jnp.mean(scaled, axis=-1, keepdims=True)
        - standard * jnp.mean(scaled * standard, axis=-1, keepdims=True)
    )


def as_row(vector):
    return vector[...].reshape(1, -1)


def vmem():
    return pl.BlockSpec(memory_space=pltpu.VMEM)


def smem():
    return pl.BlockSpec(memory_space=pltpu.SMEM)


def anywhere():
    return pl.BlockSpec(memory_space=pl.ANY)


def peer(axis, bit):
    return {axis: lax.bitwise_xor(lax.axis_index(axis), bit)}


def greet(partners):
    barrier = pltpu.get_barrier_semaphore()
    for axis, bit in partners:
        pl.semaphore_signal(barrier, inc=1, device_id=peer(axis, bit), device_id_type=MESH)
    pl.semaphore_wait(barrier, len(partners))


def bit_of(partner):
    axis, bit = partner
    return lax.rem(lax.div(lax.axis_index(axis), bit), 2)


def remote(src, dst, send, recv, partner):
    return pltpu.make_async_remote_copy(
        src_ref=src, dst_ref=dst, send_sem=send, recv_sem=recv, device_id=peer(*partner), device_id_type=MESH
    )


def project_kernel(
    rays, latents, query_w, key_w, value_w, ray_gain, ray_shift, latent_gain, latent_shift,
    ray_scene, latent_scene, latent_pad,
    ray_normed, sorted_queries, keys, values, latent_normed, latent_all, meta, position_row, position_column,
    landed, v_rays, v_latents, v_query_w, v_key_w, v_value_w,
    normed, queries, in_order, key_rows, value_rows, latent_rows,
    send_sem, recv_sem, load_sem, store_sem,
):
    me = lax.axis_index("rays")
    lat = latents.shape[0]
    total = 4 * lat
    near, far = ("rays", 1), ("rays", 2)
    pairs = ((latents, v_latents), (rays, v_rays), (query_w, v_query_w), (key_w, v_key_w), (value_w, v_value_w))
    loads = [pltpu.make_async_copy(src, dst, load_sem.at[i]) for i, (src, dst) in enumerate(pairs)]
    for load in loads:
        load.start()
    greet([near, far])

    def copy(src, slot, part, partner, index):
        return remote(src.at[part], landed.at[slot, part], send_sem.at[index], recv_sem.at[index], partner)

    whole, halves = slice(0, lat), (slice(0, lat // 2), slice(lat // 2, lat))
    to_far = [copy(latents, 1, part, far, i) for i, part in enumerate(halves)]
    to_near = copy(latents, 0, whole, near, 2)
    passed = [copy(landed.at[1], 2, part, near, 3 + i) for i, part in enumerate(halves)]
    for send in to_far:
        send.start()
    to_near.start()

    stores = []

    def keep(src, dst):
        saved = pltpu.make_async_copy(src, dst, store_sem.at[len(stores)])
        saved.start()
        stores.append(saved)

    sort_plan(ray_scene, latent_scene, latent_pad, meta, position_row, position_column)
    loads[1].wait()
    loads[2].wait()
    chunk = 256

    @pl.loop(0, rays.shape[0] // chunk)
    def _(i):
        rows = pl.ds(pl.multiple_of(i * chunk, chunk), chunk)
        standard, _ = stand(v_rays[rows, :].astype(F32))
        low = (standard * as_row(ray_gain) + as_row(ray_shift)).astype(BF16)
        normed[rows, :] = low
        projected = dot(low, v_query_w[...]).astype(BF16)
        queries[rows, :] = (projected.astype(F32) * SCALE).astype(BF16)

    keep(normed, ray_normed)
    sort_rows(in_order, queries, position_row)
    keep(in_order, sorted_queries)

    def one(raw, owner):
        rows = pl.ds(pl.multiple_of(owner * lat, 32), lat)
        standard, _ = stand(raw[...].astype(F32))
        low = (standard * as_row(latent_gain) + as_row(latent_shift)).astype(BF16)
        latent_rows[rows, :] = low
        keep(raw, latent_all.at[rows])
        keep(latent_rows.at[rows], latent_normed.at[rows])
        key_rows[rows, :] = dot(low, v_key_w[...]).astype(BF16)
        keep(key_rows.at[rows], keys.at[rows])
        value_rows[rows, :] = dot(low, v_value_w[...]).astype(BF16)
        keep(value_rows.at[rows], values.at[rows])

    key_rows[total:, :] = jnp.zeros((keys.shape[0] - total, keys.shape[1]), BF16)
    keep(key_rows.at[total:], keys.at[total:])
    keep(key_rows.at[total:], values.at[total:])
    for i in (0, 3, 4):
        loads[i].wait()
    one(v_latents, me)
    to_near.wait_recv()
    one(landed.at[0], lax.bitwise_xor(me, 1))
    for got, on in zip(to_far, passed):
        got.wait_recv()
        on.start()
    one(landed.at[1], lax.bitwise_xor(me, 2))
    for got in passed:
        got.wait_recv()
    one(landed.at[2], lax.bitwise_xor(me, 3))
    for send in to_far + [to_near] + passed:
        send.wait_send()
    for saved in stores:
        saved.wait()


def lanes_of(shape):
    return lax.broadcasted_iota(jnp.int32, shape, len(shape) - 1)


def rows_of(shape):
    return lax.broadcasted_iota(jnp.int32, shape, 0)


def sort_plan(ray_scene, latent_scene, latent_pad, meta, position_row, position_column):
    count = ray_scene.shape[1]
    for s in range(1, SCENES):
        meta[s] = jnp.sum(jnp.where(ray_scene[...] < s, 1, 0))
    meta[0] = 0
    meta[SCENES] = count
    meta[SCENES + 1] = 0
    for s in range(1, SCENES + 1):
        meta[SCENES + 1 + s] = jnp.sum(jnp.where((latent_scene[...] < s) & (latent_pad[...] == 0), 1, 0))
    order_row = (ray_scene[...] * count + lanes_of((1, count))).astype(F32)
    order_column = jnp.broadcast_to(order_row, (8, count)).T[:, :1]
    step = 256
    smaller = jnp.zeros((1, count), F32)
    for i in range(count // step):
        before = jnp.where(order_column[i * step : (i + 1) * step] < order_row, 1.0, 0.0)
        smaller = smaller + jnp.sum(before, axis=0, keepdims=True)
    position_row[...] = smaller.astype(jnp.int32)
    position_column[...] = jnp.broadcast_to(smaller, (8, count)).T[:, :1].astype(jnp.int32)


def block_range(meta, block):
    first, last = block * BLOCK, block * BLOCK + BLOCK - 1
    low = sum(jnp.where(meta[s] <= first, 1, 0) for s in range(1, SCENES))
    high = sum(jnp.where(meta[s] <= last, 1, 0) for s in range(1, SCENES))
    start = meta[SCENES + 1 + low] // 16 * 16
    return start, (meta[SCENES + 2 + high] - start + WINDOW - 1) // WINDOW


def sort_rows(target, source, position_row):
    count = source.shape[0]
    step = 512

    @pl.loop(0, count // step)
    def _(i):
        first = pl.multiple_of(i * step, step)
        index = rows_of((step, count)) + first
        chosen = jnp.where(index == position_row[...], 1.0, 0.0).astype(BF16)
        target[pl.ds(first, step), :] = dot(chosen, source[...]).astype(BF16)


def unsort_rows(target, source, position_column):
    count = source.shape[0]
    step = 512

    @pl.loop(0, count // step)
    def _(i):
        first = pl.multiple_of(i * step, step)
        index = lanes_of((step, count))
        chosen = jnp.where(index == position_column[pl.ds(first, step), :], 1.0, 0.0).astype(BF16)
        target[pl.ds(first, step), :] = dot(chosen, source[...]).astype(BF16)


def latent_features(meta, extra):
    shape = extra.shape
    row = rows_of(shape)
    lane = lanes_of((1, shape[1]))
    first = jnp.full((1, shape[1]), meta[SCENES + 1], jnp.int32)
    last = jnp.full((1, shape[1]), meta[SCENES + 2], jnp.int32)
    for s in range(1, SCENES):
        first = jnp.where(lane == s, meta[SCENES + 1 + s], first)
        last = jnp.where(lane == s, meta[SCENES + 2 + s], last)
    first = jnp.where(lane >= SCENES, 0, first)
    last = jnp.where(lane >= SCENES, shape[0], last)
    value = jnp.where((row >= first) & (row < last), 0.0, OUTSIDE)
    extra[...] = value.astype(BF16)


def ray_features(meta, block):
    shape = (BLOCK, 128)
    row = rows_of(shape) + block * BLOCK
    lane = lanes_of((1, 128))
    first = jnp.full((1, 128), count_none, jnp.int32)
    last = jnp.zeros((1, 128), jnp.int32)
    for s in range(SCENES):
        first = jnp.where(lane == s, meta[s], first)
        last = jnp.where(lane == s, meta[s + 1], last)
    return jnp.where((row >= first) & (row < last), 1.0, 0.0)


count_none = 2**30


def half_masks():
    lane = lanes_of((BLOCK, 128))
    low = jnp.where(lane < HEAD_DIM, 1.0, 0.0)
    return low, 1.0 - low


def pick_halves(both):
    lane = lanes_of((BLOCK, 128))
    return jnp.where(lane < HEAD_DIM, both[:BLOCK, :128], both[BLOCK:, :128])


def pair_columns(p):
    return slice(128 * p, 128 * (p + 1))


def over_windows(windows, body):
    @pl.loop(0, windows // 2)
    def _(i):
        body(2 * i, 2)

    @pl.when(windows % 2 == 1)
    def _():
        body(windows - 1, 1)


def attend_kernel(
    meta, sorted_queries, keys, values, position_column,
    mixture, sorted_mixture, log_total,
    latent_extra, stacked, total, peak, held,
):
    rays = sorted_queries.shape[0]
    latent_features(meta, latent_extra)
    ones = jnp.where(lanes_of((WINDOW, 128)) == 0, 1.0, 0.0).astype(BF16)
    low, high = half_masks()
    lane = lanes_of((BLOCK, 128))

    @pl.loop(0, rays // BLOCK)
    def _(block):
        rows = pl.ds(pl.multiple_of(block * BLOCK, BLOCK), BLOCK)
        start, windows = block_range(meta, block)
        extra = ray_features(meta, block).astype(BF16)
        for p in range(PAIRS):
            pair = sorted_queries[rows, pair_columns(p)].astype(F32)
            stacked[p, :BLOCK, :128] = (pair * low).astype(BF16)
            stacked[p, BLOCK:, :128] = (pair * high).astype(BF16)
            stacked[p, :BLOCK, 128:] = extra
            stacked[p, BLOCK:, 128:] = extra
            peak[p] = jnp.full((2 * BLOCK, 128), -3e38, F32)
            total[p] = jnp.zeros((2 * BLOCK, 256), F32)

        def window_at(w):
            return pl.ds(pl.multiple_of(start + w * WINDOW, 16), WINDOW)

        def score(w, number):
            for p in range(PAIRS):
                top = peak[p]
                for u in range(number):
                    window = window_at(w + u)
                    key_side = jnp.concatenate([keys[window, pair_columns(p)], latent_extra[window, :]], axis=1)
                    scores = dot(stacked[p], key_side, 1, 1)
                    held[w + u, p] = scores
                    top = jnp.maximum(top, jnp.maximum(scores[:, :128], scores[:, 128:]))
                peak[p] = top

        over_windows(windows, score)
        for p in range(PAIRS):
            peak[p] = jnp.broadcast_to(jnp.max(peak[p], axis=1, keepdims=True), (2 * BLOCK, 128))

        def mix(w, number):
            for p in range(PAIRS):
                top = peak[p]
                top = jnp.concatenate([top, top], axis=1)
                part = None
                for u in range(number):
                    lifted = jnp.exp(held[w + u, p] - top).astype(BF16)
                    value_side = jnp.concatenate([values[window_at(w + u), pair_columns(p)], ones], axis=1)
                    mixed = dot(lifted, value_side)
                    part = mixed if part is None else part + mixed
                total[p] += part

        over_windows(windows, mix)

        logs = jnp.zeros((BLOCK, 128), F32)
        for p in range(PAIRS):
            both = total[p]
            sums = both[:, 128:129]
            mixed = pick_halves(both[:, :128] * (1.0 / sums))
            sorted_mixture[rows, pair_columns(p)] = mixed.astype(BF16)
            log_rows = peak[p] + jnp.log(sums)
            logs = jnp.where(lane == 2 * p, log_rows[:BLOCK], logs)
            logs = jnp.where(lane == 2 * p + 1, log_rows[BLOCK:], logs)
        log_total[rows, :] = logs

    unsort_rows(mixture, sorted_mixture, position_column)


def attend_back_kernel(
    meta, grad_mixture, position_row, sorted_queries, sorted_mixture, log_total, keys, values,
    grad_queries, grad_keys, grad_values,
    v_queries, v_mixture, v_logs, v_keys, v_values,
    stacked, stacked_grad, sorted_grad, key_total, value_total, query_total, log_rows, inner_rows, bias, probs_low, scores_low, load_sem,
):
    rays = sorted_queries.shape[0]
    given = (sorted_queries, sorted_mixture, log_total, keys, values)
    held = (v_queries, v_mixture, v_logs, v_keys, v_values)
    loads = [pltpu.make_async_copy(src, dst, load_sem.at[i]) for i, (src, dst) in enumerate(zip(given, held))]
    for load in loads:
        load.start()
    key_total[...] = jnp.zeros(key_total.shape, F32)
    value_total[...] = jnp.zeros(value_total.shape, F32)
    sort_rows(sorted_grad, grad_mixture, position_row)
    low, high = half_masks()
    lane = lanes_of((BLOCK, 128))
    for load in loads:
        load.wait()

    @pl.loop(0, rays // BLOCK)
    def _(block):
        rows = pl.ds(pl.multiple_of(block * BLOCK, BLOCK), BLOCK)
        start, windows = block_range(meta, block)
        inner = jnp.zeros((BLOCK, 128), F32)
        for p in range(PAIRS):
            columns = pair_columns(p)
            pair = v_queries[rows, columns].astype(F32)
            grad = sorted_grad[rows, columns].astype(F32)
            product = grad * v_mixture[rows, columns].astype(F32)
            for side, mask in enumerate((low, high)):
                half = slice(side * BLOCK, (side + 1) * BLOCK)
                stacked[p, half, :] = (pair * mask).astype(BF16)
                stacked_grad[p, half, :] = (grad * mask).astype(BF16)
                inner = jnp.where(lane == 2 * p + side, jnp.sum(product * mask, axis=1, keepdims=True), inner)
            query_total[p] = jnp.zeros((2 * BLOCK, 128), F32)
        log_rows[...] = v_logs[rows, :].T
        inner_rows[...] = inner.T

        ray = lanes_of((1, BLOCK)) + block * BLOCK
        first = jnp.full((1, BLOCK), meta[SCENES + 1], jnp.int32)
        last = jnp.full((1, BLOCK), meta[SCENES + 2], jnp.int32)
        for s in range(1, SCENES):
            first = jnp.where(ray >= meta[s], meta[SCENES + 1 + s], first)
            last = jnp.where(ray >= meta[s], meta[SCENES + 2 + s], last)

        def two_rows(ref, p):
            return jnp.concatenate([ref[2 * p : 2 * p + 1, :], ref[2 * p + 1 : 2 * p + 2, :]], axis=1)

        def back(w, number):
            spots = [pl.multiple_of(start + (w + u) * WINDOW, 16) for u in range(number)]
            for u, spot in enumerate(spots):
                row = rows_of((WINDOW, BLOCK)) + spot
                bias[u] = jnp.where((row >= first) & (row < last), 0.0, OUTSIDE)
            for p in range(PAIRS):
                columns = pair_columns(p)
                for u, spot in enumerate(spots):
                    window = pl.ds(spot, WINDOW)
                    key_pair = v_keys[window, columns]
                    scores = dot(key_pair, stacked[p], 1, 1) - two_rows(log_rows, p)
                    probs = jnp.exp(scores + jnp.concatenate([bias[u], bias[u]], axis=1))
                    centered = dot(v_values[window, columns], stacked_grad[p], 1, 1) - two_rows(inner_rows, p)
                    probs_low[u, p] = probs.astype(BF16)
                    scores_low[u, p] = (probs * centered).astype(BF16)
            for p in range(PAIRS):
                columns = pair_columns(p)
                part = None
                for u, spot in enumerate(spots):
                    window = pl.ds(spot, WINDOW)
                    value_total[window, columns] += dot(probs_low[u, p], stacked_grad[p])
                    key_total[window, columns] += dot(scores_low[u, p], stacked[p])
                    query = dot(scores_low[u, p], v_keys[window, columns], 0, 0)
                    part = query if part is None else part + query
                query_total[p] += part

        over_windows(windows, back)

        for p in range(PAIRS):
            grad_queries[rows, pair_columns(p)] = (pick_halves(query_total[p]) * SCALE).astype(BF16)

    count = grad_keys.shape[0]
    grad_keys[...] = key_total[:count, :].astype(BF16)
    grad_values[...] = value_total[:count, :].astype(BF16)


def big(**rest):
    return pltpu.CompilerParams(vmem_limit_bytes=60 * MIB, **rest)


def run_attend(meta, sorted_queries, keys, values, position_column):
    count, width = sorted_queries.shape
    padded = keys.shape[0]
    shape = jax.ShapeDtypeStruct
    rows_bf16 = shape((count, width), BF16)
    most = (padded - 1) // WINDOW + 1
    return pl.pallas_call(
        attend_kernel,
        out_shape=(rows_bf16, rows_bf16, shape((count, 128), F32)),
        in_specs=[smem()] + [vmem()] * 4,
        out_specs=[vmem()] * 3,
        scratch_shapes=[
            pltpu.VMEM((padded, 128), BF16),
            pltpu.VMEM((PAIRS, 2 * BLOCK, 256), BF16),
            pltpu.VMEM((PAIRS, 2 * BLOCK, 256), F32),
            pltpu.VMEM((PAIRS, 2 * BLOCK, 128), F32),
            pltpu.VMEM((most, PAIRS, 2 * BLOCK, WINDOW), F32),
        ],
        compiler_params=big(),
        name="attend",
    )(meta, sorted_queries, keys, values, position_column)


def run_attend_back(meta, grad_mixture, position_row, sorted_queries, sorted_mixture, log_total, keys, values):
    count, width = grad_mixture.shape
    padded = keys.shape[0]
    total = padded - WINDOW
    shape = jax.ShapeDtypeStruct
    return pl.pallas_call(
        attend_back_kernel,
        out_shape=(shape((count, width), BF16), shape((total, width), BF16), shape((total, width), BF16)),
        in_specs=[smem()] + [vmem()] * 2 + [anywhere()] * 5,
        out_specs=[vmem()] * 3,
        scratch_shapes=[
            pltpu.VMEM((count, width), BF16),
            pltpu.VMEM((count, width), BF16),
            pltpu.VMEM((count, 128), F32),
            pltpu.VMEM((padded, width), BF16),
            pltpu.VMEM((padded, width), BF16),
            pltpu.VMEM((PAIRS, 2 * BLOCK, 128), BF16),
            pltpu.VMEM((PAIRS, 2 * BLOCK, 128), BF16),
            pltpu.VMEM((count, width), BF16),
            pltpu.VMEM((padded, width), F32),
            pltpu.VMEM((padded, width), F32),
            pltpu.VMEM((PAIRS, 2 * BLOCK, 128), F32),
            pltpu.VMEM((128, BLOCK), F32),
            pltpu.VMEM((128, BLOCK), F32),
            pltpu.VMEM((2, WINDOW, BLOCK), F32),
            pltpu.VMEM((2, PAIRS, WINDOW, 2 * BLOCK), BF16),
            pltpu.VMEM((2, PAIRS, WINDOW, 2 * BLOCK), BF16),
            pltpu.SemaphoreType.DMA((5,)),
        ],
        compiler_params=big(),
        name="attend_back",
    )(meta, grad_mixture, position_row, sorted_queries, sorted_mixture, log_total, keys, values)


def quarter_start(first, second, size, flips):
    one = bit_of(first) if not flips[0] else 1 - bit_of(first)
    two = bit_of(second) if not flips[1] else 1 - bit_of(second)
    return one * (size // 2) + two * (size // 4)


def mlp_kernel(
    core, first, second, size,
    given_mixture, given_out_w, given_rays, given_up_w, given_down_w, given_cotangent, out_bias, up_bias, down_bias, mlp_gain, mlp_shift,
    kept_ray_out, kept_grad_mixture, kept_grad_hidden, kept, to_first, to_second, to_both, sums,
    mixture, out_w, rays, up_w, down_w, cotangent, ray_out, grad_mixture, grad_hidden, quarters,
    act, grad_pre, normed, branch, early, landed, send_sem, recv_sem, load_sem, store_sem, quarter_sem,
):
    chunk = 512
    width = rays.shape[1]
    half_width = width // 2
    pairs = (
        (given_mixture, mixture), (given_out_w, out_w), (given_rays, rays), (given_up_w, up_w),
        (given_down_w, down_w), (given_cotangent, cotangent),
    )
    loads = [pltpu.make_async_copy(src, dst, load_sem.at[i]) for i, (src, dst) in enumerate(pairs)]
    for load in loads:
        load.start()
    greet([core])
    mine = bit_of(core)

    def keep(i):
        rows = pl.ds(pl.multiple_of(i * chunk, chunk), chunk)
        results = ((ray_out, kept_ray_out), (grad_hidden, kept_grad_hidden), (grad_mixture, kept_grad_mixture))
        return [
            pltpu.make_async_copy(src.at[rows], dst.at[rows], store_sem.at[3 * i + k])
            for k, (src, dst) in enumerate(results)
        ]

    sums[...] = jnp.zeros(sums.shape, F32)
    root = 0.7978845608028654
    cubic = 0.044715

    @pl.loop(0, rays.shape[0] // chunk)
    def _(i):
        rows = pl.ds(pl.multiple_of(i * chunk, chunk), chunk)

        def need(*which):
            @pl.when(i == 0)
            def _():
                for k in which:
                    loads[k].wait()

        need(0, 1, 2)
        hidden = rays[rows, :].astype(F32) + dot(mixture[rows, :], out_w[...]) + as_row(out_bias)
        standard, inverse = stand(hidden)
        low = (standard * as_row(mlp_gain) + as_row(mlp_shift)).astype(BF16)
        normed[rows, :] = low
        need(3, 4, 5)
        upstream = cotangent[rows, :]
        half = 768
        out = hidden + as_row(down_bias)
        grad_mlp = jnp.zeros((chunk, width), F32)
        for j in range(up_w.shape[1] // half):
            cols = slice(j * half, (j + 1) * half)
            pre = dot(low, up_w[:, cols]) + up_bias[cols].reshape(1, half)
            square = pre * pre
            bend = jnp.tanh(root * pre * (1.0 + cubic * square))
            rise = 0.5 * (1.0 + bend)
            active = (pre * rise).astype(BF16)
            slope = rise + 0.5 * pre * (1.0 - bend * bend) * (root * (1.0 + 3.0 * cubic * square))
            act[rows, cols] = active
            out = out + dot(active, down_w[cols, :])
            back = (dot(upstream, down_w[cols, :], 1, 1) * slope).astype(BF16)
            grad_pre[rows, cols] = back
            sums[1 + j : 2 + j, :] += jnp.sum(back.astype(F32), axis=0, keepdims=True)
            grad_mlp = grad_mlp + dot(back, up_w[:, cols], 1, 1)
        ray_out[rows, :] = out.astype(BF16)
        wide = upstream.astype(F32)
        sums[0:1, :] += jnp.sum(wide, axis=0, keepdims=True)
        sums[3:4, :] += jnp.sum(grad_mlp * standard, axis=0, keepdims=True)
        sums[4:5, :] += jnp.sum(grad_mlp, axis=0, keepdims=True)
        through = wide + norm_back(grad_mlp, standard, inverse, as_row(mlp_gain))
        grad_hidden[rows, :] = through
        rounded = through.astype(BF16)
        branch[rows, :] = rounded
        sums[5:6, :] += jnp.sum(rounded.astype(F32), axis=0, keepdims=True)
        grad_mixture[rows, :] = dot(rounded, out_w[...], 1, 1).astype(BF16)
        for saved in keep(i):
            saved.start()

    step = 384
    tiles = width // step

    def swap(tile):
        rows = pl.ds(pl.multiple_of(lax.div(tile, tiles) * size + lax.rem(tile, tiles) * step, step), step)
        return remote(early.at[1 - mine, rows], landed.at[rows], send_sem.at[tile], recv_sem.at[tile], core)

    def store(tile, left, right):
        rows = pl.ds(pl.multiple_of(lax.div(tile, tiles) * size + lax.rem(tile, tiles) * step, step), step)
        part = dot(left, right, 0, 0).astype(BF16)
        early[0, rows, :] = part[:, :half_width]
        early[1, rows, :] = part[:, half_width:]
        swap(tile).start()

    @pl.loop(0, 2 * tiles)
    def _(j):
        store(j, act[:, pl.ds(pl.multiple_of(j * step, step), step)], cotangent[...])

    for h in range(2):

        @pl.loop(0, tiles)
        def _(j):
            cols = pl.ds(pl.multiple_of(j * step, step), step)
            store(j + (2 + h) * tiles, normed[:, cols], grad_pre[:, h * width : (h + 1) * width])

    @pl.loop(0, tiles)
    def _(j):
        store(j + 4 * tiles, mixture[:, pl.ds(pl.multiple_of(j * step, step), step)], branch[...])

    quarter = size // 4
    targets = ((kept, (0, 0)), (to_first, (1, 0)), (to_second, (0, 1)), (to_both, (1, 1)))

    def send_off(g, k):
        return pltpu.make_async_copy(quarters.at[k, g], targets[k][0].at[g], quarter_sem.at[4 * g + k])

    for g in range(EARLY):
        for tile in range(g * tiles, (g + 1) * tiles):
            swap(tile).wait_recv()
        for k, (_, flips) in enumerate(targets):
            rows = pl.ds(pl.multiple_of(g * size + quarter_start(first, second, size, flips), 16), quarter)
            quarters[k, g] = (early[mine, rows, :].astype(F32) + landed[rows, :].astype(F32)).astype(BF16)
            send_off(g, k).start()
    for tile in range(5 * tiles):
        swap(tile).wait_send()
    for i in range(rays.shape[0] // chunk):
        for saved in keep(i):
            saved.wait()
    for g in range(EARLY):
        for k in range(4):
            send_off(g, k).wait()


def reduce_kernel(
    core, bits, halvings, doublings, size, script,
    kept, from_first, from_second, from_both,
    latent_normed, grad_keys, grad_values, key_w, value_w, latent_all,
    sorted_grad, ray_normed, query_w, rays, grad_hidden,
    ray_gain, latent_gain, early_sums, position_column,
    ray_grad, latent_grad, summed, small,
    v_kept, v_first, v_second, v_both,
    v_latent_normed, v_grad_keys, v_grad_values, v_key_w, v_value_w, v_latent_all,
    v_sorted, v_ray_normed, v_query_w, v_rays, v_grad_hidden, v_grad_queries,
    late, late_landed, early_acc, early_landed, late_acc, late_in, gathered,
    smalls, small_landed, latent_part, latent_landed, latent_mid,
    load_sem, swap_send, swap_recv, send_sem, recv_sem, back_send, back_recv,
    small_send, small_recv, latent_send, latent_recv, store_sem,
):
    count = len(bits)
    partners = sorted(bits + (core,))
    width = rays.shape[1]
    half_width = width // 2
    piece = size >> count
    held = (
        v_kept, v_first, v_second, v_both,
        v_latent_normed, v_grad_keys, v_grad_values, v_key_w, v_value_w, v_latent_all,
        v_sorted, v_ray_normed, v_query_w, v_rays, v_grad_hidden,
    )
    given = (
        kept, from_first, from_second, from_both,
        latent_normed, grad_keys, grad_values, key_w, value_w, latent_all,
        sorted_grad, ray_normed, query_w, rays, grad_hidden,
    )
    loads = [pltpu.make_async_copy(src, dst, load_sem.at[i]) for i, (src, dst) in enumerate(zip(given, held))]
    for load in loads:
        load.start()
    greet(partners)
    mine = bit_of(core)
    loaded = [0]

    def need(last):
        while loaded[0] < last:
            loads[loaded[0]].wait()
            loaded[0] += 1

    smalls[0] = jnp.zeros(smalls.shape[1:], F32)
    smalls[0, 0:8, :] = early_sums[...]


    class Group:
        pass

    groups = []
    for g in range(EARLY + late_landed.shape[0] // size):
        group = Group()
        group.index, group.at, group.live = g, 0, None
        group.early = g < EARLY
        group.free = list(bits[2:] if group.early else bits)
        group.halvings, group.doublings = list(halvings[g]), list(doublings[g])
        group.done = []
        group.acc = early_acc.at[g] if group.early else late_acc.at[g - EARLY]
        group.landed = early_landed.at[g] if group.early else late_in.at[g - EARLY]
        groups.append(group)

    def combos(names):
        for i in range(1 << len(names)):
            yield {name: (i >> k) & 1 for k, name in enumerate(names)}

    def dims(group):
        return bits[2:] if group.early else bits

    def swap_begin(group):
        i = group.index - EARLY
        rows = pl.ds(i * size, size)
        group.live = remote(late.at[1 - mine, rows], late_landed.at[rows], swap_send.at[i], swap_recv.at[i], core)
        group.live.start()

    def swap_finish(group):
        group.live.wait_recv()
        base = (group.index - EARLY) * size
        for i in range(1 << count):
            rows = slice(base + i * piece, base + (i + 1) * piece)
            total = late[mine, rows, :].astype(F32) + late_landed[rows, :].astype(F32)
            group.acc[tuple((i >> (count - 1 - k)) & 1 for k in range(count))] = total.astype(BF16)
        group.live.wait_send()

    def halve_begin(group):
        bit = group.halvings[len(group.done)]
        i = group.index * count + len(group.done)

        def at(value):
            return tuple(
                pl.ds(value, 1) if d == bit else pl.ds(bit_of(d), 1) if d in group.done else slice(None)
                for d in dims(group)
            )

        own = bit_of(bit)
        group.live = remote(group.acc.at[at(1 - own)], group.landed.at[at(own)], send_sem.at[i], recv_sem.at[i], bit)
        group.live.start()

    def halve_finish(group):
        bit = group.halvings[len(group.done)]
        group.live.wait_recv()
        own = bit_of(bit)
        group.done.append(bit)
        last = len(group.done) == len(dims(group))
        for combo in combos([d for d in dims(group) if d not in group.done]):
            keep = tuple(combo[d] if d in combo else bit_of(d) for d in dims(group))
            there = tuple(1 - own if d == bit else k for d, k in zip(dims(group), keep))
            total = (group.acc[keep].astype(F32) + group.landed[there].astype(F32)).astype(BF16)
            if last:
                gathered[(mine, group.index) + tuple(bit_of(d) for d in bits)] = total
            else:
                group.acc[keep] = total
        group.live.wait_send()

    def double_begin(group):
        done = group.doublings[: group.step]
        bit = group.doublings[group.step] if group.step < count else core
        i = group.index * (count + 1) + group.step
        part = gathered.at[
            (mine, group.index) + tuple(slice(None) if d in done else pl.ds(bit_of(d), 1) for d in bits)
        ]
        group.live = remote(part, part, back_send.at[i], back_recv.at[i], bit)
        group.live.start()
        group.step += 1

    def double_finish(group):
        group.live.wait_recv()
        group.live.wait_send()

    stores = []

    def store(group):
        for side in range(2):
            copy = pltpu.make_async_copy(
                gathered.at[side, group.index], summed.at[side, group.index], store_sem.at[2 * group.index + side]
            )
            copy.start()
            stores.append(copy)

    def plan(group):
        group.step = 0
        steps = [] if group.early else [(swap_begin, swap_finish)]
        steps += [(halve_begin, halve_finish)] * len(group.halvings)
        steps += [(double_begin, double_finish)] * (count + 1)
        return steps

    plans = [plan(group) for group in groups]

    def advance(g):
        group, steps = groups[g], plans[g]
        if group.at > 0:
            steps[group.at - 1][1](group)
        if group.at < len(steps):
            steps[group.at][0](group)
        else:
            store(group)
        group.at += 1


    me = lax.axis_index("rays")
    lat = latent_mid.shape[0]
    near, far = ("rays", 1), ("rays", 2)
    near_copies = [
        remote(latent_part.at[2 * i + 1 - lax.rem(me, 2)], latent_landed.at[i], latent_send.at[i], latent_recv.at[i], near)
        for i in range(2)
    ]
    far_copy = remote(latent_mid, latent_landed.at[2], latent_send.at[2], latent_recv.at[2], far)
    small_copies = [
        remote(smalls.at[t], small_landed.at[t], small_send.at[t], small_recv.at[t], partners[t])
        for t in range(count + 1)
    ]

    def early_begin():
        need(4)
        for g in range(EARLY):
            for i in range(1 << (count - 2)):
                rows = slice(i * piece, (i + 1) * piece)
                total = v_kept[g, rows, :].astype(F32)
                for other in (v_first, v_second, v_both):
                    total = total + other[g, rows, :].astype(F32)
                early_acc[(g,) + tuple((i >> (count - 3 - k)) & 1 for k in range(count - 2))] = total.astype(BF16)
            advance(g)

    step = 256

    def weight_grad(index, left, right):
        @pl.loop(0, width // step)
        def _(j):
            first = pl.multiple_of(j * step, step)
            part = dot(left[:, pl.ds(first, step)], right[...], 0, 0).astype(BF16)
            rows = pl.ds(pl.multiple_of(index * size + first, step), step)
            late[0, rows, :] = part[:, :half_width]
            late[1, rows, :] = part[:, half_width:]

        advance(EARLY + index)

    def query_part():
        need(12)
        unsort_rows(v_grad_queries, v_sorted, position_column)
        weight_grad(0, v_ray_normed, v_grad_queries)

    def key_part():
        need(6)
        weight_grad(1, v_latent_normed, v_grad_keys)

    def value_part():
        need(7)
        weight_grad(2, v_latent_normed, v_grad_values)

    def latents_begin():
        need(10)
        for i in range(4):
            rows = slice(i * lat, (i + 1) * lat)
            part = dot(v_grad_keys[rows, :], v_key_w[...], 1, 1) + dot(v_grad_values[rows, :], v_value_w[...], 1, 1)
            standard, _ = stand(v_latent_all[rows, :].astype(F32))
            smalls[0, 8:9, :] += jnp.sum(part * standard, axis=0, keepdims=True)
            smalls[0, 9:10, :] += jnp.sum(part, axis=0, keepdims=True)
            latent_part[i] = part.astype(BF16)
        for copy in near_copies:
            copy.start()

    def latents_next():
        for copy in near_copies:
            copy.wait_recv()
            copy.wait_send()
        other = lax.bitwise_xor(me, 2)
        latent_mid[...] = (
            latent_part[other].astype(F32) + latent_landed[lax.div(other, 2)].astype(F32)
        ).astype(BF16)
        far_copy.start()

    def latents_end():
        far_copy.wait_recv()
        far_copy.wait_send()
        grad_normed = (
            latent_part[me].astype(F32) + latent_landed[lax.div(me, 2)].astype(F32) + latent_landed[2].astype(F32)
        )
        standard, inverse = stand(v_latent_all[pl.ds(pl.multiple_of(me * lat, 32), lat), :].astype(F32))
        latent_grad[...] = norm_back(grad_normed, standard, inverse, as_row(latent_gain)).astype(BF16)

    def rays_part():
        need(15)
        chunk = 256

        @pl.loop(0, rays.shape[0] // chunk)
        def _(i):
            rows = pl.ds(pl.multiple_of(i * chunk, chunk), chunk)
            grad_normed = dot(v_grad_queries[rows, :], v_query_w[...], 1, 1)
            standard, inverse = stand(v_rays[rows, :].astype(F32))
            smalls[0, 6:7, :] += jnp.sum(grad_normed * standard, axis=0, keepdims=True)
            smalls[0, 7:8, :] += jnp.sum(grad_normed, axis=0, keepdims=True)
            ray_grad[rows, :] = (
                v_grad_hidden[rows, :] + norm_back(grad_normed, standard, inverse, as_row(ray_gain))
            ).astype(BF16)

        small_copies[0].start()

    small_at = [0]

    def small_next():
        t = small_at[0]
        small_copies[t].wait_recv()
        smalls[t + 1] = smalls[t] + small_landed[t]
        small_copies[t].wait_send()
        small_at[0] += 1
        if t + 1 <= count:
            small_copies[t + 1].start()
        else:
            small[...] = smalls[count + 1]

    tasks = {
        "E": early_begin, "Q": query_part, "K": key_part, "V": value_part, "L": latents_begin, "M": latents_next,
        "N": latents_end, "R": rays_part, "S": small_next,
    }
    for letter in script:
        if letter in tasks:
            tasks[letter]()
        else:
            advance(int(letter))
    while small_at[0] <= count:
        small_next()
    while any(group.at <= len(steps) for group, steps in zip(groups, plans)):
        for g in range(len(groups)):
            if groups[g].at <= len(plans[g]):
                advance(g)
    for copy in stores:
        copy.wait()


def widen_kernel(size, summed, small, *refs):
    down, up, out, query, key, value = refs[:6]
    vectors, up_bias, (held, wide, load_sem, store_sem) = refs[6:14], refs[14], refs[15:]
    for at, vector in zip((5, 0, 6, 7, 8, 9, 3, 4), vectors):
        vector[...] = small[at]
    up_bias[: small.shape[1]] = small[1]
    up_bias[small.shape[1] :] = small[2]
    width = held.shape[3] * 2
    half = width // 2
    step = held.shape[2]
    jobs = []
    for g in range(8):
        for r in range(0, width, step):
            if g < 2:
                target = down.at[pl.ds(g * width + r, step), :]
            elif g < 4:
                target = up.at[pl.ds(r, step), pl.ds((g - 2) * width, width)]
            else:
                target = (out, query, key, value)[g - 4].at[pl.ds(r, step), :]
            jobs.append((summed.at[:, pl.ds(g * size + r, step), :], target))
    slots = held.shape[0]
    loads = [pltpu.make_async_copy(src, held.at[i % slots], load_sem.at[i % slots]) for i, (src, _) in enumerate(jobs)]
    saves = [pltpu.make_async_copy(wide.at[i % slots], dst, store_sem.at[i % slots]) for i, (_, dst) in enumerate(jobs)]
    for i in range(slots):
        loads[i].start()
    for i in range(len(jobs)):
        slot = i % slots
        loads[i].wait()
        if i >= slots:
            saves[i - slots].wait()
        wide[slot, :, :half] = held[slot, 0].astype(F32)
        wide[slot, :, half:] = held[slot, 1].astype(F32)
        saves[i].start()
        if i + slots < len(jobs):
            loads[i + slots].start()
    for i in range(len(jobs) - slots, len(jobs)):
        saves[i].wait()


def log2(n):
    return n.bit_length() - 1


EARLY = 5


HALVINGS = ("wz", "wz", "zw", "wz", "wz", "xyzw", "xzyw", "xyzw")
DOUBLINGS = ("wzxy", "wyzx", "wyzx", "wzxy", "xwyz", "wxyz", "wzyx", "wzxy")
SCRIPT = (
    "EKVL067123QM01423R6501427S3N6S1023S547S160S25347",
    "657016507613257435267546475675",
)


def ways(items, ray_parts):
    core, y, x = ("rays", 1), ("rays", 2), ("items", 1)
    bits = (x, y) + tuple(("items", 2 << i) for i in range(log2(items) - 1)) + tuple(
        ("rays", 4 << i) for i in range(log2(ray_parts) - 2)
    )
    if len(bits) != 4:
        return core, bits, (bits[2:],) * EARLY + (bits,) * 3, (bits[::-1],) * (EARLY + 3), "EKQVLRMN"
    name = dict(zip("xyzw", bits))
    halvings = tuple(tuple(name[c] for c in word) for word in HALVINGS)
    doublings = tuple(tuple(name[c] for c in word) for word in DOUBLINGS)
    return core, bits, halvings, doublings, "".join(SCRIPT)


def on_device(
    items, ray_parts,
    rays, latents, ray_scene, latent_scene, latent_pad, cotangent,
    query_weight, key_weight, value_weight, out_weight, out_bias, up_weight, up_bias, down_weight, down_bias,
    ray_gain, ray_shift, latent_gain, latent_shift, mlp_gain, mlp_shift,
):
    _, count, width = rays.shape
    lat = latents.shape[1]
    total = lat * ray_parts
    padded = total + WINDOW
    hidden_width = up_weight.shape[1]
    x = rays[0]
    upstream = cotangent[0]

    shape = jax.ShapeDtypeStruct
    rows_bf16 = shape((count, width), BF16)
    total_bf16 = shape((total, width), BF16)
    dma = pltpu.SemaphoreType.DMA

    square = shape((width, width), BF16)
    padded_bf16 = shape((padded, width), BF16)
    (
        ray_normed, sorted_queries, keys, values, latent_normed, latent_all, meta, position_row, position_column,
    ) = pl.pallas_call(
        project_kernel,
        out_shape=(
            rows_bf16, rows_bf16, padded_bf16, padded_bf16, total_bf16, total_bf16,
            shape((2 * SCENES + 2,), jnp.int32), shape((1, count), jnp.int32), shape((count, 1), jnp.int32),
        ),
        in_specs=[anywhere()] * 5 + [vmem()] * 7,
        out_specs=[anywhere()] * 6 + [smem(), vmem(), vmem()],
        scratch_shapes=[pltpu.VMEM((3, lat, width), BF16), pltpu.VMEM((count, width), BF16)]
        + [pltpu.VMEM((lat, width), BF16)] + [pltpu.VMEM((width, width), BF16)] * 3
        + [pltpu.VMEM((count, width), BF16)] * 3
        + [pltpu.VMEM((padded, width), BF16)] * 2 + [pltpu.VMEM((total, width), BF16)]
        + [dma((5,)), dma((5,)), dma((5,)), dma((20,))],
        compiler_params=big(collective_id=1, has_side_effects=True),
        name="project",
    )(
        x, latents[0], query_weight, key_weight, value_weight,
        ray_gain, ray_shift, latent_gain, latent_shift, ray_scene, latent_scene, latent_pad,
    )

    mixture, sorted_mixture, log_total = run_attend(meta, sorted_queries, keys, values, position_column)

    core, bits, halvings, doublings, script = ways(items, ray_parts)
    first, second = bits[:2]
    nbits = len(bits)
    unit = 16 << nbits
    size = (width + unit - 1) // unit * unit
    quarter = size // 4
    half_width = width // 2
    groups = len(halvings)
    late_groups = groups - EARLY
    piece = (size >> nbits, half_width)
    quarter_bf16 = (EARLY, quarter, half_width)

    ray_out, grad_mixture, grad_hidden, kept, to_first, to_second, to_both, early_sums = pl.pallas_call(
        functools.partial(mlp_kernel, core, first, second, size),
        out_shape=(
            rows_bf16, rows_bf16, shape((count, width), F32),
            shape(quarter_bf16, BF16), shape(quarter_bf16, BF16), shape(quarter_bf16, BF16), shape(quarter_bf16, BF16),
            shape((8, width), F32),
        ),
        in_specs=[anywhere()] * 6 + [vmem()] * 5,
        out_specs=[anywhere()] * 7 + [vmem()],
        scratch_shapes=[
            pltpu.VMEM((count, width), BF16), pltpu.VMEM((width, width), BF16), pltpu.VMEM((count, width), BF16),
            pltpu.VMEM((width, hidden_width), BF16), pltpu.VMEM((hidden_width, width), BF16),
            pltpu.VMEM((count, width), BF16),
            pltpu.VMEM((count, width), BF16), pltpu.VMEM((count, width), BF16), pltpu.VMEM((count, width), F32),
            pltpu.VMEM((4,) + quarter_bf16, BF16),
            pltpu.VMEM((count, hidden_width), BF16), pltpu.VMEM((count, hidden_width), BF16),
            pltpu.VMEM((count, width), BF16), pltpu.VMEM((count, width), BF16),
            pltpu.VMEM((2, EARLY * size, half_width), BF16), pltpu.VMEM((EARLY * size, half_width), BF16),
            dma((15,)), dma((15,)), dma((6,)), dma((12,)), dma((4 * EARLY,)),
        ],
        compiler_params=big(collective_id=2, has_side_effects=True),
        name="mlp",
    )(
        mixture, out_weight, x, up_weight, down_weight, upstream,
        out_bias, up_bias, down_bias, mlp_gain, mlp_shift,
    )

    def flip(index, partners):
        item, part = index // ray_parts, index % ray_parts
        for axis, bit in partners:
            item, part = (item ^ bit, part) if axis == "items" else (item, part ^ bit)
        return item * ray_parts + part

    def exchange(array, *partners):
        return lax.ppermute(
            array, ("items", "rays"), [(i, flip(i, partners)) for i in range(items * ray_parts)]
        )

    from_first = exchange(to_first, first)
    from_second = exchange(to_second, second)
    from_both = exchange(to_both, first, second)

    sorted_grad, grad_keys, grad_values = run_attend_back(
        meta, grad_mixture, position_row, sorted_queries, sorted_mixture, log_total, keys, values
    )

    held = [shape(quarter_bf16, BF16)] * 4 + [total_bf16] * 3 + [rows_bf16] * 0
    held = held + [square, square, total_bf16, rows_bf16, rows_bf16, square, rows_bf16, shape((count, width), F32)]
    held = held + [rows_bf16]
    ray_grad, latent_grad, summed, small = pl.pallas_call(
        functools.partial(reduce_kernel, core, bits, halvings, doublings, size, script),
        out_shape=(
            rows_bf16, shape((lat, width), BF16), shape((2, groups) + (2,) * nbits + piece, BF16),
            shape((16, width), F32),
        ),
        in_specs=[anywhere()] * 15 + [vmem()] * 4,
        out_specs=[vmem(), vmem(), anywhere(), vmem()],
        scratch_shapes=[pltpu.VMEM(h.shape, h.dtype) for h in held] + [
            pltpu.VMEM((2, late_groups * size, half_width), BF16),
            pltpu.VMEM((late_groups * size, half_width), BF16),
            pltpu.VMEM((EARLY,) + (2,) * (nbits - 2) + piece, BF16),
            pltpu.VMEM((EARLY,) + (2,) * (nbits - 2) + piece, BF16),
            pltpu.VMEM((late_groups,) + (2,) * nbits + piece, BF16),
            pltpu.VMEM((late_groups,) + (2,) * nbits + piece, BF16),
            pltpu.VMEM((2, groups) + (2,) * nbits + piece, BF16),
            pltpu.VMEM((nbits + 2, 16, width), F32),
            pltpu.VMEM((nbits + 1, 16, width), F32),
            pltpu.VMEM((4, lat, width), BF16),
            pltpu.VMEM((3, lat, width), BF16),
            pltpu.VMEM((lat, width), BF16),
            dma((15,)), dma((late_groups,)), dma((late_groups,)),
            dma((groups * nbits,)), dma((groups * nbits,)), dma((groups * (nbits + 1),)), dma((groups * (nbits + 1),)),
            dma((nbits + 1,)), dma((nbits + 1,)), dma((3,)), dma((3,)), dma((2 * groups,)),
        ],
        compiler_params=big(collective_id=3, has_side_effects=True),
        name="reduce",
    )(
        kept, from_first, from_second, from_both,
        latent_normed, grad_keys, grad_values, key_weight, value_weight, latent_all,
        sorted_grad, ray_normed, query_weight, x, grad_hidden,
        ray_gain, latent_gain, early_sums, position_column,
    )

    wide = shape((width, width), F32)
    step, slots = 256, 4
    (
        down_grad, up_grad, out_grad, query_grad, key_grad, value_grad,
        out_bias_grad, down_bias_grad, ray_gain_grad, ray_shift_grad, latent_gain_grad, latent_shift_grad,
        mlp_gain_grad, mlp_shift_grad, up_bias_grad,
    ) = pl.pallas_call(
        functools.partial(widen_kernel, size),
        out_shape=(shape((2 * width, width), F32), shape((width, 2 * width), F32), wide, wide, wide, wide)
        + (shape((width,), F32),) * 8 + (shape((hidden_width,), F32),),
        in_specs=[anywhere(), vmem()],
        out_specs=[anywhere()] * 6 + [vmem()] * 9,
        scratch_shapes=[
            pltpu.VMEM((slots, 2, step, half_width), BF16), pltpu.VMEM((slots, step, width), F32),
            dma((slots,)), dma((slots,)),
        ],
        name="widen",
    )(summed.reshape(2, groups * size, half_width), small)

    return (
        ray_out[None], ray_grad[None], latent_grad[None],
        query_grad, key_grad, value_grad, out_grad, out_bias_grad,
        up_grad, up_bias_grad, down_grad, down_bias_grad,
        ray_gain_grad, ray_shift_grad, latent_gain_grad, latent_shift_grad, mlp_gain_grad, mlp_shift_grad,
    )


def solution(mesh):
    split = P("items", "rays", None)
    in_specs = (split, split, P("items", "rays"), P("items", None), P("items", None), split) + (P(),) * 15
    out_specs = (split, split, split) + (P(),) * 15
    return jax.shard_map(
        functools.partial(on_device, mesh.shape["items"], mesh.shape["rays"]),
        mesh=mesh, in_specs=in_specs, out_specs=out_specs, check_vma=False,
    )
```

```python
import functools

import jax
import jax.numpy as jnp
from jax import lax
from jax.experimental import pallas as pl
from jax.experimental.pallas import tpu as pltpu
from jax.sharding import PartitionSpec as P

HEADS = 12
HEAD_DIM = 64
PAIRS = HEADS // 2
SCENES = 4
EPSILON = 1e-05
SCALE = HEAD_DIM ** (-0.5)
BLOCK = 128
WINDOW = 256
OUTSIDE = -1e30
MANY = 5
MESH = pl.DeviceIdType.MESH
F32 = jnp.float32
BF16 = jnp.bfloat16
MIB = 2**20


def dot(left, right, left_dim=1, right_dim=0):
    return lax.dot_general(
        left, right, (((left_dim,), (right_dim,)), ((), ())), preferred_element_type=F32
    )


def stand(rows):
    center = rows - jnp.mean(rows, axis=-1, keepdims=True)
    inverse = lax.rsqrt(jnp.mean(center * center, axis=-1, keepdims=True) + EPSILON)
    return center * inverse, inverse


def norm_back(grad_out, standard, inverse, gain):
    scaled = grad_out * gain
    return inverse * (
        scaled
        - jnp.mean(scaled, axis=-1, keepdims=True)
        - standard * jnp.mean(scaled * standard, axis=-1, keepdims=True)
    )


def as_row(vector):
    return vector[...].reshape(1, -1)


def vmem():
    return pl.BlockSpec(memory_space=pltpu.VMEM)


def smem():
    return pl.BlockSpec(memory_space=pltpu.SMEM)


def anywhere():
    return pl.BlockSpec(memory_space=pl.ANY)


def peer(axis, bit):
    return {axis: lax.bitwise_xor(lax.axis_index(axis), bit)}


def greet(partners):
    barrier = pltpu.get_barrier_semaphore()
    for axis, bit in partners:
        pl.semaphore_signal(barrier, inc=1, device_id=peer(axis, bit), device_id_type=MESH)
    pl.semaphore_wait(barrier, len(partners))


def bit_of(partner):
    axis, bit = partner
    return lax.rem(lax.div(lax.axis_index(axis), bit), 2)


def remote(src, dst, send, recv, partner):
    return pltpu.make_async_remote_copy(
        src_ref=src, dst_ref=dst, send_sem=send, recv_sem=recv, device_id=peer(*partner), device_id_type=MESH
    )


def project_kernel(
    rays, latents, query_w, key_w, value_w, ray_gain, ray_shift, latent_gain, latent_shift,
    ray_scene, latent_scene, latent_pad,
    ray_normed, sorted_queries, keys, values, latent_normed, latent_all, meta, position_row, position_column,
    landed, v_rays, v_latents, v_query_w, v_key_w, v_value_w,
    normed, queries, in_order, key_rows, value_rows, latent_rows,
    send_sem, recv_sem, load_sem, store_sem,
):
    me = lax.axis_index("rays")
    lat = latents.shape[0]
    total = 4 * lat
    near, far = ("rays", 1), ("rays", 2)
    pairs = ((latents, v_latents), (rays, v_rays), (query_w, v_query_w), (key_w, v_key_w), (value_w, v_value_w))
    loads = [pltpu.make_async_copy(src, dst, load_sem.at[i]) for i, (src, dst) in enumerate(pairs)]
    for load in loads:
        load.start()
    greet([near, far])

    def copy(src, slot, part, partner, index):
        return remote(src.at[part], landed.at[slot, part], send_sem.at[index], recv_sem.at[index], partner)

    whole, halves = slice(0, lat), (slice(0, lat // 2), slice(lat // 2, lat))
    to_far = [copy(latents, 1, part, far, i) for i, part in enumerate(halves)]
    to_near = copy(latents, 0, whole, near, 2)
    passed = [copy(landed.at[1], 2, part, near, 3 + i) for i, part in enumerate(halves)]
    for send in to_far:
        send.start()
    to_near.start()

    stores = []

    def keep(src, dst):
        saved = pltpu.make_async_copy(src, dst, store_sem.at[len(stores)])
        saved.start()
        stores.append(saved)

    sort_plan(ray_scene, latent_scene, latent_pad, meta, position_row, position_column)
    loads[1].wait()
    loads[2].wait()
    chunk = 256

    @pl.loop(0, rays.shape[0] // chunk)
    def _(i):
        rows = pl.ds(pl.multiple_of(i * chunk, chunk), chunk)
        standard, _ = stand(v_rays[rows, :].astype(F32))
        low = (standard * as_row(ray_gain) + as_row(ray_shift)).astype(BF16)
        normed[rows, :] = low
        projected = dot(low, v_query_w[...]).astype(BF16)
        queries[rows, :] = (projected.astype(F32) * SCALE).astype(BF16)

    keep(normed, ray_normed)
    sort_rows(in_order, queries, position_row)
    keep(in_order, sorted_queries)

    def one(raw, owner):
        rows = pl.ds(pl.multiple_of(owner * lat, 32), lat)
        standard, _ = stand(raw[...].astype(F32))
        low = (standard * as_row(latent_gain) + as_row(latent_shift)).astype(BF16)
        latent_rows[rows, :] = low
        keep(raw, latent_all.at[rows])
        keep(latent_rows.at[rows], latent_normed.at[rows])
        key_rows[rows, :] = dot(low, v_key_w[...]).astype(BF16)
        keep(key_rows.at[rows], keys.at[rows])
        value_rows[rows, :] = dot(low, v_value_w[...]).astype(BF16)
        keep(value_rows.at[rows], values.at[rows])

    key_rows[total:, :] = jnp.zeros((keys.shape[0] - total, keys.shape[1]), BF16)
    keep(key_rows.at[total:], keys.at[total:])
    keep(key_rows.at[total:], values.at[total:])
    for i in (0, 3, 4):
        loads[i].wait()
    one(v_latents, me)
    to_near.wait_recv()
    one(landed.at[0], lax.bitwise_xor(me, 1))
    for got, on in zip(to_far, passed):
        got.wait_recv()
        on.start()
    one(landed.at[1], lax.bitwise_xor(me, 2))
    for got in passed:
        got.wait_recv()
    one(landed.at[2], lax.bitwise_xor(me, 3))
    for send in to_far + [to_near] + passed:
        send.wait_send()
    for saved in stores:
        saved.wait()


def lanes_of(shape):
    return lax.broadcasted_iota(jnp.int32, shape, len(shape) - 1)


def rows_of(shape):
    return lax.broadcasted_iota(jnp.int32, shape, 0)


def sort_plan(ray_scene, latent_scene, latent_pad, meta, position_row, position_column):
    count = ray_scene.shape[1]
    for s in range(1, SCENES):
        meta[s] = jnp.sum(jnp.where(ray_scene[...] < s, 1, 0))
    meta[0] = 0
    meta[SCENES] = count
    meta[SCENES + 1] = 0
    for s in range(1, SCENES + 1):
        meta[SCENES + 1 + s] = jnp.sum(jnp.where((latent_scene[...] < s) & (latent_pad[...] == 0), 1, 0))
    order_row = (ray_scene[...] * count + lanes_of((1, count))).astype(F32)
    order_column = jnp.broadcast_to(order_row, (8, count)).T[:, :1]
    step = 256
    smaller = jnp.zeros((1, count), F32)
    for i in range(count // step):
        before = jnp.where(order_column[i * step : (i + 1) * step] < order_row, 1.0, 0.0)
        smaller = smaller + jnp.sum(before, axis=0, keepdims=True)
    position_row[...] = smaller.astype(jnp.int32)
    position_column[...] = jnp.broadcast_to(smaller, (8, count)).T[:, :1].astype(jnp.int32)


def block_range(meta, block):
    first, last = block * BLOCK, block * BLOCK + BLOCK - 1
    low = sum(jnp.where(meta[s] <= first, 1, 0) for s in range(1, SCENES))
    high = sum(jnp.where(meta[s] <= last, 1, 0) for s in range(1, SCENES))
    start = meta[SCENES + 1 + low] // 16 * 16
    return start, (meta[SCENES + 2 + high] - start + WINDOW - 1) // WINDOW


def sort_rows(target, source, position_row):
    count = source.shape[0]
    step = 512

    @pl.loop(0, count // step)
    def _(i):
        first = pl.multiple_of(i * step, step)
        index = rows_of((step, count)) + first
        chosen = jnp.where(index == position_row[...], 1.0, 0.0).astype(BF16)
        target[pl.ds(first, step), :] = dot(chosen, source[...]).astype(BF16)


def unsort_rows(target, source, position_column):
    count = source.shape[0]
    step = 512

    @pl.loop(0, count // step)
    def _(i):
        first = pl.multiple_of(i * step, step)
        index = lanes_of((step, count))
        chosen = jnp.where(index == position_column[pl.ds(first, step), :], 1.0, 0.0).astype(BF16)
        target[pl.ds(first, step), :] = dot(chosen, source[...]).astype(BF16)


def latent_features(meta, extra):
    shape = extra.shape
    row = rows_of(shape)
    lane = lanes_of((1, shape[1]))
    first = jnp.full((1, shape[1]), meta[SCENES + 1], jnp.int32)
    last = jnp.full((1, shape[1]), meta[SCENES + 2], jnp.int32)
    for s in range(1, SCENES):
        first = jnp.where(lane == s, meta[SCENES + 1 + s], first)
        last = jnp.where(lane == s, meta[SCENES + 2 + s], last)
    first = jnp.where(lane >= SCENES, 0, first)
    last = jnp.where(lane >= SCENES, shape[0], last)
    value = jnp.where((row >= first) & (row < last), 0.0, OUTSIDE)
    extra[...] = value.astype(BF16)


def ray_features(meta, block):
    shape = (BLOCK, 128)
    row = rows_of(shape) + block * BLOCK
    lane = lanes_of((1, 128))
    first = jnp.full((1, 128), count_none, jnp.int32)
    last = jnp.zeros((1, 128), jnp.int32)
    for s in range(SCENES):
        first = jnp.where(lane == s, meta[s], first)
        last = jnp.where(lane == s, meta[s + 1], last)
    return jnp.where((row >= first) & (row < last), 1.0, 0.0)


count_none = 2**30


def half_masks():
    lane = lanes_of((BLOCK, 128))
    low = jnp.where(lane < HEAD_DIM, 1.0, 0.0)
    return low, 1.0 - low


def pick_halves(both):
    lane = lanes_of((BLOCK, 128))
    return jnp.where(lane < HEAD_DIM, both[:BLOCK, :128], both[BLOCK:, :128])


def pair_columns(p):
    return slice(128 * p, 128 * (p + 1))


def over_windows(windows, body):
    @pl.loop(0, windows // 2)
    def _(i):
        body(2 * i, 2)

    @pl.when(windows % 2 == 1)
    def _():
        body(windows - 1, 1)


def attend_kernel(
    meta, sorted_queries, keys, values, position_column,
    mixture, sorted_mixture, log_total,
    latent_extra, stacked, total, peak, held,
):
    rays = sorted_queries.shape[0]
    latent_features(meta, latent_extra)
    ones = jnp.where(lanes_of((WINDOW, 128)) == 0, 1.0, 0.0).astype(BF16)
    low, high = half_masks()
    lane = lanes_of((BLOCK, 128))

    @pl.loop(0, rays // BLOCK)
    def _(block):
        rows = pl.ds(pl.multiple_of(block * BLOCK, BLOCK), BLOCK)
        start, windows = block_range(meta, block)
        extra = ray_features(meta, block).astype(BF16)
        for p in range(PAIRS):
            pair = sorted_queries[rows, pair_columns(p)].astype(F32)
            stacked[p, :BLOCK, :128] = (pair * low).astype(BF16)
            stacked[p, BLOCK:, :128] = (pair * high).astype(BF16)
            stacked[p, :BLOCK, 128:] = extra
            stacked[p, BLOCK:, 128:] = extra

        def window_at(w):
            return pl.ds(pl.multiple_of(start + w * WINDOW, 16), WINDOW)

        def score(w, p):
            window = window_at(w)
            key_side = jnp.concatenate([keys[window, pair_columns(p)], latent_extra[window, :]], axis=1)
            scores = dot(stacked[p], key_side, 1, 1)
            held[w, p] = scores
            return jnp.maximum(scores[:, :128], scores[:, 128:])

        def mix(w, p):
            top = peak[p]
            lifted = jnp.exp(held[w, p] - jnp.concatenate([top, top], axis=1)).astype(BF16)
            return dot(lifted, jnp.concatenate([values[window_at(w), pair_columns(p)], ones], axis=1))

        def highest(top):
            return jnp.broadcast_to(jnp.max(top, axis=1, keepdims=True), (2 * BLOCK, 128))

        def finish(p, both, logs):
            sums = both[:, 128:129]
            mixed = pick_halves(both[:, :128] * (1.0 / sums))
            sorted_mixture[rows, pair_columns(p)] = mixed.astype(BF16)
            log_rows = peak[p] + jnp.log(sums)
            logs = jnp.where(lane == 2 * p, log_rows[:BLOCK], logs)
            return jnp.where(lane == 2 * p + 1, log_rows[BLOCK:], logs)

        def few(number):
            for p in range(PAIRS):
                peak[p] = highest(functools.reduce(jnp.maximum, [score(w, p) for w in range(number)]))
            logs = jnp.zeros((BLOCK, 128), F32)
            for p in range(PAIRS):
                logs = finish(p, functools.reduce(jnp.add, [mix(w, p) for w in range(number)]), logs)
            log_total[rows, :] = logs

        for number in range(1, MANY):
            pl.when(windows == number)(functools.partial(few, number))

        @pl.when(windows >= MANY)
        def _():
            for p in range(PAIRS):
                peak[p] = jnp.full((2 * BLOCK, 128), -3e38, F32)
                total[p] = jnp.zeros((2 * BLOCK, 256), F32)

            @pl.loop(0, windows)
            def _(w):
                for p in range(PAIRS):
                    peak[p] = jnp.maximum(peak[p], score(w, p))

            for p in range(PAIRS):
                peak[p] = highest(peak[p])

            @pl.loop(0, windows)
            def _(w):
                for p in range(PAIRS):
                    total[p] += mix(w, p)

            logs = jnp.zeros((BLOCK, 128), F32)
            for p in range(PAIRS):
                logs = finish(p, total[p], logs)
            log_total[rows, :] = logs

    unsort_rows(mixture, sorted_mixture, position_column)


def attend_back_kernel(
    meta, grad_mixture, position_row, sorted_queries, sorted_mixture, log_total, keys, values,
    grad_queries, grad_keys, grad_values,
    v_queries, v_mixture, v_logs, v_keys, v_values,
    stacked, stacked_grad, sorted_grad, key_total, value_total, query_total, log_rows, inner_rows, bias, probs_low, scores_low, load_sem,
):
    rays = sorted_queries.shape[0]
    given = (sorted_queries, sorted_mixture, log_total, keys, values)
    held = (v_queries, v_mixture, v_logs, v_keys, v_values)
    loads = [pltpu.make_async_copy(src, dst, load_sem.at[i]) for i, (src, dst) in enumerate(zip(given, held))]
    for load in loads:
        load.start()
    key_total[...] = jnp.zeros(key_total.shape, F32)
    value_total[...] = jnp.zeros(value_total.shape, F32)
    sort_rows(sorted_grad, grad_mixture, position_row)
    low, high = half_masks()
    lane = lanes_of((BLOCK, 128))
    for load in loads:
        load.wait()

    @pl.loop(0, rays // BLOCK)
    def _(block):
        rows = pl.ds(pl.multiple_of(block * BLOCK, BLOCK), BLOCK)
        start, windows = block_range(meta, block)
        inner = jnp.zeros((BLOCK, 128), F32)
        for p in range(PAIRS):
            columns = pair_columns(p)
            pair = v_queries[rows, columns].astype(F32)
            grad = sorted_grad[rows, columns].astype(F32)
            product = grad * v_mixture[rows, columns].astype(F32)
            for side, mask in enumerate((low, high)):
                half = slice(side * BLOCK, (side + 1) * BLOCK)
                stacked[p, half, :] = (pair * mask).astype(BF16)
                stacked_grad[p, half, :] = (grad * mask).astype(BF16)
                inner = jnp.where(lane == 2 * p + side, jnp.sum(product * mask, axis=1, keepdims=True), inner)
            query_total[p] = jnp.zeros((2 * BLOCK, 128), F32)
        log_rows[...] = v_logs[rows, :].T
        inner_rows[...] = inner.T

        ray = lanes_of((1, BLOCK)) + block * BLOCK
        first = jnp.full((1, BLOCK), meta[SCENES + 1], jnp.int32)
        last = jnp.full((1, BLOCK), meta[SCENES + 2], jnp.int32)
        for s in range(1, SCENES):
            first = jnp.where(ray >= meta[s], meta[SCENES + 1 + s], first)
            last = jnp.where(ray >= meta[s], meta[SCENES + 2 + s], last)

        def two_rows(ref, p):
            return jnp.concatenate([ref[2 * p : 2 * p + 1, :], ref[2 * p + 1 : 2 * p + 2, :]], axis=1)

        def back(w, number):
            spots = [pl.multiple_of(start + (w + u) * WINDOW, 16) for u in range(number)]
            for u, spot in enumerate(spots):
                row = rows_of((WINDOW, BLOCK)) + spot
                bias[u] = jnp.where((row >= first) & (row < last), 0.0, OUTSIDE)
            for p in range(PAIRS):
                columns = pair_columns(p)
                for u, spot in enumerate(spots):
                    window = pl.ds(spot, WINDOW)
                    key_pair = v_keys[window, columns]
                    scores = dot(key_pair, stacked[p], 1, 1) - two_rows(log_rows, p)
                    probs = jnp.exp(scores + jnp.concatenate([bias[u], bias[u]], axis=1))
                    centered = dot(v_values[window, columns], stacked_grad[p], 1, 1) - two_rows(inner_rows, p)
                    probs_low[u, p] = probs.astype(BF16)
                    scores_low[u, p] = (probs * centered).astype(BF16)
            for p in range(PAIRS):
                columns = pair_columns(p)
                part = None
                for u, spot in enumerate(spots):
                    window = pl.ds(spot, WINDOW)
                    value_total[window, columns] += dot(probs_low[u, p], stacked_grad[p])
                    key_total[window, columns] += dot(scores_low[u, p], stacked[p])
                    query = dot(scores_low[u, p], v_keys[window, columns], 0, 0)
                    part = query if part is None else part + query
                query_total[p] += part

        over_windows(windows, back)

        for p in range(PAIRS):
            grad_queries[rows, pair_columns(p)] = (pick_halves(query_total[p]) * SCALE).astype(BF16)

    count = grad_keys.shape[0]
    grad_keys[...] = key_total[:count, :].astype(BF16)
    grad_values[...] = value_total[:count, :].astype(BF16)


def big(**rest):
    return pltpu.CompilerParams(vmem_limit_bytes=60 * MIB, **rest)


def run_attend(meta, sorted_queries, keys, values, position_column):
    count, width = sorted_queries.shape
    padded = keys.shape[0]
    shape = jax.ShapeDtypeStruct
    rows_bf16 = shape((count, width), BF16)
    most = (padded - 1) // WINDOW + 1
    return pl.pallas_call(
        attend_kernel,
        out_shape=(rows_bf16, rows_bf16, shape((count, 128), F32)),
        in_specs=[smem()] + [vmem()] * 4,
        out_specs=[vmem()] * 3,
        scratch_shapes=[
            pltpu.VMEM((padded, 128), BF16),
            pltpu.VMEM((PAIRS, 2 * BLOCK, 256), BF16),
            pltpu.VMEM((PAIRS, 2 * BLOCK, 256), F32),
            pltpu.VMEM((PAIRS, 2 * BLOCK, 128), F32),
            pltpu.VMEM((most, PAIRS, 2 * BLOCK, WINDOW), F32),
        ],
        compiler_params=big(),
        name="attend",
    )(meta, sorted_queries, keys, values, position_column)


def run_attend_back(meta, grad_mixture, position_row, sorted_queries, sorted_mixture, log_total, keys, values):
    count, width = grad_mixture.shape
    padded = keys.shape[0]
    total = padded - WINDOW
    shape = jax.ShapeDtypeStruct
    return pl.pallas_call(
        attend_back_kernel,
        out_shape=(shape((count, width), BF16), shape((total, width), BF16), shape((total, width), BF16)),
        in_specs=[smem()] + [vmem()] * 2 + [anywhere()] * 5,
        out_specs=[vmem()] * 3,
        scratch_shapes=[
            pltpu.VMEM((count, width), BF16),
            pltpu.VMEM((count, width), BF16),
            pltpu.VMEM((count, 128), F32),
            pltpu.VMEM((padded, width), BF16),
            pltpu.VMEM((padded, width), BF16),
            pltpu.VMEM((PAIRS, 2 * BLOCK, 128), BF16),
            pltpu.VMEM((PAIRS, 2 * BLOCK, 128), BF16),
            pltpu.VMEM((count, width), BF16),
            pltpu.VMEM((padded, width), F32),
            pltpu.VMEM((padded, width), F32),
            pltpu.VMEM((PAIRS, 2 * BLOCK, 128), F32),
            pltpu.VMEM((128, BLOCK), F32),
            pltpu.VMEM((128, BLOCK), F32),
            pltpu.VMEM((2, WINDOW, BLOCK), F32),
            pltpu.VMEM((2, PAIRS, WINDOW, 2 * BLOCK), BF16),
            pltpu.VMEM((2, PAIRS, WINDOW, 2 * BLOCK), BF16),
            pltpu.SemaphoreType.DMA((5,)),
        ],
        compiler_params=big(),
        name="attend_back",
    )(meta, grad_mixture, position_row, sorted_queries, sorted_mixture, log_total, keys, values)


def quarter_start(first, second, size, flips):
    one = bit_of(first) if not flips[0] else 1 - bit_of(first)
    two = bit_of(second) if not flips[1] else 1 - bit_of(second)
    return one * (size // 2) + two * (size // 4)


def mlp_kernel(
    core, first, second, size,
    given_mixture, given_out_w, given_rays, given_up_w, given_down_w, given_cotangent, out_bias, up_bias, down_bias, mlp_gain, mlp_shift,
    kept_ray_out, kept_grad_mixture, kept_grad_hidden, kept, to_first, to_second, to_both, sums,
    mixture, out_w, rays, up_w, down_w, cotangent, ray_out, grad_mixture, grad_hidden, quarters,
    act, grad_pre, normed, branch, early, landed, send_sem, recv_sem, load_sem, store_sem, quarter_sem,
):
    chunk = 512
    width = rays.shape[1]
    half_width = width // 2
    pairs = (
        (given_mixture, mixture), (given_out_w, out_w), (given_rays, rays), (given_up_w, up_w),
        (given_down_w, down_w), (given_cotangent, cotangent),
    )
    loads = [pltpu.make_async_copy(src, dst, load_sem.at[i]) for i, (src, dst) in enumerate(pairs)]
    for load in loads:
        load.start()
    greet([core])
    mine = bit_of(core)

    def keep(i):
        rows = pl.ds(pl.multiple_of(i * chunk, chunk), chunk)
        results = ((ray_out, kept_ray_out), (grad_hidden, kept_grad_hidden), (grad_mixture, kept_grad_mixture))
        return [
            pltpu.make_async_copy(src.at[rows], dst.at[rows], store_sem.at[3 * i + k])
            for k, (src, dst) in enumerate(results)
        ]

    sums[...] = jnp.zeros(sums.shape, F32)
    root = 0.7978845608028654
    cubic = 0.044715

    @pl.loop(0, rays.shape[0] // chunk)
    def _(i):
        rows = pl.ds(pl.multiple_of(i * chunk, chunk), chunk)

        def need(*which):
            @pl.when(i == 0)
            def _():
                for k in which:
                    loads[k].wait()

        need(0, 1, 2)
        hidden = rays[rows, :].astype(F32) + dot(mixture[rows, :], out_w[...]) + as_row(out_bias)
        standard, inverse = stand(hidden)
        low = (standard * as_row(mlp_gain) + as_row(mlp_shift)).astype(BF16)
        normed[rows, :] = low
        need(3, 4, 5)
        upstream = cotangent[rows, :]
        half = 768
        out = hidden + as_row(down_bias)
        grad_mlp = jnp.zeros((chunk, width), F32)
        for j in range(up_w.shape[1] // half):
            cols = slice(j * half, (j + 1) * half)
            pre = dot(low, up_w[:, cols]) + up_bias[cols].reshape(1, half)
            square = pre * pre
            bend = jnp.tanh(root * pre * (1.0 + cubic * square))
            rise = 0.5 * (1.0 + bend)
            active = (pre * rise).astype(BF16)
            slope = rise + 0.5 * pre * (1.0 - bend * bend) * (root * (1.0 + 3.0 * cubic * square))
            act[rows, cols] = active
            out = out + dot(active, down_w[cols, :])
            back = (dot(upstream, down_w[cols, :], 1, 1) * slope).astype(BF16)
            grad_pre[rows, cols] = back
            sums[1 + j : 2 + j, :] += jnp.sum(back.astype(F32), axis=0, keepdims=True)
            grad_mlp = grad_mlp + dot(back, up_w[:, cols], 1, 1)
        ray_out[rows, :] = out.astype(BF16)
        wide = upstream.astype(F32)
        sums[0:1, :] += jnp.sum(wide, axis=0, keepdims=True)
        sums[3:4, :] += jnp.sum(grad_mlp * standard, axis=0, keepdims=True)
        sums[4:5, :] += jnp.sum(grad_mlp, axis=0, keepdims=True)
        through = wide + norm_back(grad_mlp, standard, inverse, as_row(mlp_gain))
        grad_hidden[rows, :] = through
        rounded = through.astype(BF16)
        branch[rows, :] = rounded
        sums[5:6, :] += jnp.sum(rounded.astype(F32), axis=0, keepdims=True)
        grad_mixture[rows, :] = dot(rounded, out_w[...], 1, 1).astype(BF16)
        for saved in keep(i):
            saved.start()

    step = 384
    tiles = width // step

    def swap(tile):
        rows = pl.ds(pl.multiple_of(lax.div(tile, tiles) * size + lax.rem(tile, tiles) * step, step), step)
        return remote(early.at[1 - mine, rows], landed.at[rows], send_sem.at[tile], recv_sem.at[tile], core)

    def store(tile, left, right):
        rows = pl.ds(pl.multiple_of(lax.div(tile, tiles) * size + lax.rem(tile, tiles) * step, step), step)
        part = dot(left, right, 0, 0).astype(BF16)
        early[0, rows, :] = part[:, :half_width]
        early[1, rows, :] = part[:, half_width:]
        swap(tile).start()

    @pl.loop(0, 2 * tiles)
    def _(j):
        store(j, act[:, pl.ds(pl.multiple_of(j * step, step), step)], cotangent[...])

    for h in range(2):

        @pl.loop(0, tiles)
        def _(j):
            cols = pl.ds(pl.multiple_of(j * step, step), step)
            store(j + (2 + h) * tiles, normed[:, cols], grad_pre[:, h * width : (h + 1) * width])

    @pl.loop(0, tiles)
    def _(j):
        store(j + 4 * tiles, mixture[:, pl.ds(pl.multiple_of(j * step, step), step)], branch[...])

    quarter = size // 4
    targets = ((kept, (0, 0)), (to_first, (1, 0)), (to_second, (0, 1)), (to_both, (1, 1)))

    def send_off(g, k):
        return pltpu.make_async_copy(quarters.at[k, g], targets[k][0].at[g], quarter_sem.at[4 * g + k])

    for g in range(EARLY):
        for tile in range(g * tiles, (g + 1) * tiles):
            swap(tile).wait_recv()
        for k, (_, flips) in enumerate(targets):
            rows = pl.ds(pl.multiple_of(g * size + quarter_start(first, second, size, flips), 16), quarter)
            quarters[k, g] = (early[mine, rows, :].astype(F32) + landed[rows, :].astype(F32)).astype(BF16)
            send_off(g, k).start()
    for tile in range(5 * tiles):
        swap(tile).wait_send()
    for i in range(rays.shape[0] // chunk):
        for saved in keep(i):
            saved.wait()
    for g in range(EARLY):
        for k in range(4):
            send_off(g, k).wait()


def reduce_kernel(
    core, bits, halvings, doublings, size, script,
    kept, from_first, from_second, from_both,
    latent_normed, grad_keys, grad_values, key_w, value_w, latent_all,
    sorted_grad, ray_normed, query_w, rays, grad_hidden,
    ray_gain, latent_gain, early_sums, position_column,
    ray_grad, latent_grad, summed, small,
    v_kept, v_first, v_second, v_both,
    v_latent_normed, v_grad_keys, v_grad_values, v_key_w, v_value_w, v_latent_all,
    v_sorted, v_ray_normed, v_query_w, v_rays, v_grad_hidden, v_grad_queries,
    late, late_landed, early_acc, early_landed, late_acc, late_in, gathered,
    smalls, small_landed, latent_part, latent_landed, latent_mid,
    load_sem, swap_send, swap_recv, send_sem, recv_sem, back_send, back_recv,
    small_send, small_recv, latent_send, latent_recv, store_sem,
):
    count = len(bits)
    partners = sorted(bits + (core,))
    width = rays.shape[1]
    half_width = width // 2
    piece = size >> count
    held = (
        v_kept, v_first, v_second, v_both,
        v_latent_normed, v_grad_keys, v_grad_values, v_key_w, v_value_w, v_latent_all,
        v_sorted, v_ray_normed, v_query_w, v_rays, v_grad_hidden,
    )
    given = (
        kept, from_first, from_second, from_both,
        latent_normed, grad_keys, grad_values, key_w, value_w, latent_all,
        sorted_grad, ray_normed, query_w, rays, grad_hidden,
    )
    loads = [pltpu.make_async_copy(src, dst, load_sem.at[i]) for i, (src, dst) in enumerate(zip(given, held))]
    for load in loads:
        load.start()
    greet(partners)
    mine = bit_of(core)
    loaded = [0]

    def need(last):
        while loaded[0] < last:
            loads[loaded[0]].wait()
            loaded[0] += 1

    smalls[0] = jnp.zeros(smalls.shape[1:], F32)
    smalls[0, 0:8, :] = early_sums[...]


    class Group:
        pass

    groups = []
    for g in range(EARLY + late_landed.shape[0] // size):
        group = Group()
        group.index, group.at, group.live = g, 0, None
        group.early = g < EARLY
        group.free = list(bits[2:] if group.early else bits)
        group.halvings, group.doublings = list(halvings[g]), list(doublings[g])
        group.done = []
        group.acc = early_acc.at[g] if group.early else late_acc.at[g - EARLY]
        group.landed = early_landed.at[g] if group.early else late_in.at[g - EARLY]
        groups.append(group)

    def combos(names):
        for i in range(1 << len(names)):
            yield {name: (i >> k) & 1 for k, name in enumerate(names)}

    def dims(group):
        return bits[2:] if group.early else bits

    def swap_begin(group):
        i = group.index - EARLY
        rows = pl.ds(i * size, size)
        group.live = remote(late.at[1 - mine, rows], late_landed.at[rows], swap_send.at[i], swap_recv.at[i], core)
        group.live.start()

    def swap_finish(group):
        group.live.wait_recv()
        base = (group.index - EARLY) * size
        for i in range(1 << count):
            rows = slice(base + i * piece, base + (i + 1) * piece)
            total = late[mine, rows, :].astype(F32) + late_landed[rows, :].astype(F32)
            group.acc[tuple((i >> (count - 1 - k)) & 1 for k in range(count))] = total.astype(BF16)
        group.live.wait_send()

    def halve_begin(group):
        bit = group.halvings[len(group.done)]
        i = group.index * count + len(group.done)

        def at(value):
            return tuple(
                pl.ds(value, 1) if d == bit else pl.ds(bit_of(d), 1) if d in group.done else slice(None)
                for d in dims(group)
            )

        own = bit_of(bit)
        group.live = remote(group.acc.at[at(1 - own)], group.landed.at[at(own)], send_sem.at[i], recv_sem.at[i], bit)
        group.live.start()

    def halve_finish(group):
        bit = group.halvings[len(group.done)]
        group.live.wait_recv()
        own = bit_of(bit)
        group.done.append(bit)
        last = len(group.done) == len(dims(group))
        for combo in combos([d for d in dims(group) if d not in group.done]):
            keep = tuple(combo[d] if d in combo else bit_of(d) for d in dims(group))
            there = tuple(1 - own if d == bit else k for d, k in zip(dims(group), keep))
            total = (group.acc[keep].astype(F32) + group.landed[there].astype(F32)).astype(BF16)
            if last:
                gathered[(mine, group.index) + tuple(bit_of(d) for d in bits)] = total
            else:
                group.acc[keep] = total
        group.live.wait_send()

    def double_begin(group):
        done = group.doublings[: group.step]
        bit = group.doublings[group.step] if group.step < count else core
        i = group.index * (count + 1) + group.step
        part = gathered.at[
            (mine, group.index) + tuple(slice(None) if d in done else pl.ds(bit_of(d), 1) for d in bits)
        ]
        group.live = remote(part, part, back_send.at[i], back_recv.at[i], bit)
        group.live.start()
        group.step += 1

    def double_finish(group):
        group.live.wait_recv()
        group.live.wait_send()

    stores = []

    def store(group):
        for side in range(2):
            copy = pltpu.make_async_copy(
                gathered.at[side, group.index], summed.at[side, group.index], store_sem.at[2 * group.index + side]
            )
            copy.start()
            stores.append(copy)

    def plan(group):
        group.step = 0
        steps = [] if group.early else [(swap_begin, swap_finish)]
        steps += [(halve_begin, halve_finish)] * len(group.halvings)
        steps += [(double_begin, double_finish)] * (count + 1)
        return steps

    plans = [plan(group) for group in groups]

    def advance(g):
        group, steps = groups[g], plans[g]
        if group.at > 0:
            steps[group.at - 1][1](group)
        if group.at < len(steps):
            steps[group.at][0](group)
        else:
            store(group)
        group.at += 1


    me = lax.axis_index("rays")
    lat = latent_mid.shape[0]
    near, far = ("rays", 1), ("rays", 2)
    near_copies = [
        remote(latent_part.at[2 * i + 1 - lax.rem(me, 2)], latent_landed.at[i], latent_send.at[i], latent_recv.at[i], near)
        for i in range(2)
    ]
    far_copy = remote(latent_mid, latent_landed.at[2], latent_send.at[2], latent_recv.at[2], far)
    small_copies = [
        remote(smalls.at[t], small_landed.at[t], small_send.at[t], small_recv.at[t], partners[t])
        for t in range(count + 1)
    ]

    def early_begin():
        need(4)
        for g in range(EARLY):
            for i in range(1 << (count - 2)):
                rows = slice(i * piece, (i + 1) * piece)
                total = v_kept[g, rows, :].astype(F32)
                for other in (v_first, v_second, v_both):
                    total = total + other[g, rows, :].astype(F32)
                early_acc[(g,) + tuple((i >> (count - 3 - k)) & 1 for k in range(count - 2))] = total.astype(BF16)
            advance(g)

    step = 256

    def weight_grad(index, left, right):
        @pl.loop(0, width // step)
        def _(j):
            first = pl.multiple_of(j * step, step)
            part = dot(left[:, pl.ds(first, step)], right[...], 0, 0).astype(BF16)
            rows = pl.ds(pl.multiple_of(index * size + first, step), step)
            late[0, rows, :] = part[:, :half_width]
            late[1, rows, :] = part[:, half_width:]

        advance(EARLY + index)

    def unsort_part():
        need(11)
        unsort_rows(v_grad_queries, v_sorted, position_column)

    def query_part():
        need(12)
        weight_grad(0, v_ray_normed, v_grad_queries)

    def key_part():
        need(6)
        weight_grad(1, v_latent_normed, v_grad_keys)

    def value_part():
        need(7)
        weight_grad(2, v_latent_normed, v_grad_values)

    turns = {"L": 0, "R": 0}

    def latents_begin():
        need(10)
        i = turns["L"]
        turns["L"] += 1
        rows = slice(i * lat, (i + 1) * lat)
        part = dot(v_grad_keys[rows, :], v_key_w[...], 1, 1) + dot(v_grad_values[rows, :], v_value_w[...], 1, 1)
        standard, _ = stand(v_latent_all[rows, :].astype(F32))
        smalls[0, 8:9, :] += jnp.sum(part * standard, axis=0, keepdims=True)
        smalls[0, 9:10, :] += jnp.sum(part, axis=0, keepdims=True)
        latent_part[i] = part.astype(BF16)
        if i == 3:
            for copy in near_copies:
                copy.start()

    def latents_next():
        for copy in near_copies:
            copy.wait_recv()
            copy.wait_send()
        other = lax.bitwise_xor(me, 2)
        latent_mid[...] = (
            latent_part[other].astype(F32) + latent_landed[lax.div(other, 2)].astype(F32)
        ).astype(BF16)
        far_copy.start()

    def latents_end():
        far_copy.wait_recv()
        far_copy.wait_send()
        grad_normed = (
            latent_part[me].astype(F32) + latent_landed[lax.div(me, 2)].astype(F32) + latent_landed[2].astype(F32)
        )
        standard, inverse = stand(v_latent_all[pl.ds(pl.multiple_of(me * lat, 32), lat), :].astype(F32))
        latent_grad[...] = norm_back(grad_normed, standard, inverse, as_row(latent_gain)).astype(BF16)

    def rays_part():
        need(15)
        chunk = rays.shape[0] // 4
        i = turns["R"]
        turns["R"] += 1
        rows = slice(i * chunk, (i + 1) * chunk)
        grad_normed = dot(v_grad_queries[rows, :], v_query_w[...], 1, 1)
        standard, inverse = stand(v_rays[rows, :].astype(F32))
        smalls[0, 6:7, :] += jnp.sum(grad_normed * standard, axis=0, keepdims=True)
        smalls[0, 7:8, :] += jnp.sum(grad_normed, axis=0, keepdims=True)
        ray_grad[rows, :] = (
            v_grad_hidden[rows, :] + norm_back(grad_normed, standard, inverse, as_row(ray_gain))
        ).astype(BF16)
        if i == 3:
            small_copies[0].start()

    small_at = [0]

    def small_next():
        t = small_at[0]
        small_copies[t].wait_recv()
        smalls[t + 1] = smalls[t] + small_landed[t]
        small_copies[t].wait_send()
        small_at[0] += 1
        if t + 1 <= count:
            small_copies[t + 1].start()
        else:
            small[...] = smalls[count + 1]

    tasks = {
        "E": early_begin, "U": unsort_part, "Q": query_part, "K": key_part, "V": value_part, "L": latents_begin, "M": latents_next,
        "N": latents_end, "R": rays_part, "S": small_next,
    }
    for letter in script:
        if letter in tasks:
            tasks[letter]()
        else:
            advance(int(letter))
    while small_at[0] <= count:
        small_next()
    while any(group.at <= len(steps) for group, steps in zip(groups, plans)):
        for g in range(len(groups)):
            if groups[g].at <= len(plans[g]):
                advance(g)
    for copy in stores:
        copy.wait()


def widen_kernel(size, summed, small, *refs):
    down, up, out, query, key, value = refs[:6]
    vectors, up_bias, (held, wide, load_sem, store_sem) = refs[6:14], refs[14], refs[15:]
    for at, vector in zip((5, 0, 6, 7, 8, 9, 3, 4), vectors):
        vector[...] = small[at]
    up_bias[: small.shape[1]] = small[1]
    up_bias[small.shape[1] :] = small[2]
    width = held.shape[3] * 2
    half = width // 2
    step = held.shape[2]
    jobs = []
    for g in range(8):
        for r in range(0, width, step):
            if g < 2:
                target = down.at[pl.ds(g * width + r, step), :]
            elif g < 4:
                target = up.at[pl.ds(r, step), pl.ds((g - 2) * width, width)]
            else:
                target = (out, query, key, value)[g - 4].at[pl.ds(r, step), :]
            jobs.append((summed.at[:, pl.ds(g * size + r, step), :], target))
    slots = held.shape[0]
    loads = [pltpu.make_async_copy(src, held.at[i % slots], load_sem.at[i % slots]) for i, (src, _) in enumerate(jobs)]
    saves = [pltpu.make_async_copy(wide.at[i % slots], dst, store_sem.at[i % slots]) for i, (_, dst) in enumerate(jobs)]
    for i in range(slots):
        loads[i].start()
    for i in range(len(jobs)):
        slot = i % slots
        loads[i].wait()
        if i >= slots:
            saves[i - slots].wait()
        wide[slot, :, :half] = held[slot, 0].astype(F32)
        wide[slot, :, half:] = held[slot, 1].astype(F32)
        saves[i].start()
        if i + slots < len(jobs):
            loads[i + slots].start()
    for i in range(len(jobs) - slots, len(jobs)):
        saves[i].wait()


def log2(n):
    return n.bit_length() - 1


EARLY = 5


HALVINGS = ("zw", "zw", "wz", "zw", "zw", "yzxw", "xzyw", "yxwz")
DOUBLINGS = ("zwyx", "wyzx", "wzxy", "ywxz", "zxyw", "wyxz", "wzxy", "zwyx")
SCRIPT = (
    "EKV0U16723Q4L0L12536047L1L2R67R5430M21R6R47502S3",
    "5S176S57SN06S543067215627153463745675",
)


def ways(items, ray_parts):
    core, y, x = ("rays", 1), ("rays", 2), ("items", 1)
    bits = (x, y) + tuple(("items", 2 << i) for i in range(log2(items) - 1)) + tuple(
        ("rays", 4 << i) for i in range(log2(ray_parts) - 2)
    )
    if len(bits) != 4:
        return core, bits, (bits[2:],) * EARLY + (bits,) * 3, (bits[::-1],) * (EARLY + 3), "EKVUQLLLLRRRRMN"
    name = dict(zip("xyzw", bits))
    halvings = tuple(tuple(name[c] for c in word) for word in HALVINGS)
    doublings = tuple(tuple(name[c] for c in word) for word in DOUBLINGS)
    return core, bits, halvings, doublings, "".join(SCRIPT)


def on_device(
    items, ray_parts,
    rays, latents, ray_scene, latent_scene, latent_pad, cotangent,
    query_weight, key_weight, value_weight, out_weight, out_bias, up_weight, up_bias, down_weight, down_bias,
    ray_gain, ray_shift, latent_gain, latent_shift, mlp_gain, mlp_shift,
):
    _, count, width = rays.shape
    lat = latents.shape[1]
    total = lat * ray_parts
    padded = total + WINDOW
    hidden_width = up_weight.shape[1]
    x = rays[0]
    upstream = cotangent[0]

    shape = jax.ShapeDtypeStruct
    rows_bf16 = shape((count, width), BF16)
    total_bf16 = shape((total, width), BF16)
    dma = pltpu.SemaphoreType.DMA

    square = shape((width, width), BF16)
    padded_bf16 = shape((padded, width), BF16)
    (
        ray_normed, sorted_queries, keys, values, latent_normed, latent_all, meta, position_row, position_column,
    ) = pl.pallas_call(
        project_kernel,
        out_shape=(
            rows_bf16, rows_bf16, padded_bf16, padded_bf16, total_bf16, total_bf16,
            shape((2 * SCENES + 2,), jnp.int32), shape((1, count), jnp.int32), shape((count, 1), jnp.int32),
        ),
        in_specs=[anywhere()] * 5 + [vmem()] * 7,
        out_specs=[anywhere()] * 6 + [smem(), vmem(), vmem()],
        scratch_shapes=[pltpu.VMEM((3, lat, width), BF16), pltpu.VMEM((count, width), BF16)]
        + [pltpu.VMEM((lat, width), BF16)] + [pltpu.VMEM((width, width), BF16)] * 3
        + [pltpu.VMEM((count, width), BF16)] * 3
        + [pltpu.VMEM((padded, width), BF16)] * 2 + [pltpu.VMEM((total, width), BF16)]
        + [dma((5,)), dma((5,)), dma((5,)), dma((20,))],
        compiler_params=big(collective_id=1, has_side_effects=True),
        name="project",
    )(
        x, latents[0], query_weight, key_weight, value_weight,
        ray_gain, ray_shift, latent_gain, latent_shift, ray_scene, latent_scene, latent_pad,
    )

    mixture, sorted_mixture, log_total = run_attend(meta, sorted_queries, keys, values, position_column)

    core, bits, halvings, doublings, script = ways(items, ray_parts)
    first, second = bits[:2]
    nbits = len(bits)
    unit = 16 << nbits
    size = (width + unit - 1) // unit * unit
    quarter = size // 4
    half_width = width // 2
    groups = len(halvings)
    late_groups = groups - EARLY
    piece = (size >> nbits, half_width)
    quarter_bf16 = (EARLY, quarter, half_width)

    ray_out, grad_mixture, grad_hidden, kept, to_first, to_second, to_both, early_sums = pl.pallas_call(
        functools.partial(mlp_kernel, core, first, second, size),
        out_shape=(
            rows_bf16, rows_bf16, shape((count, width), F32),
            shape(quarter_bf16, BF16), shape(quarter_bf16, BF16), shape(quarter_bf16, BF16), shape(quarter_bf16, BF16),
            shape((8, width), F32),
        ),
        in_specs=[anywhere()] * 6 + [vmem()] * 5,
        out_specs=[anywhere()] * 7 + [vmem()],
        scratch_shapes=[
            pltpu.VMEM((count, width), BF16), pltpu.VMEM((width, width), BF16), pltpu.VMEM((count, width), BF16),
            pltpu.VMEM((width, hidden_width), BF16), pltpu.VMEM((hidden_width, width), BF16),
            pltpu.VMEM((count, width), BF16),
            pltpu.VMEM((count, width), BF16), pltpu.VMEM((count, width), BF16), pltpu.VMEM((count, width), F32),
            pltpu.VMEM((4,) + quarter_bf16, BF16),
            pltpu.VMEM((count, hidden_width), BF16), pltpu.VMEM((count, hidden_width), BF16),
            pltpu.VMEM((count, width), BF16), pltpu.VMEM((count, width), BF16),
            pltpu.VMEM((2, EARLY * size, half_width), BF16), pltpu.VMEM((EARLY * size, half_width), BF16),
            dma((15,)), dma((15,)), dma((6,)), dma((12,)), dma((4 * EARLY,)),
        ],
        compiler_params=big(collective_id=2, has_side_effects=True),
        name="mlp",
    )(
        mixture, out_weight, x, up_weight, down_weight, upstream,
        out_bias, up_bias, down_bias, mlp_gain, mlp_shift,
    )

    def flip(index, partners):
        item, part = index // ray_parts, index % ray_parts
        for axis, bit in partners:
            item, part = (item ^ bit, part) if axis == "items" else (item, part ^ bit)
        return item * ray_parts + part

    def exchange(array, *partners):
        return lax.ppermute(
            array, ("items", "rays"), [(i, flip(i, partners)) for i in range(items * ray_parts)]
        )

    from_first = exchange(to_first, first)
    from_second = exchange(to_second, second)
    from_both = exchange(to_both, first, second)

    sorted_grad, grad_keys, grad_values = run_attend_back(
        meta, grad_mixture, position_row, sorted_queries, sorted_mixture, log_total, keys, values
    )

    held = [shape(quarter_bf16, BF16)] * 4 + [total_bf16] * 3 + [rows_bf16] * 0
    held = held + [square, square, total_bf16, rows_bf16, rows_bf16, square, rows_bf16, shape((count, width), F32)]
    held = held + [rows_bf16]
    ray_grad, latent_grad, summed, small = pl.pallas_call(
        functools.partial(reduce_kernel, core, bits, halvings, doublings, size, script),
        out_shape=(
            rows_bf16, shape((lat, width), BF16), shape((2, groups) + (2,) * nbits + piece, BF16),
            shape((16, width), F32),
        ),
        in_specs=[anywhere()] * 15 + [vmem()] * 4,
        out_specs=[vmem(), vmem(), anywhere(), vmem()],
        scratch_shapes=[pltpu.VMEM(h.shape, h.dtype) for h in held] + [
            pltpu.VMEM((2, late_groups * size, half_width), BF16),
            pltpu.VMEM((late_groups * size, half_width), BF16),
            pltpu.VMEM((EARLY,) + (2,) * (nbits - 2) + piece, BF16),
            pltpu.VMEM((EARLY,) + (2,) * (nbits - 2) + piece, BF16),
            pltpu.VMEM((late_groups,) + (2,) * nbits + piece, BF16),
            pltpu.VMEM((late_groups,) + (2,) * nbits + piece, BF16),
            pltpu.VMEM((2, groups) + (2,) * nbits + piece, BF16),
            pltpu.VMEM((nbits + 2, 16, width), F32),
            pltpu.VMEM((nbits + 1, 16, width), F32),
            pltpu.VMEM((4, lat, width), BF16),
            pltpu.VMEM((3, lat, width), BF16),
            pltpu.VMEM((lat, width), BF16),
            dma((15,)), dma((late_groups,)), dma((late_groups,)),
            dma((groups * nbits,)), dma((groups * nbits,)), dma((groups * (nbits + 1),)), dma((groups * (nbits + 1),)),
            dma((nbits + 1,)), dma((nbits + 1,)), dma((3,)), dma((3,)), dma((2 * groups,)),
        ],
        compiler_params=big(collective_id=3, has_side_effects=True),
        name="reduce",
    )(
        kept, from_first, from_second, from_both,
        latent_normed, grad_keys, grad_values, key_weight, value_weight, latent_all,
        sorted_grad, ray_normed, query_weight, x, grad_hidden,
        ray_gain, latent_gain, early_sums, position_column,
    )

    wide = shape((width, width), F32)
    step, slots = 768, 8
    (
        down_grad, up_grad, out_grad, query_grad, key_grad, value_grad,
        out_bias_grad, down_bias_grad, ray_gain_grad, ray_shift_grad, latent_gain_grad, latent_shift_grad,
        mlp_gain_grad, mlp_shift_grad, up_bias_grad,
    ) = pl.pallas_call(
        functools.partial(widen_kernel, size),
        out_shape=(shape((2 * width, width), F32), shape((width, 2 * width), F32), wide, wide, wide, wide)
        + (shape((width,), F32),) * 8 + (shape((hidden_width,), F32),),
        in_specs=[anywhere(), vmem()],
        out_specs=[anywhere()] * 6 + [vmem()] * 9,
        scratch_shapes=[
            pltpu.VMEM((slots, 2, step, half_width), BF16), pltpu.VMEM((slots, step, width), F32),
            dma((slots,)), dma((slots,)),
        ],
        compiler_params=big(),
        name="widen",
    )(summed.reshape(2, groups * size, half_width), small)

    return (
        ray_out[None], ray_grad[None], latent_grad[None],
        query_grad, key_grad, value_grad, out_grad, out_bias_grad,
        up_grad, up_bias_grad, down_grad, down_bias_grad,
        ray_gain_grad, ray_shift_grad, latent_gain_grad, latent_shift_grad, mlp_gain_grad, mlp_shift_grad,
    )


def solution(mesh):
    split = P("items", "rays", None)
    in_specs = (split, split, P("items", "rays"), P("items", None), P("items", None), split) + (P(),) * 15
    out_specs = (split, split, split) + (P(),) * 15
    return jax.shard_map(
        functools.partial(on_device, mesh.shape["items"], mesh.shape["rays"]),
        mesh=mesh, in_specs=in_specs, out_specs=out_specs, check_vma=False,
    )
```

```python
import functools

import jax
import jax.numpy as jnp
from jax import lax
from jax.experimental import pallas as pl
from jax.experimental.pallas import tpu as pltpu
from jax.sharding import PartitionSpec as P

HEADS = 12
HEAD_DIM = 64
PAIRS = HEADS // 2
SCENES = 4
EPSILON = 1e-05
SCALE = HEAD_DIM ** (-0.5)
BLOCK = 128
WINDOW = 256
OUTSIDE = -1e30
MANY = 5
MESH = pl.DeviceIdType.MESH
F32 = jnp.float32
BF16 = jnp.bfloat16
MIB = 2**20


def dot(left, right, left_dim=1, right_dim=0):
    return lax.dot_general(
        left, right, (((left_dim,), (right_dim,)), ((), ())), preferred_element_type=F32
    )


def stand(rows):
    center = rows - jnp.mean(rows, axis=-1, keepdims=True)
    inverse = lax.rsqrt(jnp.mean(center * center, axis=-1, keepdims=True) + EPSILON)
    return center * inverse, inverse


def norm_back(grad_out, standard, inverse, gain):
    scaled = grad_out * gain
    return inverse * (
        scaled
        - jnp.mean(scaled, axis=-1, keepdims=True)
        - standard * jnp.mean(scaled * standard, axis=-1, keepdims=True)
    )


def as_row(vector):
    return vector[...].reshape(1, -1)


def vmem():
    return pl.BlockSpec(memory_space=pltpu.VMEM)


def smem():
    return pl.BlockSpec(memory_space=pltpu.SMEM)


def anywhere():
    return pl.BlockSpec(memory_space=pl.ANY)


def peer(axis, bit):
    return {axis: lax.bitwise_xor(lax.axis_index(axis), bit)}


def greet(partners):
    barrier = pltpu.get_barrier_semaphore()
    for axis, bit in partners:
        pl.semaphore_signal(barrier, inc=1, device_id=peer(axis, bit), device_id_type=MESH)
    pl.semaphore_wait(barrier, len(partners))


def bit_of(partner):
    axis, bit = partner
    return lax.rem(lax.div(lax.axis_index(axis), bit), 2)


def remote(src, dst, send, recv, partner):
    return pltpu.make_async_remote_copy(
        src_ref=src, dst_ref=dst, send_sem=send, recv_sem=recv, device_id=peer(*partner), device_id_type=MESH
    )


def project_kernel(
    rays, latents, query_w, key_w, value_w, ray_gain, ray_shift, latent_gain, latent_shift,
    ray_scene, latent_scene, latent_pad,
    ray_normed, sorted_queries, keys, values, latent_normed, latent_all, meta, position_row, position_column,
    landed, v_rays, v_latents, v_query_w, v_key_w, v_value_w,
    normed, queries, in_order, key_rows, value_rows, latent_rows,
    send_sem, recv_sem, load_sem, store_sem,
):
    me = lax.axis_index("rays")
    lat = latents.shape[0]
    total = 4 * lat
    near, far = ("rays", 1), ("rays", 2)
    pairs = ((latents, v_latents), (rays, v_rays), (query_w, v_query_w), (key_w, v_key_w), (value_w, v_value_w))
    loads = [pltpu.make_async_copy(src, dst, load_sem.at[i]) for i, (src, dst) in enumerate(pairs)]
    for load in loads:
        load.start()
    greet([near, far])

    def copy(src, slot, part, partner, index):
        return remote(src.at[part], landed.at[slot, part], send_sem.at[index], recv_sem.at[index], partner)

    whole, halves = slice(0, lat), (slice(0, lat // 2), slice(lat // 2, lat))
    to_far = [copy(latents, 1, part, far, i) for i, part in enumerate(halves)]
    to_near = copy(latents, 0, whole, near, 2)
    passed = [copy(landed.at[1], 2, part, near, 3 + i) for i, part in enumerate(halves)]
    for send in to_far:
        send.start()
    to_near.start()

    stores = []

    def keep(src, dst):
        saved = pltpu.make_async_copy(src, dst, store_sem.at[len(stores)])
        saved.start()
        stores.append(saved)

    sort_plan(ray_scene, latent_scene, latent_pad, meta, position_row, position_column)
    loads[1].wait()
    loads[2].wait()
    chunk = 256

    @pl.loop(0, rays.shape[0] // chunk)
    def _(i):
        rows = pl.ds(pl.multiple_of(i * chunk, chunk), chunk)
        standard, _ = stand(v_rays[rows, :].astype(F32))
        low = (standard * as_row(ray_gain) + as_row(ray_shift)).astype(BF16)
        normed[rows, :] = low
        projected = dot(low, v_query_w[...]).astype(BF16)
        queries[rows, :] = (projected.astype(F32) * SCALE).astype(BF16)

    keep(normed, ray_normed)
    sort_rows(in_order, queries, position_row)
    keep(in_order, sorted_queries)

    def one(raw, owner):
        rows = pl.ds(pl.multiple_of(owner * lat, 32), lat)
        standard, _ = stand(raw[...].astype(F32))
        low = (standard * as_row(latent_gain) + as_row(latent_shift)).astype(BF16)
        latent_rows[rows, :] = low
        keep(raw, latent_all.at[rows])
        keep(latent_rows.at[rows], latent_normed.at[rows])
        key_rows[rows, :] = dot(low, v_key_w[...]).astype(BF16)
        keep(key_rows.at[rows], keys.at[rows])
        value_rows[rows, :] = dot(low, v_value_w[...]).astype(BF16)
        keep(value_rows.at[rows], values.at[rows])

    key_rows[total:, :] = jnp.zeros((keys.shape[0] - total, keys.shape[1]), BF16)
    keep(key_rows.at[total:], keys.at[total:])
    keep(key_rows.at[total:], values.at[total:])
    for i in (0, 3, 4):
        loads[i].wait()
    one(v_latents, me)
    to_near.wait_recv()
    one(landed.at[0], lax.bitwise_xor(me, 1))
    for got, on in zip(to_far, passed):
        got.wait_recv()
        on.start()
    one(landed.at[1], lax.bitwise_xor(me, 2))
    for got in passed:
        got.wait_recv()
    one(landed.at[2], lax.bitwise_xor(me, 3))
    for send in to_far + [to_near] + passed:
        send.wait_send()
    for saved in stores:
        saved.wait()


def lanes_of(shape):
    return lax.broadcasted_iota(jnp.int32, shape, len(shape) - 1)


def rows_of(shape):
    return lax.broadcasted_iota(jnp.int32, shape, 0)


def sort_plan(ray_scene, latent_scene, latent_pad, meta, position_row, position_column):
    count = ray_scene.shape[1]
    for s in range(1, SCENES):
        meta[s] = jnp.sum(jnp.where(ray_scene[...] < s, 1, 0))
    meta[0] = 0
    meta[SCENES] = count
    meta[SCENES + 1] = 0
    for s in range(1, SCENES + 1):
        meta[SCENES + 1 + s] = jnp.sum(jnp.where((latent_scene[...] < s) & (latent_pad[...] == 0), 1, 0))
    order_row = (ray_scene[...] * count + lanes_of((1, count))).astype(F32)
    order_column = jnp.broadcast_to(order_row, (8, count)).T[:, :1]
    step = 256
    smaller = jnp.zeros((1, count), F32)
    for i in range(count // step):
        before = jnp.where(order_column[i * step : (i + 1) * step] < order_row, 1.0, 0.0)
        smaller = smaller + jnp.sum(before, axis=0, keepdims=True)
    position_row[...] = smaller.astype(jnp.int32)
    position_column[...] = jnp.broadcast_to(smaller, (8, count)).T[:, :1].astype(jnp.int32)


def block_range(meta, block):
    first, last = block * BLOCK, block * BLOCK + BLOCK - 1
    low = sum(jnp.where(meta[s] <= first, 1, 0) for s in range(1, SCENES))
    high = sum(jnp.where(meta[s] <= last, 1, 0) for s in range(1, SCENES))
    start = meta[SCENES + 1 + low] // 16 * 16
    return start, (meta[SCENES + 2 + high] - start + WINDOW - 1) // WINDOW


def sort_rows(target, source, position_row):
    count = source.shape[0]
    step = 512

    @pl.loop(0, count // step)
    def _(i):
        first = pl.multiple_of(i * step, step)
        index = rows_of((step, count)) + first
        chosen = jnp.where(index == position_row[...], 1.0, 0.0).astype(BF16)
        target[pl.ds(first, step), :] = dot(chosen, source[...]).astype(BF16)


def unsort_rows(target, source, position_column):
    count = source.shape[0]
    step = 512

    @pl.loop(0, count // step)
    def _(i):
        first = pl.multiple_of(i * step, step)
        index = lanes_of((step, count))
        chosen = jnp.where(index == position_column[pl.ds(first, step), :], 1.0, 0.0).astype(BF16)
        target[pl.ds(first, step), :] = dot(chosen, source[...]).astype(BF16)


def latent_features(meta, extra):
    shape = extra.shape
    row = rows_of(shape)
    lane = lanes_of((1, shape[1]))
    first = jnp.full((1, shape[1]), meta[SCENES + 1], jnp.int32)
    last = jnp.full((1, shape[1]), meta[SCENES + 2], jnp.int32)
    for s in range(1, SCENES):
        first = jnp.where(lane == s, meta[SCENES + 1 + s], first)
        last = jnp.where(lane == s, meta[SCENES + 2 + s], last)
    first = jnp.where(lane >= SCENES, 0, first)
    last = jnp.where(lane >= SCENES, shape[0], last)
    value = jnp.where((row >= first) & (row < last), 0.0, OUTSIDE)
    extra[...] = value.astype(BF16)


def ray_features(meta, block):
    shape = (BLOCK, 128)
    row = rows_of(shape) + block * BLOCK
    lane = lanes_of((1, 128))
    first = jnp.full((1, 128), count_none, jnp.int32)
    last = jnp.zeros((1, 128), jnp.int32)
    for s in range(SCENES):
        first = jnp.where(lane == s, meta[s], first)
        last = jnp.where(lane == s, meta[s + 1], last)
    return jnp.where((row >= first) & (row < last), 1.0, 0.0)


count_none = 2**30


def half_masks():
    lane = lanes_of((BLOCK, 128))
    low = jnp.where(lane < HEAD_DIM, 1.0, 0.0)
    return low, 1.0 - low


def pick_halves(both):
    lane = lanes_of((BLOCK, 128))
    return jnp.where(lane < HEAD_DIM, both[:BLOCK, :128], both[BLOCK:, :128])


def pair_columns(p):
    return slice(128 * p, 128 * (p + 1))


def over_windows(windows, body):
    @pl.loop(0, windows // 2)
    def _(i):
        body(2 * i, 2)

    @pl.when(windows % 2 == 1)
    def _():
        body(windows - 1, 1)


def attend_kernel(
    meta, sorted_queries, keys, values, position_column,
    mixture, sorted_mixture, log_total,
    latent_extra, stacked, total, peak, held,
):
    rays = sorted_queries.shape[0]
    latent_features(meta, latent_extra)
    ones = jnp.where(lanes_of((WINDOW, 128)) == 0, 1.0, 0.0).astype(BF16)
    low, high = half_masks()
    lane = lanes_of((BLOCK, 128))

    @pl.loop(0, rays // BLOCK)
    def _(block):
        rows = pl.ds(pl.multiple_of(block * BLOCK, BLOCK), BLOCK)
        start, windows = block_range(meta, block)
        extra = ray_features(meta, block).astype(BF16)
        for p in range(PAIRS):
            pair = sorted_queries[rows, pair_columns(p)].astype(F32)
            stacked[p, :BLOCK, :128] = (pair * low).astype(BF16)
            stacked[p, BLOCK:, :128] = (pair * high).astype(BF16)
            stacked[p, :BLOCK, 128:] = extra
            stacked[p, BLOCK:, 128:] = extra

        def window_at(w):
            return pl.ds(pl.multiple_of(start + w * WINDOW, 16), WINDOW)

        def score(w, p):
            window = window_at(w)
            key_side = jnp.concatenate([keys[window, pair_columns(p)], latent_extra[window, :]], axis=1)
            scores = dot(stacked[p], key_side, 1, 1)
            held[w, p] = scores
            return jnp.maximum(scores[:, :128], scores[:, 128:])

        def mix(w, p):
            top = peak[p]
            lifted = jnp.exp(held[w, p] - jnp.concatenate([top, top], axis=1)).astype(BF16)
            return dot(lifted, jnp.concatenate([values[window_at(w), pair_columns(p)], ones], axis=1))

        def highest(top):
            return jnp.broadcast_to(jnp.max(top, axis=1, keepdims=True), (2 * BLOCK, 128))

        def finish(p, both, logs):
            sums = both[:, 128:129]
            mixed = pick_halves(both[:, :128] * (1.0 / sums))
            sorted_mixture[rows, pair_columns(p)] = mixed.astype(BF16)
            log_rows = peak[p] + jnp.log(sums)
            logs = jnp.where(lane == 2 * p, log_rows[:BLOCK], logs)
            return jnp.where(lane == 2 * p + 1, log_rows[BLOCK:], logs)

        def few(number):
            for p in range(PAIRS):
                peak[p] = highest(functools.reduce(jnp.maximum, [score(w, p) for w in range(number)]))
            logs = jnp.zeros((BLOCK, 128), F32)
            for p in range(PAIRS):
                logs = finish(p, functools.reduce(jnp.add, [mix(w, p) for w in range(number)]), logs)
            log_total[rows, :] = logs

        for number in range(1, MANY):
            pl.when(windows == number)(functools.partial(few, number))

        @pl.when(windows >= MANY)
        def _():
            for p in range(PAIRS):
                peak[p] = jnp.full((2 * BLOCK, 128), -3e38, F32)
                total[p] = jnp.zeros((2 * BLOCK, 256), F32)

            @pl.loop(0, windows)
            def _(w):
                for p in range(PAIRS):
                    peak[p] = jnp.maximum(peak[p], score(w, p))

            for p in range(PAIRS):
                peak[p] = highest(peak[p])

            @pl.loop(0, windows)
            def _(w):
                for p in range(PAIRS):
                    total[p] += mix(w, p)

            logs = jnp.zeros((BLOCK, 128), F32)
            for p in range(PAIRS):
                logs = finish(p, total[p], logs)
            log_total[rows, :] = logs

    unsort_rows(mixture, sorted_mixture, position_column)


def attend_back_kernel(
    meta, grad_mixture, position_row, sorted_queries, sorted_mixture, log_total, keys, values,
    grad_queries, grad_keys, grad_values,
    v_queries, v_mixture, v_logs, v_keys, v_values,
    stacked, stacked_grad, sorted_grad, key_total, value_total, query_total, log_rows, inner_rows, bias, probs_low, scores_low, load_sem,
):
    rays = sorted_queries.shape[0]
    given = (sorted_queries, sorted_mixture, log_total, keys, values)
    held = (v_queries, v_mixture, v_logs, v_keys, v_values)
    loads = [pltpu.make_async_copy(src, dst, load_sem.at[i]) for i, (src, dst) in enumerate(zip(given, held))]
    for load in loads:
        load.start()
    key_total[...] = jnp.zeros(key_total.shape, F32)
    value_total[...] = jnp.zeros(value_total.shape, F32)
    sort_rows(sorted_grad, grad_mixture, position_row)
    low, high = half_masks()
    lane = lanes_of((BLOCK, 128))
    for load in loads:
        load.wait()

    @pl.loop(0, rays // BLOCK)
    def _(block):
        rows = pl.ds(pl.multiple_of(block * BLOCK, BLOCK), BLOCK)
        start, windows = block_range(meta, block)
        inner = jnp.zeros((BLOCK, 128), F32)
        for p in range(PAIRS):
            columns = pair_columns(p)
            pair = v_queries[rows, columns].astype(F32)
            grad = sorted_grad[rows, columns].astype(F32)
            product = grad * v_mixture[rows, columns].astype(F32)
            for side, mask in enumerate((low, high)):
                half = slice(side * BLOCK, (side + 1) * BLOCK)
                stacked[p, half, :] = (pair * mask).astype(BF16)
                stacked_grad[p, half, :] = (grad * mask).astype(BF16)
                inner = jnp.where(lane == 2 * p + side, jnp.sum(product * mask, axis=1, keepdims=True), inner)
            query_total[p] = jnp.zeros((2 * BLOCK, 128), F32)
        log_rows[...] = v_logs[rows, :].T
        inner_rows[...] = inner.T

        ray = lanes_of((1, BLOCK)) + block * BLOCK
        first = jnp.full((1, BLOCK), meta[SCENES + 1], jnp.int32)
        last = jnp.full((1, BLOCK), meta[SCENES + 2], jnp.int32)
        for s in range(1, SCENES):
            first = jnp.where(ray >= meta[s], meta[SCENES + 1 + s], first)
            last = jnp.where(ray >= meta[s], meta[SCENES + 2 + s], last)

        def two_rows(ref, p):
            return jnp.concatenate([ref[2 * p : 2 * p + 1, :], ref[2 * p + 1 : 2 * p + 2, :]], axis=1)

        def back(w, number):
            spots = [pl.multiple_of(start + (w + u) * WINDOW, 16) for u in range(number)]
            for u, spot in enumerate(spots):
                row = rows_of((WINDOW, BLOCK)) + spot
                bias[u] = jnp.where((row >= first) & (row < last), 0.0, OUTSIDE)
            for p in range(PAIRS):
                columns = pair_columns(p)
                for u, spot in enumerate(spots):
                    window = pl.ds(spot, WINDOW)
                    key_pair = v_keys[window, columns]
                    scores = dot(key_pair, stacked[p], 1, 1) - two_rows(log_rows, p)
                    probs = jnp.exp(scores + jnp.concatenate([bias[u], bias[u]], axis=1))
                    centered = dot(v_values[window, columns], stacked_grad[p], 1, 1) - two_rows(inner_rows, p)
                    probs_low[u, p] = probs.astype(BF16)
                    scores_low[u, p] = (probs * centered).astype(BF16)
            for p in range(PAIRS):
                columns = pair_columns(p)
                part = None
                for u, spot in enumerate(spots):
                    window = pl.ds(spot, WINDOW)
                    value_total[window, columns] += dot(probs_low[u, p], stacked_grad[p])
                    key_total[window, columns] += dot(scores_low[u, p], stacked[p])
                    query = dot(scores_low[u, p], v_keys[window, columns], 0, 0)
                    part = query if part is None else part + query
                query_total[p] += part

        over_windows(windows, back)

        for p in range(PAIRS):
            grad_queries[rows, pair_columns(p)] = (pick_halves(query_total[p]) * SCALE).astype(BF16)

    count = grad_keys.shape[0]
    grad_keys[...] = key_total[:count, :].astype(BF16)
    grad_values[...] = value_total[:count, :].astype(BF16)


def big(**rest):
    return pltpu.CompilerParams(vmem_limit_bytes=60 * MIB, **rest)


def run_attend(meta, sorted_queries, keys, values, position_column):
    count, width = sorted_queries.shape
    padded = keys.shape[0]
    shape = jax.ShapeDtypeStruct
    rows_bf16 = shape((count, width), BF16)
    most = (padded - 1) // WINDOW + 1
    return pl.pallas_call(
        attend_kernel,
        out_shape=(rows_bf16, rows_bf16, shape((count, 128), F32)),
        in_specs=[smem()] + [vmem()] * 4,
        out_specs=[vmem()] * 3,
        scratch_shapes=[
            pltpu.VMEM((padded, 128), BF16),
            pltpu.VMEM((PAIRS, 2 * BLOCK, 256), BF16),
            pltpu.VMEM((PAIRS, 2 * BLOCK, 256), F32),
            pltpu.VMEM((PAIRS, 2 * BLOCK, 128), F32),
            pltpu.VMEM((most, PAIRS, 2 * BLOCK, WINDOW), F32),
        ],
        compiler_params=big(),
        name="attend",
    )(meta, sorted_queries, keys, values, position_column)


def run_attend_back(meta, grad_mixture, position_row, sorted_queries, sorted_mixture, log_total, keys, values):
    count, width = grad_mixture.shape
    padded = keys.shape[0]
    total = padded - WINDOW
    shape = jax.ShapeDtypeStruct
    return pl.pallas_call(
        attend_back_kernel,
        out_shape=(shape((count, width), BF16), shape((total, width), BF16), shape((total, width), BF16)),
        in_specs=[smem()] + [vmem()] * 2 + [anywhere()] * 5,
        out_specs=[vmem()] * 3,
        scratch_shapes=[
            pltpu.VMEM((count, width), BF16),
            pltpu.VMEM((count, width), BF16),
            pltpu.VMEM((count, 128), F32),
            pltpu.VMEM((padded, width), BF16),
            pltpu.VMEM((padded, width), BF16),
            pltpu.VMEM((PAIRS, 2 * BLOCK, 128), BF16),
            pltpu.VMEM((PAIRS, 2 * BLOCK, 128), BF16),
            pltpu.VMEM((count, width), BF16),
            pltpu.VMEM((padded, width), F32),
            pltpu.VMEM((padded, width), F32),
            pltpu.VMEM((PAIRS, 2 * BLOCK, 128), F32),
            pltpu.VMEM((128, BLOCK), F32),
            pltpu.VMEM((128, BLOCK), F32),
            pltpu.VMEM((2, WINDOW, BLOCK), F32),
            pltpu.VMEM((2, PAIRS, WINDOW, 2 * BLOCK), BF16),
            pltpu.VMEM((2, PAIRS, WINDOW, 2 * BLOCK), BF16),
            pltpu.SemaphoreType.DMA((5,)),
        ],
        compiler_params=big(),
        name="attend_back",
    )(meta, grad_mixture, position_row, sorted_queries, sorted_mixture, log_total, keys, values)


def quarter_start(first, second, size, flips):
    one = bit_of(first) if not flips[0] else 1 - bit_of(first)
    two = bit_of(second) if not flips[1] else 1 - bit_of(second)
    return one * (size // 2) + two * (size // 4)


def mlp_kernel(
    core, first, second, size,
    given_mixture, given_out_w, given_rays, given_up_w, given_down_w, given_cotangent, out_bias, up_bias, down_bias, mlp_gain, mlp_shift,
    kept_ray_out, kept_grad_mixture, kept_grad_hidden, kept, to_first, to_second, to_both, sums,
    mixture, out_w, rays, up_w, down_w, cotangent, ray_out, grad_mixture, grad_hidden, quarters,
    act, grad_pre, normed, branch, early, landed, send_sem, recv_sem, load_sem, store_sem, quarter_sem,
):
    chunk = 512
    width = rays.shape[1]
    half_width = width // 2
    pairs = (
        (given_mixture, mixture), (given_out_w, out_w), (given_rays, rays), (given_up_w, up_w),
        (given_down_w, down_w), (given_cotangent, cotangent),
    )
    loads = [pltpu.make_async_copy(src, dst, load_sem.at[i]) for i, (src, dst) in enumerate(pairs)]
    for load in loads:
        load.start()
    greet([core])
    mine = bit_of(core)

    def keep(i):
        rows = pl.ds(pl.multiple_of(i * chunk, chunk), chunk)
        results = ((ray_out, kept_ray_out), (grad_hidden, kept_grad_hidden), (grad_mixture, kept_grad_mixture))
        return [
            pltpu.make_async_copy(src.at[rows], dst.at[rows], store_sem.at[3 * i + k])
            for k, (src, dst) in enumerate(results)
        ]

    sums[...] = jnp.zeros(sums.shape, F32)
    root = 0.7978845608028654
    cubic = 0.044715

    @pl.loop(0, rays.shape[0] // chunk)
    def _(i):
        rows = pl.ds(pl.multiple_of(i * chunk, chunk), chunk)

        def need(*which):
            @pl.when(i == 0)
            def _():
                for k in which:
                    loads[k].wait()

        need(0, 1, 2)
        hidden = rays[rows, :].astype(F32) + dot(mixture[rows, :], out_w[...]) + as_row(out_bias)
        standard, inverse = stand(hidden)
        low = (standard * as_row(mlp_gain) + as_row(mlp_shift)).astype(BF16)
        normed[rows, :] = low
        need(3)
        half = 768
        out = hidden + as_row(down_bias)
        grad_mlp = jnp.zeros((chunk, width), F32)
        for j in range(up_w.shape[1] // half):
            cols = slice(j * half, (j + 1) * half)
            pre = dot(low, up_w[:, cols]) + up_bias[cols].reshape(1, half)
            square = pre * pre
            bend = jnp.tanh(root * pre * (1.0 + cubic * square))
            rise = 0.5 * (1.0 + bend)
            active = (pre * rise).astype(BF16)
            slope = rise + 0.5 * pre * (1.0 - bend * bend) * (root * (1.0 + 3.0 * cubic * square))
            act[rows, cols] = active
            if j == 0:
                need(4, 5)
                upstream = cotangent[rows, :]
            out = out + dot(active, down_w[cols, :])
            back = (dot(upstream, down_w[cols, :], 1, 1) * slope).astype(BF16)
            grad_pre[rows, cols] = back
            sums[1 + j : 2 + j, :] += jnp.sum(back.astype(F32), axis=0, keepdims=True)
            grad_mlp = grad_mlp + dot(back, up_w[:, cols], 1, 1)
        ray_out[rows, :] = out.astype(BF16)
        wide = upstream.astype(F32)
        sums[0:1, :] += jnp.sum(wide, axis=0, keepdims=True)
        sums[3:4, :] += jnp.sum(grad_mlp * standard, axis=0, keepdims=True)
        sums[4:5, :] += jnp.sum(grad_mlp, axis=0, keepdims=True)
        through = wide + norm_back(grad_mlp, standard, inverse, as_row(mlp_gain))
        grad_hidden[rows, :] = through
        rounded = through.astype(BF16)
        branch[rows, :] = rounded
        sums[5:6, :] += jnp.sum(rounded.astype(F32), axis=0, keepdims=True)
        grad_mixture[rows, :] = dot(rounded, out_w[...], 1, 1).astype(BF16)
        for saved in keep(i):
            saved.start()

    step = 384
    tiles = width // step

    def swap(tile):
        rows = pl.ds(pl.multiple_of(lax.div(tile, tiles) * size + lax.rem(tile, tiles) * step, step), step)
        return remote(early.at[1 - mine, rows], landed.at[rows], send_sem.at[tile], recv_sem.at[tile], core)

    def store(tile, left, right):
        rows = pl.ds(pl.multiple_of(lax.div(tile, tiles) * size + lax.rem(tile, tiles) * step, step), step)
        part = dot(left, right, 0, 0).astype(BF16)
        early[0, rows, :] = part[:, :half_width]
        early[1, rows, :] = part[:, half_width:]
        swap(tile).start()

    @pl.loop(0, 2 * tiles)
    def _(j):
        store(j, act[:, pl.ds(pl.multiple_of(j * step, step), step)], cotangent[...])

    for h in range(2):

        @pl.loop(0, tiles)
        def _(j):
            cols = pl.ds(pl.multiple_of(j * step, step), step)
            store(j + (2 + h) * tiles, normed[:, cols], grad_pre[:, h * width : (h + 1) * width])

    @pl.loop(0, tiles)
    def _(j):
        store(j + 4 * tiles, mixture[:, pl.ds(pl.multiple_of(j * step, step), step)], branch[...])

    quarter = size // 4
    targets = ((kept, (0, 0)), (to_first, (1, 0)), (to_second, (0, 1)), (to_both, (1, 1)))

    def send_off(g, k):
        return pltpu.make_async_copy(quarters.at[k, g], targets[k][0].at[g], quarter_sem.at[4 * g + k])

    for g in range(EARLY):
        for tile in range(g * tiles, (g + 1) * tiles):
            swap(tile).wait_recv()
        for k, (_, flips) in enumerate(targets):
            rows = pl.ds(pl.multiple_of(g * size + quarter_start(first, second, size, flips), 16), quarter)
            quarters[k, g] = (early[mine, rows, :].astype(F32) + landed[rows, :].astype(F32)).astype(BF16)
            send_off(g, k).start()
    for tile in range(5 * tiles):
        swap(tile).wait_send()
    for i in range(rays.shape[0] // chunk):
        for saved in keep(i):
            saved.wait()
    for g in range(EARLY):
        for k in range(4):
            send_off(g, k).wait()


def reduce_kernel(
    core, bits, halvings, doublings, size, script,
    kept, from_first, from_second, from_both,
    latent_normed, grad_keys, grad_values, key_w, value_w, latent_all,
    sorted_grad, ray_normed, query_w, rays, grad_hidden,
    ray_gain, latent_gain, early_sums, position_column,
    ray_grad, latent_grad, summed, small,
    v_kept, v_first, v_second, v_both,
    v_latent_normed, v_grad_keys, v_grad_values, v_key_w, v_value_w, v_latent_all,
    v_sorted, v_ray_normed, v_query_w, v_rays, v_grad_hidden, v_grad_queries,
    late, late_landed, early_acc, early_landed, late_acc, late_in, gathered,
    smalls, small_landed, latent_part, latent_landed, latent_mid,
    load_sem, swap_send, swap_recv, send_sem, recv_sem, back_send, back_recv,
    small_send, small_recv, latent_send, latent_recv, store_sem,
):
    count = len(bits)
    partners = sorted(bits + (core,))
    width = rays.shape[1]
    half_width = width // 2
    piece = size >> count
    held = (
        v_kept, v_first, v_second, v_both,
        v_latent_normed, v_grad_keys, v_grad_values, v_key_w, v_value_w, v_latent_all,
        v_sorted, v_ray_normed, v_query_w, v_rays, v_grad_hidden,
    )
    given = (
        kept, from_first, from_second, from_both,
        latent_normed, grad_keys, grad_values, key_w, value_w, latent_all,
        sorted_grad, ray_normed, query_w, rays, grad_hidden,
    )
    loads = [pltpu.make_async_copy(src, dst, load_sem.at[i]) for i, (src, dst) in enumerate(zip(given, held))]
    for load in loads:
        load.start()
    greet(partners)
    mine = bit_of(core)
    loaded = [0]

    def need(last):
        while loaded[0] < last:
            loads[loaded[0]].wait()
            loaded[0] += 1

    smalls[0] = jnp.zeros(smalls.shape[1:], F32)
    smalls[0, 0:8, :] = early_sums[...]


    class Group:
        pass

    groups = []
    for g in range(EARLY + late_landed.shape[0] // size):
        group = Group()
        group.index, group.at, group.live = g, 0, None
        group.early = g < EARLY
        group.free = list(bits[2:] if group.early else bits)
        group.halvings, group.doublings = list(halvings[g]), list(doublings[g])
        group.done = []
        group.acc = early_acc.at[g] if group.early else late_acc.at[g - EARLY]
        group.landed = early_landed.at[g] if group.early else late_in.at[g - EARLY]
        groups.append(group)

    def combos(names):
        for i in range(1 << len(names)):
            yield {name: (i >> k) & 1 for k, name in enumerate(names)}

    def dims(group):
        return bits[2:] if group.early else bits

    def swap_begin(group):
        i = group.index - EARLY
        rows = pl.ds(i * size, size)
        group.live = remote(late.at[1 - mine, rows], late_landed.at[rows], swap_send.at[i], swap_recv.at[i], core)
        group.live.start()

    def swap_finish(group):
        group.live.wait_recv()
        base = (group.index - EARLY) * size
        for i in range(1 << count):
            rows = slice(base + i * piece, base + (i + 1) * piece)
            total = late[mine, rows, :].astype(F32) + late_landed[rows, :].astype(F32)
            group.acc[tuple((i >> (count - 1 - k)) & 1 for k in range(count))] = total.astype(BF16)
        group.live.wait_send()

    def halve_begin(group):
        bit = group.halvings[len(group.done)]
        i = group.index * count + len(group.done)

        def at(value):
            return tuple(
                pl.ds(value, 1) if d == bit else pl.ds(bit_of(d), 1) if d in group.done else slice(None)
                for d in dims(group)
            )

        own = bit_of(bit)
        group.live = remote(group.acc.at[at(1 - own)], group.landed.at[at(own)], send_sem.at[i], recv_sem.at[i], bit)
        group.live.start()

    def halve_finish(group):
        bit = group.halvings[len(group.done)]
        group.live.wait_recv()
        own = bit_of(bit)
        group.done.append(bit)
        last = len(group.done) == len(dims(group))
        for combo in combos([d for d in dims(group) if d not in group.done]):
            keep = tuple(combo[d] if d in combo else bit_of(d) for d in dims(group))
            there = tuple(1 - own if d == bit else k for d, k in zip(dims(group), keep))
            total = (group.acc[keep].astype(F32) + group.landed[there].astype(F32)).astype(BF16)
            if last:
                gathered[(mine, group.index) + tuple(bit_of(d) for d in bits)] = total
            else:
                group.acc[keep] = total
        group.live.wait_send()

    def double_begin(group):
        done = group.doublings[: group.step]
        bit = group.doublings[group.step] if group.step < count else core
        i = group.index * (count + 1) + group.step
        part = gathered.at[
            (mine, group.index) + tuple(slice(None) if d in done else pl.ds(bit_of(d), 1) for d in bits)
        ]
        group.live = remote(part, part, back_send.at[i], back_recv.at[i], bit)
        group.live.start()
        group.step += 1

    def double_finish(group):
        group.live.wait_recv()
        group.live.wait_send()

    stores = []

    def store(group):
        for side in range(2):
            copy = pltpu.make_async_copy(
                gathered.at[side, group.index], summed.at[side, group.index], store_sem.at[2 * group.index + side]
            )
            copy.start()
            stores.append(copy)

    def plan(group):
        group.step = 0
        steps = [] if group.early else [(swap_begin, swap_finish)]
        steps += [(halve_begin, halve_finish)] * len(group.halvings)
        steps += [(double_begin, double_finish)] * (count + 1)
        return steps

    plans = [plan(group) for group in groups]

    def advance(g):
        group, steps = groups[g], plans[g]
        if group.at > 0:
            steps[group.at - 1][1](group)
        if group.at < len(steps):
            steps[group.at][0](group)
        else:
            store(group)
        group.at += 1


    me = lax.axis_index("rays")
    lat = latent_mid.shape[0]
    near, far = ("rays", 1), ("rays", 2)
    near_copies = [
        remote(latent_part.at[2 * i + 1 - lax.rem(me, 2)], latent_landed.at[i], latent_send.at[i], latent_recv.at[i], near)
        for i in range(2)
    ]
    far_copy = remote(latent_mid, latent_landed.at[2], latent_send.at[2], latent_recv.at[2], far)
    small_copies = [
        remote(smalls.at[t], small_landed.at[t], small_send.at[t], small_recv.at[t], partners[t])
        for t in range(count + 1)
    ]

    def early_begin():
        need(4)
        for g in range(EARLY):
            for i in range(1 << (count - 2)):
                rows = slice(i * piece, (i + 1) * piece)
                total = v_kept[g, rows, :].astype(F32)
                for other in (v_first, v_second, v_both):
                    total = total + other[g, rows, :].astype(F32)
                early_acc[(g,) + tuple((i >> (count - 3 - k)) & 1 for k in range(count - 2))] = total.astype(BF16)
            advance(g)

    step = 256

    def weight_grad(index, left, right):
        @pl.loop(0, width // step)
        def _(j):
            first = pl.multiple_of(j * step, step)
            part = dot(left[:, pl.ds(first, step)], right[...], 0, 0).astype(BF16)
            rows = pl.ds(pl.multiple_of(index * size + first, step), step)
            late[0, rows, :] = part[:, :half_width]
            late[1, rows, :] = part[:, half_width:]

        advance(EARLY + index)

    def unsort_part():
        need(11)
        unsort_rows(v_grad_queries, v_sorted, position_column)

    def query_part():
        need(12)
        weight_grad(0, v_ray_normed, v_grad_queries)

    def key_part():
        need(6)
        weight_grad(1, v_latent_normed, v_grad_keys)

    def value_part():
        need(7)
        weight_grad(2, v_latent_normed, v_grad_values)

    turns = {"L": 0, "R": 0}

    def latents_begin():
        need(10)
        i = turns["L"]
        turns["L"] += 1
        rows = slice(i * lat, (i + 1) * lat)
        part = dot(v_grad_keys[rows, :], v_key_w[...], 1, 1) + dot(v_grad_values[rows, :], v_value_w[...], 1, 1)
        standard, _ = stand(v_latent_all[rows, :].astype(F32))
        smalls[0, 8:9, :] += jnp.sum(part * standard, axis=0, keepdims=True)
        smalls[0, 9:10, :] += jnp.sum(part, axis=0, keepdims=True)
        latent_part[i] = part.astype(BF16)
        if i == 3:
            for copy in near_copies:
                copy.start()

    def latents_next():
        for copy in near_copies:
            copy.wait_recv()
            copy.wait_send()
        other = lax.bitwise_xor(me, 2)
        latent_mid[...] = (
            latent_part[other].astype(F32) + latent_landed[lax.div(other, 2)].astype(F32)
        ).astype(BF16)
        far_copy.start()

    def latents_end():
        far_copy.wait_recv()
        far_copy.wait_send()
        grad_normed = (
            latent_part[me].astype(F32) + latent_landed[lax.div(me, 2)].astype(F32) + latent_landed[2].astype(F32)
        )
        standard, inverse = stand(v_latent_all[pl.ds(pl.multiple_of(me * lat, 32), lat), :].astype(F32))
        latent_grad[...] = norm_back(grad_normed, standard, inverse, as_row(latent_gain)).astype(BF16)

    def rays_part():
        need(15)
        chunk = rays.shape[0] // 4
        i = turns["R"]
        turns["R"] += 1
        rows = slice(i * chunk, (i + 1) * chunk)
        grad_normed = dot(v_grad_queries[rows, :], v_query_w[...], 1, 1)
        standard, inverse = stand(v_rays[rows, :].astype(F32))
        smalls[0, 6:7, :] += jnp.sum(grad_normed * standard, axis=0, keepdims=True)
        smalls[0, 7:8, :] += jnp.sum(grad_normed, axis=0, keepdims=True)
        ray_grad[rows, :] = (
            v_grad_hidden[rows, :] + norm_back(grad_normed, standard, inverse, as_row(ray_gain))
        ).astype(BF16)
        if i == 3:
            small_copies[0].start()

    small_at = [0]

    def small_next():
        t = small_at[0]
        small_copies[t].wait_recv()
        smalls[t + 1] = smalls[t] + small_landed[t]
        small_copies[t].wait_send()
        small_at[0] += 1
        if t + 1 <= count:
            small_copies[t + 1].start()
        else:
            small[...] = smalls[count + 1]

    tasks = {
        "E": early_begin, "U": unsort_part, "Q": query_part, "K": key_part, "V": value_part, "L": latents_begin, "M": latents_next,
        "N": latents_end, "R": rays_part, "S": small_next,
    }
    for letter in script:
        if letter in tasks:
            tasks[letter]()
        else:
            advance(int(letter))
    while small_at[0] <= count:
        small_next()
    while any(group.at <= len(steps) for group, steps in zip(groups, plans)):
        for g in range(len(groups)):
            if groups[g].at <= len(plans[g]):
                advance(g)
    for copy in stores:
        copy.wait()


def widen_kernel(size, summed, small, *refs):
    down, up, out, query, key, value = refs[:6]
    vectors, up_bias, (held, wide, load_sem, store_sem) = refs[6:14], refs[14], refs[15:]
    for at, vector in zip((5, 0, 6, 7, 8, 9, 3, 4), vectors):
        vector[...] = small[at]
    up_bias[: small.shape[1]] = small[1]
    up_bias[small.shape[1] :] = small[2]
    width = held.shape[3] * 2
    half = width // 2
    step = held.shape[2]
    jobs = []
    for g in range(8):
        for r in range(0, width, step):
            if g < 2:
                target = down.at[pl.ds(g * width + r, step), :]
            elif g < 4:
                target = up.at[pl.ds(r, step), pl.ds((g - 2) * width, width)]
            else:
                target = (out, query, key, value)[g - 4].at[pl.ds(r, step), :]
            jobs.append((summed.at[:, pl.ds(g * size + r, step), :], target))
    slots = held.shape[0]
    loads = [pltpu.make_async_copy(src, held.at[i % slots], load_sem.at[i % slots]) for i, (src, _) in enumerate(jobs)]
    saves = [pltpu.make_async_copy(wide.at[i % slots], dst, store_sem.at[i % slots]) for i, (_, dst) in enumerate(jobs)]
    for i in range(slots):
        loads[i].start()
    for i in range(len(jobs)):
        slot = i % slots
        loads[i].wait()
        if i >= slots:
            saves[i - slots].wait()
        wide[slot, :, :half] = held[slot, 0].astype(F32)
        wide[slot, :, half:] = held[slot, 1].astype(F32)
        saves[i].start()
        if i + slots < len(jobs):
            loads[i + slots].start()
    for i in range(len(jobs) - slots, len(jobs)):
        saves[i].wait()


def log2(n):
    return n.bit_length() - 1


EARLY = 5


HALVINGS = ("zw", "zw", "wz", "zw", "zw", "yzxw", "xzyw", "yxwz")
DOUBLINGS = ("zwyx", "wyzx", "wzxy", "ywxz", "zxyw", "wyxz", "wzxy", "zwyx")
SCRIPT = (
    "EKV0U16723Q4L0L12536047L1L2R67R5430M21R6R47502S3",
    "5S176S57SN06S543067215627153463745675",
)


def ways(items, ray_parts):
    core, y, x = ("rays", 1), ("rays", 2), ("items", 1)
    bits = (x, y) + tuple(("items", 2 << i) for i in range(log2(items) - 1)) + tuple(
        ("rays", 4 << i) for i in range(log2(ray_parts) - 2)
    )
    if len(bits) != 4:
        return core, bits, (bits[2:],) * EARLY + (bits,) * 3, (bits[::-1],) * (EARLY + 3), "EKVUQLLLLRRRRMN"
    name = dict(zip("xyzw", bits))
    halvings = tuple(tuple(name[c] for c in word) for word in HALVINGS)
    doublings = tuple(tuple(name[c] for c in word) for word in DOUBLINGS)
    return core, bits, halvings, doublings, "".join(SCRIPT)


def on_device(
    items, ray_parts,
    rays, latents, ray_scene, latent_scene, latent_pad, cotangent,
    query_weight, key_weight, value_weight, out_weight, out_bias, up_weight, up_bias, down_weight, down_bias,
    ray_gain, ray_shift, latent_gain, latent_shift, mlp_gain, mlp_shift,
):
    _, count, width = rays.shape
    lat = latents.shape[1]
    total = lat * ray_parts
    padded = total + WINDOW
    hidden_width = up_weight.shape[1]
    x = rays[0]
    upstream = cotangent[0]

    shape = jax.ShapeDtypeStruct
    rows_bf16 = shape((count, width), BF16)
    total_bf16 = shape((total, width), BF16)
    dma = pltpu.SemaphoreType.DMA

    square = shape((width, width), BF16)
    padded_bf16 = shape((padded, width), BF16)
    (
        ray_normed, sorted_queries, keys, values, latent_normed, latent_all, meta, position_row, position_column,
    ) = pl.pallas_call(
        project_kernel,
        out_shape=(
            rows_bf16, rows_bf16, padded_bf16, padded_bf16, total_bf16, total_bf16,
            shape((2 * SCENES + 2,), jnp.int32), shape((1, count), jnp.int32), shape((count, 1), jnp.int32),
        ),
        in_specs=[anywhere()] * 5 + [vmem()] * 7,
        out_specs=[anywhere()] * 6 + [smem(), vmem(), vmem()],
        scratch_shapes=[pltpu.VMEM((3, lat, width), BF16), pltpu.VMEM((count, width), BF16)]
        + [pltpu.VMEM((lat, width), BF16)] + [pltpu.VMEM((width, width), BF16)] * 3
        + [pltpu.VMEM((count, width), BF16)] * 3
        + [pltpu.VMEM((padded, width), BF16)] * 2 + [pltpu.VMEM((total, width), BF16)]
        + [dma((5,)), dma((5,)), dma((5,)), dma((20,))],
        compiler_params=big(collective_id=1, has_side_effects=True),
        name="project",
    )(
        x, latents[0], query_weight, key_weight, value_weight,
        ray_gain, ray_shift, latent_gain, latent_shift, ray_scene, latent_scene, latent_pad,
    )

    mixture, sorted_mixture, log_total = run_attend(meta, sorted_queries, keys, values, position_column)

    core, bits, halvings, doublings, script = ways(items, ray_parts)
    first, second = bits[:2]
    nbits = len(bits)
    unit = 16 << nbits
    size = (width + unit - 1) // unit * unit
    quarter = size // 4
    half_width = width // 2
    groups = len(halvings)
    late_groups = groups - EARLY
    piece = (size >> nbits, half_width)
    quarter_bf16 = (EARLY, quarter, half_width)

    ray_out, grad_mixture, grad_hidden, kept, to_first, to_second, to_both, early_sums = pl.pallas_call(
        functools.partial(mlp_kernel, core, first, second, size),
        out_shape=(
            rows_bf16, rows_bf16, shape((count, width), F32),
            shape(quarter_bf16, BF16), shape(quarter_bf16, BF16), shape(quarter_bf16, BF16), shape(quarter_bf16, BF16),
            shape((8, width), F32),
        ),
        in_specs=[anywhere()] * 6 + [vmem()] * 5,
        out_specs=[anywhere()] * 7 + [vmem()],
        scratch_shapes=[
            pltpu.VMEM((count, width), BF16), pltpu.VMEM((width, width), BF16), pltpu.VMEM((count, width), BF16),
            pltpu.VMEM((width, hidden_width), BF16), pltpu.VMEM((hidden_width, width), BF16),
            pltpu.VMEM((count, width), BF16),
            pltpu.VMEM((count, width), BF16), pltpu.VMEM((count, width), BF16), pltpu.VMEM((count, width), F32),
            pltpu.VMEM((4,) + quarter_bf16, BF16),
            pltpu.VMEM((count, hidden_width), BF16), pltpu.VMEM((count, hidden_width), BF16),
            pltpu.VMEM((count, width), BF16), pltpu.VMEM((count, width), BF16),
            pltpu.VMEM((2, EARLY * size, half_width), BF16), pltpu.VMEM((EARLY * size, half_width), BF16),
            dma((15,)), dma((15,)), dma((6,)), dma((12,)), dma((4 * EARLY,)),
        ],
        compiler_params=big(collective_id=2, has_side_effects=True),
        name="mlp",
    )(
        mixture, out_weight, x, up_weight, down_weight, upstream,
        out_bias, up_bias, down_bias, mlp_gain, mlp_shift,
    )

    def flip(index, partners):
        item, part = index // ray_parts, index % ray_parts
        for axis, bit in partners:
            item, part = (item ^ bit, part) if axis == "items" else (item, part ^ bit)
        return item * ray_parts + part

    def exchange(array, *partners):
        return lax.ppermute(
            array, ("items", "rays"), [(i, flip(i, partners)) for i in range(items * ray_parts)]
        )

    from_first = exchange(to_first, first)
    from_second = exchange(to_second, second)
    from_both = exchange(to_both, first, second)

    sorted_grad, grad_keys, grad_values = run_attend_back(
        meta, grad_mixture, position_row, sorted_queries, sorted_mixture, log_total, keys, values
    )

    held = [shape(quarter_bf16, BF16)] * 4 + [total_bf16] * 3 + [rows_bf16] * 0
    held = held + [square, square, total_bf16, rows_bf16, rows_bf16, square, rows_bf16, shape((count, width), F32)]
    held = held + [rows_bf16]
    ray_grad, latent_grad, summed, small = pl.pallas_call(
        functools.partial(reduce_kernel, core, bits, halvings, doublings, size, script),
        out_shape=(
            rows_bf16, shape((lat, width), BF16), shape((2, groups) + (2,) * nbits + piece, BF16),
            shape((16, width), F32),
        ),
        in_specs=[anywhere()] * 15 + [vmem()] * 4,
        out_specs=[vmem(), vmem(), anywhere(), vmem()],
        scratch_shapes=[pltpu.VMEM(h.shape, h.dtype) for h in held] + [
            pltpu.VMEM((2, late_groups * size, half_width), BF16),
            pltpu.VMEM((late_groups * size, half_width), BF16),
            pltpu.VMEM((EARLY,) + (2,) * (nbits - 2) + piece, BF16),
            pltpu.VMEM((EARLY,) + (2,) * (nbits - 2) + piece, BF16),
            pltpu.VMEM((late_groups,) + (2,) * nbits + piece, BF16),
            pltpu.VMEM((late_groups,) + (2,) * nbits + piece, BF16),
            pltpu.VMEM((2, groups) + (2,) * nbits + piece, BF16),
            pltpu.VMEM((nbits + 2, 16, width), F32),
            pltpu.VMEM((nbits + 1, 16, width), F32),
            pltpu.VMEM((4, lat, width), BF16),
            pltpu.VMEM((3, lat, width), BF16),
            pltpu.VMEM((lat, width), BF16),
            dma((15,)), dma((late_groups,)), dma((late_groups,)),
            dma((groups * nbits,)), dma((groups * nbits,)), dma((groups * (nbits + 1),)), dma((groups * (nbits + 1),)),
            dma((nbits + 1,)), dma((nbits + 1,)), dma((3,)), dma((3,)), dma((2 * groups,)),
        ],
        compiler_params=big(collective_id=3, has_side_effects=True),
        name="reduce",
    )(
        kept, from_first, from_second, from_both,
        latent_normed, grad_keys, grad_values, key_weight, value_weight, latent_all,
        sorted_grad, ray_normed, query_weight, x, grad_hidden,
        ray_gain, latent_gain, early_sums, position_column,
    )

    wide = shape((width, width), F32)
    step, slots = 768, 8
    (
        down_grad, up_grad, out_grad, query_grad, key_grad, value_grad,
        out_bias_grad, down_bias_grad, ray_gain_grad, ray_shift_grad, latent_gain_grad, latent_shift_grad,
        mlp_gain_grad, mlp_shift_grad, up_bias_grad,
    ) = pl.pallas_call(
        functools.partial(widen_kernel, size),
        out_shape=(shape((2 * width, width), F32), shape((width, 2 * width), F32), wide, wide, wide, wide)
        + (shape((width,), F32),) * 8 + (shape((hidden_width,), F32),),
        in_specs=[anywhere(), vmem()],
        out_specs=[anywhere()] * 6 + [vmem()] * 9,
        scratch_shapes=[
            pltpu.VMEM((slots, 2, step, half_width), BF16), pltpu.VMEM((slots, step, width), F32),
            dma((slots,)), dma((slots,)),
        ],
        compiler_params=big(),
        name="widen",
    )(summed.reshape(2, groups * size, half_width), small)

    return (
        ray_out[None], ray_grad[None], latent_grad[None],
        query_grad, key_grad, value_grad, out_grad, out_bias_grad,
        up_grad, up_bias_grad, down_grad, down_bias_grad,
        ray_gain_grad, ray_shift_grad, latent_gain_grad, latent_shift_grad, mlp_gain_grad, mlp_shift_grad,
    )


def solution(mesh):
    split = P("items", "rays", None)
    in_specs = (split, split, P("items", "rays"), P("items", None), P("items", None), split) + (P(),) * 15
    out_specs = (split, split, split) + (P(),) * 15
    return jax.shard_map(
        functools.partial(on_device, mesh.shape["items"], mesh.shape["rays"]),
        mesh=mesh, in_specs=in_specs, out_specs=out_specs, check_vma=False,
    )
```
